32 devices in a mesh: row: 4 (over z), col: 8 (over y, x, core).
Axes of the slice: x: 2, y: 2, z: 4, core: 2. Of those that a mesh axis runs over, the one named last changes fastest.
Arguments:
- inputs: bfloat16 [12288, 2560], P(('col', 'row')), may hold values from -6 to 6
- segments: int32 [12288], P('col'), may hold values from 0 to 4, as said below
- valid_mask: int32 [12288], P(('col', 'row')), may hold values from 0 to 1
- teacher: bfloat16 [12288, 2560], P(('col', 'row')), may hold values from -15 to 15
- cotangent: bfloat16 [12288, 2560], P(('col', 'row')), may hold values from -6 to 6
- query_down: bfloat16 [2560, 768], P(('row', 'col')), may hold values from -0.125 to 0.125
- latent_down: bfloat16 [2560, 288], P(('row', 'col')), may hold values from -0.125 to 0.125
- query_up: bfloat16 [768, 3840], P('col', 'row'), may hold values from -0.21875 to 0.21875
- latent_up: bfloat16 [256, 5120], P('col', 'row'), may hold values from -0.375 to 0.375
- output_weight: bfloat16 [2560, 2560], P('row', 'col'), may hold values from -6 to 6
- gate_weight: bfloat16 [2560, 6400], P('col', 'row'), may hold values from -0.125 to 0.125
- up_weight: bfloat16 [2560, 6400], P('col', 'row'), may hold values from -0.125 to 0.125
- down_weight: bfloat16 [6400, 2560], P('row', 'col'), may hold values from -0.4375 to 0.4375
- attn_gain: bfloat16 [2560], P(('row', 'col')), may hold values from 0.5 to 1.5
- query_gain: bfloat16 [768], P(('row', 'col')), may hold values from 0.5 to 1.5
- latent_gain: bfloat16 [256], P(('row', 'col')), may hold values from 0.5 to 1.5
- mlp_gain: bfloat16 [2560], P(('row', 'col')), may hold values from 0.5 to 1.5
Outputs:
- block_out: bfloat16 [12288, 2560], P(('col', 'row'))
- loss: float32 [], replicated
- inputs_grad: float32 [12288, 2560], P(('col', 'row'))
- query_down_grad: float32 [2560, 768], P(('row', 'col'))
- latent_down_grad: float32 [2560, 288], P(('row', 'col'))
- query_up_grad: float32 [768, 3840], P('col', 'row')
- latent_up_grad: float32 [256, 5120], P('col', 'row')
- output_weight_grad: float32 [2560, 2560], P('row', 'col')
- gate_weight_grad: float32 [2560, 6400], P('col', 'row')
- up_weight_grad: float32 [2560, 6400], P('col', 'row')
- down_weight_grad: float32 [6400, 2560], P('row', 'col')
- attention_gain_gradient: float32 [2560], P(('row', 'col'))
- query_gain_grad: float32 [768], P(('row', 'col'))
- latent_gain_grad: float32 [256], P(('row', 'col'))
- mlp_gain_grad: float32 [2560], P(('row', 'col'))
The draws below stay inside these ranges and needn't reach their ends.
Inputs may be any that keep to these rules, and one draw needn't show every extreme that they name: `segments`: each group of 1536 consecutive tokens starts with its prompt (segment 0) of 256 to 512 tokens, then continuations 1 to 4 in order, each of 256 tokens or more; the last continuation ends the group, so that late tokens of a group read prompt keys from its first tokens.
All inputs are finite; a program needn't handle non-finite values.
Results may differ from the reference program's by a relative error of at most 0.019.
Values may be sent and summed in bfloat16 or wider, within the bound.
A program may use at most 256 MiB of HBM per device.

```python
import math
import jax
import jax.numpy as jnp
from jax import lax

D = 2560
HEADS = 40
NOPE = 64
ROPE = 32
VDIM = 64
Q_RANK = 768
KV_RANK = 256
FF = 6400
PROMPT = 512
CONT_LEN = 256
CONTS = 4
GROUP = 1536
TOKENS = 12288
N_ROW = 4


def draw_segments(key, part):
    key = jax.random.fold_in(key, 11)
    groups = TOKENS // GROUP
    prompt_len = jax.random.randint(key, (groups, 1), PROMPT // 2, PROMPT + 1)
    spare_rows = PROMPT - prompt_len
    indices = jnp.arange(GROUP, dtype=jnp.int32)[None, :]
    labels = (indices >= prompt_len).astype(jnp.int32)
    for border in range(1, CONTS):
        border_at = prompt_len + border * CONT_LEN + spare_rows * border // CONTS
        labels = labels + (indices >= border_at).astype(jnp.int32)
    return labels.reshape(groups * GROUP)


def draw_valid_mask(key, part):
    key = jax.random.fold_in(key, 23)
    within = jnp.arange(TOKENS, dtype=jnp.int32) % GROUP
    threshold = 50 + 900 * within // GROUP
    return (jax.random.randint(key, (TOKENS,), 0, 1000) < threshold).astype(jnp.int32)


def draw_teacher(key, part):
    key = jax.random.fold_in(key, 37)
    within = (jnp.arange(TOKENS, dtype=jnp.int32) % GROUP).astype(jnp.float32)
    place = within[:, None] / GROUP
    base = jnp.clip(jax.random.normal(key, (TOKENS, D), jnp.float32), -6.0, 6.0)
    scale = 0.4 + 2.0 * place
    return (base * scale).astype(jnp.bfloat16)


def block_levels(stream_key, extent, split, least, top_value):
    level = 1.0
    for dim, parts in split:
        steps = jax.random.uniform(jax.random.fold_in(jax.random.fold_in(stream_key, 6), dim), (parts,), jnp.float32, least / len(split), top_value / len(split))
        level = level * jnp.repeat(jnp.exp(steps), extent[dim] // parts).reshape((-1,) + (1,) * (len(extent) - 1 - dim))
    return level


def gaussian(rng, shape, scale, limit, shards=(), kind=jnp.bfloat16):
    values = jax.random.normal(rng, shape, jnp.float32) * scale
    if len(shards) > 0:
        values = block_levels(rng, shape, shards, -0.22, 0.18) * values
    return jnp.clip(values, min=-limit, max=limit).astype(kind)


def setup_inputs(seed: int = 0) -> dict:
    streams_of = jax.random.split(jax.random.key(seed), 18)
    inputs = gaussian(streams_of[0], (TOKENS, D), 1.0, 6.0, ((0, 32),))
    segments = draw_segments(jax.random.fold_in(streams_of[17], 71), 0)
    valid_mask = draw_valid_mask(jax.random.fold_in(streams_of[17], 71), 0)
    teacher = draw_teacher(jax.random.fold_in(streams_of[17], 71), 0)
    cotangent = gaussian(streams_of[4], (TOKENS, D), 1.0, 6.0, ((0, 32),))
    query_down = gaussian(streams_of[5], (D, Q_RANK), D ** -0.5, 0.125, ((0, 32),))
    latent_down = gaussian(streams_of[6], (D, KV_RANK + ROPE), D ** -0.5, 0.125, ((0, 32),))
    query_up = gaussian(streams_of[7], (Q_RANK, HEADS * (NOPE + ROPE)), Q_RANK ** -0.5, 0.21875, ((0, 8), (1, 4)))
    latent_up = gaussian(streams_of[8], (KV_RANK, HEADS * (NOPE + VDIM)), KV_RANK ** -0.5, 0.375, ((0, 8), (1, 4)))
    output_weight = gaussian(streams_of[9], (HEADS * VDIM, D), (max(1, HEADS * VDIM // 2560)) ** -0.5, 6.0, ((0, 4), (1, 8)))
    gate_weight = gaussian(streams_of[10], (D, FF), D ** -0.5, 0.125, ((0, 8), (1, 4)))
    up_weight = gaussian(streams_of[11], (D, FF), D ** -0.5, 0.125, ((0, 8), (1, 4)))
    down_weight = gaussian(streams_of[12], (FF, D), (max(1, FF // 32)) ** -0.5, 0.4375, ((0, 4), (1, 8)))
    attn_gain = jnp.clip(1.0 + 0.1 * jax.random.normal(streams_of[13], (D,), jnp.float32), 0.5, 1.5).astype(jnp.bfloat16)
    query_gain = jnp.clip(1.0 + 0.1 * jax.random.normal(streams_of[14], (Q_RANK,), jnp.float32), 0.5, 1.5).astype(jnp.bfloat16)
    latent_gain = jnp.clip(1.0 + 0.1 * jax.random.normal(streams_of[15], (KV_RANK,), jnp.float32), 0.5, 1.5).astype(jnp.bfloat16)
    mlp_gain = jnp.clip(1.0 + 0.1 * jax.random.normal(streams_of[16], (D,), jnp.float32), 0.5, 1.5).astype(jnp.bfloat16)
    return {"inputs": inputs, "segments": segments, "valid_mask": valid_mask, "teacher": teacher, "cotangent": cotangent, "query_down": query_down, "latent_down": latent_down, "query_up": query_up, "latent_up": latent_up, "output_weight": output_weight, "gate_weight": gate_weight, "up_weight": up_weight, "down_weight": down_weight, "attn_gain": attn_gain, "query_gain": query_gain, "latent_gain": latent_gain, "mlp_gain": mlp_gain}


EPS = 1e-05
RES = 1.4 / math.sqrt(62.0)
BASE = 10000.0
HIGH_PRECISION = lax.Precision.HIGHEST

@jax.custom_vjp
def low(v):
    return lax.optimization_barrier(v.astype(jnp.bfloat16)).astype(jnp.float32)

@jax.custom_vjp
def low_back(v):
    return v

def low_keep(v):
    return (low(v), None)

def low_pass(kept, grad):
    return (grad,)

def back_keep(v):
    return (v, None)

def back_low(kept, grad):
    return (low(grad),)
low.defvjp(low_keep, low_pass)
low_back.defvjp(back_keep, back_low)

def root_norm(values, gain):
    return values * lax.rsqrt(lax.optimization_barrier(jnp.mean(values * values, axis=-1, keepdims=True)) + EPS) * gain

def rotary(segments):
    length = segments.shape[0]
    indices = jnp.arange(length, dtype=jnp.int32)
    labels = jnp.arange(CONTS + 1, dtype=jnp.int32)
    member = (segments[:, None] == labels[None, :]).astype(jnp.int32)
    counts = lax.optimization_barrier(jnp.sum(member, axis=0))
    starts = jnp.cumsum(counts) - counts
    first_at = lax.optimization_barrier(jnp.sum(member * starts[None, :], axis=1))
    places = jnp.where(segments == 0, indices, counts[0] + indices - first_at).astype(jnp.float32)
    freqs = BASE ** (-jnp.arange(ROPE // 2, dtype=jnp.float32) * 2.0 / ROPE)
    angles = places[:, None] * freqs[None, :]
    return (jnp.cos(angles), jnp.sin(angles))

def rotate(values, cosine, sine):
    half = values.shape[-1] // 2
    first_half = values[..., :half]
    second_half = values[..., half:]
    return jnp.concatenate([first_half * cosine - second_half * sine, second_half * cosine + first_half * sine], axis=-1)

def attend(query_vectors, key_rows, values, segments):
    length = query_vectors.shape[0]
    block = math.gcd(length, 512)
    scale = (NOPE + ROPE) ** (-0.5)
    positions = jnp.arange(length, dtype=jnp.int32)

    def one_block(block_idx):
        begin = (block_idx * block).astype(jnp.int32)
        query_rows = lax.dynamic_slice_in_dim(query_vectors, begin, block, 0)
        query_pos = begin + jnp.arange(block, dtype=jnp.int32)
        query_seg = lax.dynamic_slice_in_dim(segments, begin, block, 0)
        allowed = (positions[None, :] <= query_pos[:, None]) & ((segments[None, :] == 0) | (segments[None, :] == query_seg[:, None]))
        scores = low_back(jnp.einsum('qhd,khd->hqk', query_rows, key_rows, precision=HIGH_PRECISION) * scale)
        scores = jnp.where(allowed[None], scores, -jnp.inf)
        weights_p = low(jax.nn.softmax(scores, axis=-1))
        return jnp.einsum('hqk,khd->qhd', weights_p, values, precision=HIGH_PRECISION)
    result = lax.map(jax.checkpoint(one_block), jnp.arange(length // block, dtype=jnp.int32))
    return result.reshape(length, HEADS, VDIM)

def blocked_sum(left_operand_rows, right_operand_rows):
    feature_width = left_operand_rows.shape[1] // N_ROW
    split_pieces = jnp.einsum('wml,mlv->mwv', left_operand_rows.reshape(left_operand_rows.shape[0], N_ROW, feature_width), right_operand_rows.reshape(N_ROW, feature_width, right_operand_rows.shape[1]), precision=HIGH_PRECISION)
    return lax.optimization_barrier(jnp.sum(low(split_pieces), axis=0))

def group_forward(tokens_in, segments, params):
    query_down, latent_down, query_up, latent_up, output_weight, gate_weight, up_weight, down_weight, attn_gain, query_gain, latent_gain, mlp_gain = params
    length = tokens_in.shape[0]
    cosine, sine = rotary(segments)
    normed = low(root_norm(tokens_in, attn_gain))
    query_lat = low_back(jnp.dot(normed, query_down, precision=HIGH_PRECISION))
    query_norm = low(root_norm(query_lat, query_gain))
    kv_lat = low_back(jnp.dot(normed, latent_down, precision=HIGH_PRECISION))
    kv_norm = low(root_norm(kv_lat[:, :KV_RANK], latent_gain))
    key_rope = low(rotate(kv_lat[:, KV_RANK:], cosine, sine))
    query_proj = low_back(jnp.dot(query_norm, query_up, precision=HIGH_PRECISION)).reshape(length, HEADS, NOPE + ROPE)
    query_vectors = low(jnp.concatenate([query_proj[:, :, :NOPE], rotate(query_proj[:, :, NOPE:], cosine[:, None, :], sine[:, None, :])], axis=-1))
    kv_proj = low_back(jnp.dot(kv_norm, latent_up, precision=HIGH_PRECISION)).reshape(length, HEADS, NOPE + VDIM)
    key_rows = jnp.concatenate([low(kv_proj[:, :, :NOPE]), jnp.broadcast_to(key_rope[:, None, :], (length, HEADS, ROPE))], axis=-1)
    values = low(kv_proj[:, :, NOPE:])
    mixed_out = low(low_back(attend(query_vectors, key_rows, values, segments))).reshape(length, HEADS * VDIM)
    attn_sum = low_back(blocked_sum(mixed_out, output_weight))
    residual = tokens_in + RES * attn_sum
    mlp_in = low(root_norm(residual, mlp_gain))
    gate_act = low_back(jnp.dot(mlp_in, gate_weight, precision=HIGH_PRECISION))
    up_act = low_back(jnp.dot(mlp_in, up_weight, precision=HIGH_PRECISION))
    hidden = low(jax.nn.silu(gate_act) * up_act)
    return residual + RES * low_back(blocked_sum(hidden, down_weight))

def reference(inputs, segments, valid_mask, teacher, cotangent, query_down, latent_down, query_up, latent_up, output_weight, gate_weight, up_weight, down_weight, attn_gain, query_gain, latent_gain, mlp_gain):
    params = tuple((array.astype(jnp.float32) for array in (query_down, latent_down, query_up, latent_up, output_weight, gate_weight, up_weight, down_weight, attn_gain, query_gain, latent_gain, mlp_gain)))
    tokens_f = inputs.astype(jnp.float32)
    teacher_f = teacher.astype(jnp.float32)
    cot_f = cotangent.astype(jnp.float32)
    weight_v = valid_mask.astype(jnp.float32)[:, None]
    valid_total = jnp.sum(valid_mask).astype(jnp.float32)
    total_tokens = inputs.shape[0]
    group_segs = segments.reshape(-1, GROUP)

    def objective(tokens_all, weights_all):

        def one_group(pair):
            return group_forward(pair[0], pair[1], weights_all)
        outputs = lax.map(jax.checkpoint(one_group), (tokens_all.reshape(-1, GROUP, D), group_segs)).reshape(-1, D)
        error_val = outputs - teacher_f
        squared = 0.5 * jnp.sum(weight_v * error_val * error_val)
        return (jnp.sum(cot_f * outputs) + total_tokens * squared / valid_total, (outputs, squared))
    value_j, pullback, (outputs, squared) = jax.vjp(objective, tokens_f, params, has_aux=True)
    input_grad, grads = pullback(jnp.ones((), jnp.float32))
    return (outputs.astype(jnp.bfloat16), squared / valid_total, input_grad, grads[0], grads[1], grads[2], grads[3], grads[4], grads[5], grads[6], grads[7], grads[8], grads[9], grads[10], grads[11])
```

```python
import functools
import math

import jax
import jax.numpy as jnp
from jax import lax
from jax.experimental import pallas as pl
from jax.experimental.pallas import tpu as pltpu
from jax.sharding import PartitionSpec as P

NOPE = 64
ROPE = 32
VDIM = 64
KV_RANK = 256
CONTS = 4
HEAD = 128

EPS = 1e-05
RES = 1.4 / math.sqrt(62.0)
BASE = 10000.0
SCALE = (NOPE + ROPE) ** (-0.5)
LOG2E = math.log2(math.e)
HIDE = -1e30
BF = jnp.bfloat16
F32 = jnp.float32


def dot_plain(left_op, right_op):
    return jnp.dot(left_op, right_op, preferred_element_type=F32)


def dot_dims(left_op, right_op, left_dims, right_dims):
    return lax.dot_general(
        left_op, right_op, ((left_dims, right_dims), ((), ())), preferred_element_type=F32
    )


def dot_trans_left(left_op, right_op):
    return dot_dims(left_op, right_op, (0,), (0,))


def dot_trans_right(left_op, right_op):
    return dot_dims(left_op, right_op, (1,), (1,))


def root_norm(values, gain):
    unit_rows = values * lax.rsqrt(jnp.mean(values * values, axis=-1, keepdims=True) + EPS)
    return (unit_rows * gain, unit_rows)


def norm_back(grad_rows, unit_rows, values, gain):
    factor = lax.rsqrt(jnp.mean(values * values, axis=-1, keepdims=True) + EPS)
    scaled = grad_rows * gain
    value_grad = factor * (
        scaled - unit_rows * jnp.mean(scaled * unit_rows, axis=-1, keepdims=True)
    )
    return (value_grad, jnp.sum(grad_rows * unit_rows, axis=0))


def rotary(segments):
    length = segments.shape[0]
    indices = jnp.arange(length, dtype=jnp.int32)
    labels = jnp.arange(CONTS + 1, dtype=jnp.int32)
    member = (segments[:, None] == labels[None, :]).astype(jnp.int32)
    counts = jnp.sum(member, axis=0)
    starts = jnp.cumsum(counts) - counts
    first_at = jnp.sum(member * starts[None, :], axis=1)
    places = jnp.where(segments == 0, indices, counts[0] + indices - first_at).astype(F32)
    freqs = BASE ** (-jnp.arange(ROPE // 2, dtype=F32) * 2.0 / ROPE)
    angles = places[:, None] * freqs[None, :]
    return (jnp.cos(angles), jnp.sin(angles))


def rotate(values, cosine, sine):
    half = values.shape[-1] // 2
    first_half = values[..., :half]
    second_half = values[..., half:]
    return jnp.concatenate(
        [first_half * cosine - second_half * sine, second_half * cosine + first_half * sine],
        axis=-1,
    )


def head_weights(weights_ref, query_rows):
    block = weights_ref[0]
    col_total = block.shape[0]
    query_w = block[:, :query_rows, :].reshape(col_total * query_rows, HEAD)
    latent_w = block[:, query_rows:, :].reshape(-1, HEAD)
    return (query_w, latent_w)


def head_vectors(weights_ref, query_t_ref, latent_ref, rope_ref, cos_ref, sin_ref, query_rows):
    query_w, latent_w = head_weights(weights_ref, query_rows)
    half = ROPE // 2
    proj_t = dot_plain(query_w.T, query_t_ref[...])
    first, second = proj_t[NOPE : NOPE + half], proj_t[NOPE + half : NOPE + ROPE]
    cosine, sine = cos_ref[...], sin_ref[...]
    query_t = jnp.concatenate(
        [
            proj_t[:NOPE],
            first * cosine - second * sine,
            second * cosine + first * sine,
            proj_t[NOPE + ROPE :],
        ],
        axis=0,
    ).astype(BF)
    both = dot_plain(latent_ref[...], latent_w).astype(BF)
    lane = lax.broadcasted_iota(jnp.int32, both.shape, 1)
    keys = jnp.where(lane < NOPE, both, rope_ref[...])
    return (query_w, latent_w, query_t, keys, both)


def attend_kernel(
    query_rows, tile, weights_ref, query_t_ref, latent_ref, rope_ref, cos_ref, sin_ref, bias_ref,
    mixed_ref, lse_ref, scores_ref,
):
    _, _, query_t, keys, both = head_vectors(
        weights_ref, query_t_ref, latent_ref, rope_ref, cos_ref, sin_ref, query_rows
    )
    values_t = both.T[NOPE:]
    length = keys.shape[0]
    top = None
    for begin in range(0, length, tile):
        part = dot_plain(keys[begin : begin + tile], query_t) * (SCALE * LOG2E)
        part = part + bias_ref[begin : begin + tile, :]
        scores_ref[begin : begin + tile, :] = part
        tile_top = jnp.max(part, axis=0, keepdims=True)
        top = tile_top if top is None else jnp.maximum(top, tile_top)
    total, out_t = None, None
    for begin in range(0, length, tile):
        expo = jnp.exp2(scores_ref[begin : begin + tile, :] - top)
        tile_sum = jnp.sum(expo, axis=0, keepdims=True)
        term = dot_plain(values_t[:, begin : begin + tile], expo.astype(BF))
        total = tile_sum if total is None else total + tile_sum
        out_t = term if out_t is None else out_t + term
    mixed_ref[...] = (out_t / total).astype(BF)
    lse_ref[0] = top + jnp.log2(total)


def attend_back_kernel(
    query_rows, tile, weights_ref, query_t_ref, latent_ref, latent_t_ref, rope_ref, cos_ref,
    sin_ref, bias_ref, mixed_ref, grad_ref, lse_ref,
    weights_grad_ref, query_grad_ref, latent_grad_ref, rope_grad_ref,
    query_acc, latent_acc, rope_acc, both_scr,
):
    head = pl.program_id(0)
    query_w, latent_w, query_t, keys, both = head_vectors(
        weights_ref, query_t_ref, latent_ref, rope_ref, cos_ref, sin_ref, query_rows
    )

    @pl.when(head == 0)
    def _():
        query_acc[...] = jnp.zeros_like(query_acc)
        latent_acc[...] = jnp.zeros_like(latent_acc)
        rope_acc[...] = jnp.zeros_like(rope_acc)

    keys_t = keys.T
    query = query_t.T
    grad_t = grad_ref[...]
    delta = jnp.sum(
        grad_t.astype(F32) * mixed_ref[...].astype(F32), axis=0, keepdims=True
    )
    grad_pad_t = jnp.concatenate([jnp.zeros_like(grad_t), grad_t], axis=0)
    grad_pad = grad_pad_t.T
    lse = lse_ref[0]
    length = keys.shape[0]
    query_back_t = None
    for begin in range(0, length, tile):
        rows = slice(begin, begin + tile)
        scores = dot_plain(keys[rows], query_t) * (SCALE * LOG2E)
        probs = jnp.exp2(scores + bias_ref[rows, :] - lse)
        prob_grad = dot_plain(both[rows], grad_pad_t)
        score_grad = (probs * (prob_grad - delta)).astype(BF)
        term = dot_plain(keys_t[:, rows], score_grad)
        query_back_t = term if query_back_t is None else query_back_t + term
        key_back = dot_plain(score_grad, query) * SCALE
        value_back = dot_plain(probs.astype(BF), grad_pad)
        lane = lax.broadcasted_iota(jnp.int32, key_back.shape, 1)
        rope_acc[rows, :] += key_back
        both_scr[rows, :] = jnp.where(lane < NOPE, key_back, value_back).astype(BF)
    query_back_t = query_back_t * SCALE
    half = ROPE // 2
    first, second = query_back_t[NOPE : NOPE + half], query_back_t[NOPE + half : NOPE + ROPE]
    cosine, sine = cos_ref[...], sin_ref[...]
    query_back_t = jnp.concatenate(
        [
            query_back_t[:NOPE],
            first * cosine + second * sine,
            second * cosine - first * sine,
            jnp.zeros_like(query_back_t[NOPE + ROPE :]),
        ],
        axis=0,
    ).astype(BF)
    both_back = both_scr[...]
    query_acc[...] += dot_plain(query_w, query_back_t)
    latent_acc[...] += dot_trans_right(both_back, latent_w)
    query_wg = dot_trans_right(query_t_ref[...], query_back_t)
    latent_wg = dot_plain(latent_t_ref[...], both_back)
    col_total = weights_ref.shape[1]
    weights_grad_ref[0, :, :query_rows, :] = query_wg.astype(BF).reshape(col_total, query_rows, HEAD)
    weights_grad_ref[0, :, query_rows:, :] = latent_wg.astype(BF).reshape(col_total, -1, HEAD)

    @pl.when(head == pl.num_programs(0) - 1)
    def _():
        query_grad_ref[...] = query_acc[...]
        latent_grad_ref[...] = latent_acc[...].astype(BF)
        rope_grad_ref[...] = rope_acc[...].astype(BF)


def whole(shape):
    return pl.BlockSpec(shape, lambda head: (0,) * len(shape))


def attend(weights, query_t, latent, rope, cos_t, sin_t, bias_t, query_rows):
    row_total, col_total, pack_rows, pack_cols = weights.shape
    here = pack_cols // HEAD
    heads = row_total * here
    length, local = bias_t.shape
    tile = math.gcd(length, 256)
    return pl.pallas_call(
        functools.partial(attend_kernel, query_rows, tile),
        grid=(heads,),
        in_specs=[
            pl.BlockSpec(
                (1, col_total, pack_rows, HEAD), lambda head: (head // here, 0, 0, head % here)
            ),
            whole(query_t.shape),
            whole(latent.shape),
            whole(rope.shape),
            whole(cos_t.shape),
            whole(sin_t.shape),
            whole(bias_t.shape),
        ],
        out_specs=[
            pl.BlockSpec((VDIM, local), lambda head: (head, 0)),
            pl.BlockSpec((1, 1, local), lambda head: (head, 0, 0)),
        ],
        out_shape=[
            jax.ShapeDtypeStruct((heads * VDIM, local), BF),
            jax.ShapeDtypeStruct((heads, 1, local), F32),
        ],
        scratch_shapes=[pltpu.VMEM((length, local), F32)],
        compiler_params=pltpu.CompilerParams(
            dimension_semantics=("arbitrary",), vmem_limit_bytes=48 * 1024 * 1024
        ),
        cost_estimate=pl.CostEstimate(
            flops=heads * 2 * local * length * 512,
            bytes_accessed=weights.size * 2,
            transcendentals=heads * local * length,
        ),
        name="attend",
    )(weights, query_t, latent, rope, cos_t, sin_t, bias_t)


def attend_back(
    weights, query_t, latent, latent_t, rope, cos_t, sin_t, bias_t, mixed_t, grad_t, lse, query_rows
):
    row_total, col_total, pack_rows, pack_cols = weights.shape
    here = pack_cols // HEAD
    heads = row_total * here
    length, local = bias_t.shape
    tile = math.gcd(length, 256)
    pack_spec = pl.BlockSpec(
        (1, col_total, pack_rows, HEAD), lambda head: (head // here, 0, 0, head % here)
    )
    return pl.pallas_call(
        functools.partial(attend_back_kernel, query_rows, tile),
        grid=(heads,),
        in_specs=[
            pack_spec,
            whole(query_t.shape),
            whole(latent.shape),
            whole(latent_t.shape),
            whole(rope.shape),
            whole(cos_t.shape),
            whole(sin_t.shape),
            whole(bias_t.shape),
            pl.BlockSpec((VDIM, local), lambda head: (head, 0)),
            pl.BlockSpec((VDIM, local), lambda head: (head, 0)),
            pl.BlockSpec((1, 1, local), lambda head: (head, 0, 0)),
        ],
        out_specs=[
            pack_spec,
            whole(query_t.shape),
            whole(latent.shape),
            whole(rope.shape),
        ],
        out_shape=[
            jax.ShapeDtypeStruct(weights.shape, BF),
            jax.ShapeDtypeStruct(query_t.shape, F32),
            jax.ShapeDtypeStruct(latent.shape, BF),
            jax.ShapeDtypeStruct(rope.shape, BF),
        ],
        scratch_shapes=[
            pltpu.VMEM(query_t.shape, F32),
            pltpu.VMEM(latent.shape, F32),
            pltpu.VMEM(rope.shape, F32),
            pltpu.VMEM((length, HEAD), BF),
        ],
        compiler_params=pltpu.CompilerParams(
            dimension_semantics=("arbitrary",), vmem_limit_bytes=48 * 1024 * 1024
        ),
        cost_estimate=pl.CostEstimate(
            flops=heads * 2 * local * length * 1280,
            bytes_accessed=weights.size * 4,
            transcendentals=heads * local * length,
        ),
        name="attend_back",
    )(weights, query_t, latent, latent_t, rope, cos_t, sin_t, bias_t, mixed_t, grad_t, lse)


def partial_rows(product):
    return lax.psum_scatter(
        product.astype(BF), "row", scatter_dimension=0, tiled=True
    ).astype(F32)


def token_rows(values):
    return lax.all_gather(values, "row", axis=0, tiled=True)


def pad_to(values, width):
    return jnp.pad(values, ((0, 0), (0, width - values.shape[1])))


def body(
    inputs,
    segments,
    valid_mask,
    teacher,
    cotangent,
    query_down,
    latent_down,
    query_up,
    latent_up,
    output_weight,
    gate_weight,
    up_weight,
    down_weight,
    attn_gain,
    query_gain,
    latent_gain,
    mlp_gain,
):
    both_axes = ("row", "col")
    row_total = lax.axis_size("row")
    col_total = lax.axis_size("col")
    devices = row_total * col_total
    row_rank = lax.axis_index("row")
    local_rows, width = inputs.shape
    length = segments.shape[0]
    q_rank = query_down.shape[1]
    kv_wide = latent_down.shape[1]
    lat_wide = q_rank + kv_wide
    down_rows = query_down.shape[0]
    q_part, kv_part = query_gain.shape[0], latent_gain.shape[0]
    heads_here = output_weight.shape[0] // VDIM
    query_rows = query_up.shape[0]
    offset = row_rank * local_rows

    count = jnp.sum(valid_mask)
    count_parts = jnp.stack([count // 256, count % 256]).astype(F32)
    misc = jnp.concatenate(
        [query_gain.astype(F32), latent_gain.astype(F32), count_parts]
    )
    misc = jnp.pad(misc, (0, down_rows - misc.shape[0])).astype(BF)
    down_pack = jnp.concatenate(
        [query_down, latent_down, attn_gain[:, None], mlp_gain[:, None], misc[:, None]], axis=1
    )
    pack_wide = -(-(lat_wide + 3) // 128) * 128
    down_all = lax.all_gather(pad_to(down_pack, pack_wide), both_axes, axis=0, tiled=True)
    down_w = down_all[:, :lat_wide]
    attn_g = down_all[:, lat_wide].astype(F32)
    mlp_g = down_all[:, lat_wide + 1].astype(F32)
    misc_all = down_all[:, lat_wide + 2].astype(F32).reshape(devices, down_rows)
    query_g = misc_all[:, :q_part].reshape(-1)
    latent_g = misc_all[:, q_part : q_part + kv_part].reshape(-1)
    counts = jnp.sum(misc_all[:, q_part + kv_part : q_part + kv_part + 2], axis=0)
    valid_total = counts[0] * 256.0 + counts[1]

    query_pack = jnp.pad(
        query_up.reshape(query_rows, heads_here, NOPE + ROPE),
        ((0, 0), (0, 0), (0, HEAD - NOPE - ROPE)),
    ).reshape(query_rows, heads_here * HEAD)
    up_pack = jnp.concatenate([query_pack, latent_up], axis=0)
    pack_rows = up_pack.shape[0]
    head_w = lax.all_gather(up_pack, both_axes, axis=0, tiled=True).reshape(
        row_total, col_total, pack_rows, heads_here * HEAD
    )
    out_all = lax.all_gather(output_weight.T, both_axes, axis=0, tiled=True).reshape(
        row_total, width, heads_here * VDIM
    )
    gate_full, up_full, down_t = (
        lax.all_gather(gate_weight, "col", axis=0, tiled=True),
        lax.all_gather(up_weight, "col", axis=0, tiled=True),
        lax.all_gather(down_weight.T, "col", axis=0, tiled=True),
    )

    cosine, sine = rotary(segments)
    cos_here = lax.dynamic_slice_in_dim(cosine, offset, local_rows, 0)
    sin_here = lax.dynamic_slice_in_dim(sine, offset, local_rows, 0)
    tokens_f = inputs.astype(F32)
    normed, normed_unit = root_norm(tokens_f, attn_g)
    normed_b = normed.astype(BF)
    lat = dot_plain(normed_b, down_w)
    query_lat, kv_lat = lat[:, :q_rank], lat[:, q_rank:]
    query_norm, query_unit = root_norm(query_lat, query_g)
    kv_norm, kv_unit = root_norm(kv_lat[:, :KV_RANK], latent_g)
    key_rope = rotate(kv_lat[:, KV_RANK:], cos_here, sin_here)
    query_nb = query_norm.astype(BF)
    latent_pack = jnp.concatenate(
        [
            kv_norm,
            jnp.zeros((local_rows, NOPE), F32),
            key_rope,
            jnp.zeros((local_rows, HEAD - NOPE - ROPE), F32),
        ],
        axis=1,
    ).astype(BF)
    latent_all = token_rows(latent_pack)
    kv_all = latent_all[:, :KV_RANK]
    rope_all = latent_all[:, KV_RANK:]

    query_at = offset + jnp.arange(local_rows, dtype=jnp.int32)
    query_seg = lax.dynamic_slice_in_dim(segments, offset, local_rows, 0)
    key_at = jnp.arange(length, dtype=jnp.int32)
    allowed_t = (key_at[:, None] <= query_at[None, :]) & (
        (segments[:, None] == 0) | (segments[:, None] == query_seg[None, :])
    )
    bias_t = jnp.where(allowed_t, 0.0, HIDE).astype(F32)
    query_t = query_nb.T
    cos_t, sin_t = cos_here.T, sin_here.T
    mixed_t, lse = attend(head_w, query_t, kv_all, rope_all, cos_t, sin_t, bias_t, query_rows)
    mixed_heads = mixed_t.reshape(row_total, heads_here * VDIM, local_rows)
    attn_sum = dot_dims(mixed_heads, out_all, (0, 1), (0, 2))

    residual = tokens_f + RES * attn_sum
    mlp_in, mlp_unit = root_norm(residual, mlp_g)
    mlp_all = token_rows(mlp_in.astype(BF))
    gate_act = dot_plain(mlp_all, gate_full)
    up_act = dot_plain(mlp_all, up_full)
    gate_sig = jax.nn.sigmoid(gate_act)
    silu_val = gate_act * gate_sig
    hidden = (silu_val * up_act).astype(BF)
    outputs = residual + RES * partial_rows(dot_trans_right(hidden, down_t))
    error_val = outputs - teacher.astype(F32)
    weight_v = valid_mask.astype(F32)[:, None]
    total_tokens = local_rows * row_total * col_total
    squared = 0.5 * jnp.sum(weight_v * error_val * error_val)
    out_grad = cotangent.astype(F32) + total_tokens / valid_total * weight_v * error_val
    branch_grad = token_rows((RES * out_grad).astype(BF))
    hidden_grad = dot_plain(branch_grad, down_t)
    gate_grad = (hidden_grad * up_act * gate_sig * (1.0 + gate_act * (1.0 - gate_sig))).astype(BF)
    up_grad = (hidden_grad * silu_val).astype(BF)
    mlp_in_grad = partial_rows(
        dot_trans_right(gate_grad, gate_full) + dot_trans_right(up_grad, up_full)
    )
    gate_wg = dot_trans_left(mlp_all, gate_grad).astype(BF)
    up_wg = dot_trans_left(mlp_all, up_grad).astype(BF)
    down_wg = dot_trans_left(branch_grad, hidden).astype(BF)
    gate_wg, up_wg, down_wg = (
        lax.psum_scatter(gate_wg, "col", scatter_dimension=0, tiled=True).astype(F32),
        lax.psum_scatter(up_wg, "col", scatter_dimension=0, tiled=True).astype(F32),
        lax.psum_scatter(down_wg, "col", scatter_dimension=0, tiled=True).astype(F32).T,
    )
    residual_part, mlp_gain_grad = norm_back(mlp_in_grad, mlp_unit, residual, mlp_g)
    residual_grad = out_grad + residual_part

    attn_grad_in = (RES * residual_grad).astype(BF)
    grad_t = dot_dims(out_all, attn_grad_in, (1,), (1,)).astype(BF)
    out_wg = dot_dims(attn_grad_in, mixed_heads, (0,), (2,)).astype(BF)
    out_wg = jnp.transpose(out_wg, (1, 0, 2)).reshape(row_total * width, heads_here * VDIM)
    out_wg = lax.psum_scatter(out_wg, both_axes, scatter_dimension=0, tiled=True).astype(F32).T
    head_wg, query_back_t, kv_back, rope_back = attend_back(
        head_w, query_t, kv_all, kv_all.T, rope_all, cos_t, sin_t, bias_t, mixed_t,
        grad_t.reshape(mixed_t.shape), lse, query_rows,
    )
    head_wg = lax.psum_scatter(
        head_wg.reshape(devices * pack_rows, heads_here * HEAD),
        both_axes, scatter_dimension=0, tiled=True,
    ).astype(F32)
    qu_wg = head_wg[:query_rows].reshape(query_rows, heads_here, HEAD)[:, :, : NOPE + ROPE]
    qu_wg = qu_wg.reshape(query_rows, heads_here * (NOPE + ROPE))
    kvu_wg = head_wg[query_rows:]
    latent_back = partial_rows(jnp.concatenate([kv_back, rope_back], axis=1))
    kv_norm_grad = latent_back[:, :KV_RANK]
    rope_grad = latent_back[:, KV_RANK + NOPE : KV_RANK + NOPE + ROPE]
    query_norm_grad = query_back_t.T
    query_lat_grad, query_gain_grad = norm_back(query_norm_grad, query_unit, query_lat, query_g)
    kv_lat_part, latent_gain_grad = norm_back(kv_norm_grad, kv_unit, kv_lat[:, :KV_RANK], latent_g)
    lat_grad = jnp.concatenate(
        [query_lat_grad, kv_lat_part, rotate(rope_grad, cos_here, -sin_here)], axis=-1
    ).astype(BF)
    lat_wg = dot_trans_left(normed_b, lat_grad)
    normed_grad = dot_trans_right(lat_grad, down_w)
    input_part, attention_gain_gradient = norm_back(normed_grad, normed_unit, tokens_f, attn_g)
    input_grad = residual_grad + input_part

    loss_high = squared.astype(BF).astype(F32)
    loss_low = squared - loss_high
    misc_grad = jnp.concatenate(
        [
            query_gain_grad.reshape(devices, q_part),
            latent_gain_grad.reshape(devices, kv_part),
            jnp.broadcast_to(loss_high, (devices, 1)),
            jnp.broadcast_to(loss_low, (devices, 1)),
        ],
        axis=1,
    )
    misc_grad = pad_to(misc_grad, down_rows).reshape(devices * down_rows, 1)
    small = jnp.concatenate(
        [lat_wg, attention_gain_gradient[:, None], mlp_gain_grad[:, None], misc_grad], axis=1
    )
    small = lax.psum_scatter(
        pad_to(small, pack_wide), both_axes, scatter_dimension=0, tiled=True
    )
    misc_sum = small[:, lat_wide + 2]
    at = q_part + kv_part
    loss = (misc_sum[at] + misc_sum[at + 1]) / valid_total
    return (
        outputs.astype(BF),
        loss,
        input_grad,
        small[:, :q_rank],
        small[:, q_rank:lat_wide],
        qu_wg,
        kvu_wg,
        out_wg,
        gate_wg,
        up_wg,
        down_wg,
        small[:, lat_wide],
        misc_sum[:q_part],
        misc_sum[q_part : q_part + kv_part],
        small[:, lat_wide + 1],
    )


def solution(mesh):
    in_specs = (
        P(("col", "row"), None),
        P("col"),
        P(("col", "row")),
        P(("col", "row"), None),
        P(("col", "row"), None),
        P(("row", "col"), None),
        P(("row", "col"), None),
        P("col", "row"),
        P("col", "row"),
        P("row", "col"),
        P("col", "row"),
        P("col", "row"),
        P("row", "col"),
        P(("row", "col")),
        P(("row", "col")),
        P(("row", "col")),
        P(("row", "col")),
    )
    out_specs = (
        P(("col", "row"), None),
        P(),
        P(("col", "row"), None),
        P(("row", "col"), None),
        P(("row", "col"), None),
        P("col", "row"),
        P("col", "row"),
        P("row", "col"),
        P("col", "row"),
        P("col", "row"),
        P("row", "col"),
        P(("row", "col")),
        P(("row", "col")),
        P(("row", "col")),
        P(("row", "col")),
    )
    return jax.shard_map(body, mesh=mesh, in_specs=in_specs, out_specs=out_specs, check_vma=False)
```

```python
import functools
import math

import jax
import jax.numpy as jnp
from jax import lax
from jax.experimental import pallas as pl
from jax.experimental.pallas import tpu as pltpu
from jax.sharding import PartitionSpec as P

NOPE = 64
ROPE = 32
VDIM = 64
KV_RANK = 256
CONTS = 4
HEAD = 128

EPS = 1e-05
RES = 1.4 / math.sqrt(62.0)
BASE = 10000.0
SCALE = (NOPE + ROPE) ** (-0.5)
LOG2E = math.log2(math.e)
HIDE = -1e30
BF = jnp.bfloat16
F32 = jnp.float32


def dot_plain(left_op, right_op):
    return jnp.dot(left_op, right_op, preferred_element_type=F32)


def dot_dims(left_op, right_op, left_dims, right_dims):
    return lax.dot_general(
        left_op, right_op, ((left_dims, right_dims), ((), ())), preferred_element_type=F32
    )


def dot_trans_left(left_op, right_op):
    return dot_dims(left_op, right_op, (0,), (0,))


def dot_trans_right(left_op, right_op):
    return dot_dims(left_op, right_op, (1,), (1,))


def root_norm(values, gain):
    unit_rows = values * lax.rsqrt(jnp.mean(values * values, axis=-1, keepdims=True) + EPS)
    return (unit_rows * gain, unit_rows)


def norm_back(grad_rows, unit_rows, values, gain):
    factor = lax.rsqrt(jnp.mean(values * values, axis=-1, keepdims=True) + EPS)
    scaled = grad_rows * gain
    value_grad = factor * (
        scaled - unit_rows * jnp.mean(scaled * unit_rows, axis=-1, keepdims=True)
    )
    return (value_grad, jnp.sum(grad_rows * unit_rows, axis=0))


def rotary(segments):
    length = segments.shape[0]
    indices = jnp.arange(length, dtype=jnp.int32)
    labels = jnp.arange(CONTS + 1, dtype=jnp.int32)
    member = (segments[:, None] == labels[None, :]).astype(jnp.int32)
    counts = jnp.sum(member, axis=0)
    starts = jnp.cumsum(counts) - counts
    first_at = jnp.sum(member * starts[None, :], axis=1)
    places = jnp.where(segments == 0, indices, counts[0] + indices - first_at).astype(F32)
    freqs = BASE ** (-jnp.arange(ROPE // 2, dtype=F32) * 2.0 / ROPE)
    angles = places[:, None] * freqs[None, :]
    return (jnp.cos(angles), jnp.sin(angles))


def rotate(values, cosine, sine):
    half = values.shape[-1] // 2
    first_half = values[..., :half]
    second_half = values[..., half:]
    return jnp.concatenate(
        [first_half * cosine - second_half * sine, second_half * cosine + first_half * sine],
        axis=-1,
    )


def head_weights(weights_ref, query_rows):
    block = weights_ref[0]
    col_total = block.shape[0]
    query_w = block[:, :query_rows, :].reshape(col_total * query_rows, HEAD)
    latent_w = block[:, query_rows:, :].reshape(-1, HEAD)
    return (query_w, latent_w)


def head_vectors(weights_ref, query_t_ref, latent_ref, rope_ref, cos_ref, sin_ref, query_rows):
    query_w, latent_w = head_weights(weights_ref, query_rows)
    half = ROPE // 2
    proj_t = dot_plain(query_w.T, query_t_ref[...])
    first, second = proj_t[NOPE : NOPE + half], proj_t[NOPE + half : NOPE + ROPE]
    cosine, sine = cos_ref[...], sin_ref[...]
    query_t = jnp.concatenate(
        [
            proj_t[:NOPE],
            first * cosine - second * sine,
            second * cosine + first * sine,
            proj_t[NOPE + ROPE :],
        ],
        axis=0,
    ).astype(BF)
    both = dot_plain(latent_ref[...], latent_w).astype(BF)
    lane = lax.broadcasted_iota(jnp.int32, both.shape, 1)
    keys = jnp.where(lane < NOPE, both, rope_ref[...])
    return (query_w, latent_w, query_t, keys, both)


def attend_kernel(
    query_rows, tile, weights_ref, query_t_ref, latent_ref, rope_ref, cos_ref, sin_ref, bias_ref,
    mixed_ref, lse_ref, scores_ref,
):
    _, _, query_t, keys, both = head_vectors(
        weights_ref, query_t_ref, latent_ref, rope_ref, cos_ref, sin_ref, query_rows
    )
    values_t = both.T[NOPE:]
    length = keys.shape[0]
    top = None
    for begin in range(0, length, tile):
        part = dot_plain(keys[begin : begin + tile], query_t) * (SCALE * LOG2E)
        part = part + bias_ref[begin : begin + tile, :]
        scores_ref[begin : begin + tile, :] = part
        tile_top = jnp.max(part, axis=0, keepdims=True)
        top = tile_top if top is None else jnp.maximum(top, tile_top)
    total, out_t = None, None
    for begin in range(0, length, tile):
        expo = jnp.exp2(scores_ref[begin : begin + tile, :] - top)
        tile_sum = jnp.sum(expo, axis=0, keepdims=True)
        term = dot_plain(values_t[:, begin : begin + tile], expo.astype(BF))
        total = tile_sum if total is None else total + tile_sum
        out_t = term if out_t is None else out_t + term
    mixed_ref[...] = (out_t / total).astype(BF)
    lse_ref[0] = top + jnp.log2(total)


def attend_back_kernel(
    query_rows, tile, weights_ref, query_t_ref, latent_ref, latent_t_ref, rope_ref, cos_ref,
    sin_ref, bias_ref, mixed_ref, grad_ref, lse_ref,
    weights_grad_ref, query_grad_ref, latent_grad_ref, rope_grad_ref,
    query_acc, latent_acc, rope_acc, both_scr,
):
    head = pl.program_id(0)
    query_w, latent_w, query_t, keys, both = head_vectors(
        weights_ref, query_t_ref, latent_ref, rope_ref, cos_ref, sin_ref, query_rows
    )

    @pl.when(head == 0)
    def _():
        query_acc[...] = jnp.zeros_like(query_acc)
        latent_acc[...] = jnp.zeros_like(latent_acc)
        rope_acc[...] = jnp.zeros_like(rope_acc)

    keys_t = keys.T
    query = query_t.T
    grad_t = grad_ref[...]
    delta = jnp.sum(
        grad_t.astype(F32) * mixed_ref[...].astype(F32), axis=0, keepdims=True
    )
    grad_pad_t = jnp.concatenate([jnp.zeros_like(grad_t), grad_t], axis=0)
    grad_pad = grad_pad_t.T
    lse = lse_ref[0]
    length = keys.shape[0]
    query_back_t = None
    for begin in range(0, length, tile):
        rows = slice(begin, begin + tile)
        scores = dot_plain(keys[rows], query_t) * (SCALE * LOG2E)
        probs = jnp.exp2(scores + bias_ref[rows, :] - lse)
        prob_grad = dot_plain(both[rows], grad_pad_t)
        score_grad = (probs * (prob_grad - delta)).astype(BF)
        term = dot_plain(keys_t[:, rows], score_grad)
        query_back_t = term if query_back_t is None else query_back_t + term
        key_back = dot_plain(score_grad, query) * SCALE
        value_back = dot_plain(probs.astype(BF), grad_pad)
        lane = lax.broadcasted_iota(jnp.int32, key_back.shape, 1)
        rope_acc[rows, :] += key_back
        both_scr[rows, :] = jnp.where(lane < NOPE, key_back, value_back).astype(BF)
    query_back_t = query_back_t * SCALE
    half = ROPE // 2
    first, second = query_back_t[NOPE : NOPE + half], query_back_t[NOPE + half : NOPE + ROPE]
    cosine, sine = cos_ref[...], sin_ref[...]
    query_back_t = jnp.concatenate(
        [
            query_back_t[:NOPE],
            first * cosine + second * sine,
            second * cosine - first * sine,
            jnp.zeros_like(query_back_t[NOPE + ROPE :]),
        ],
        axis=0,
    ).astype(BF)
    both_back = both_scr[...]
    query_acc[...] += dot_plain(query_w, query_back_t)
    latent_acc[...] += dot_trans_right(both_back, latent_w)
    query_wg = dot_trans_right(query_t_ref[...], query_back_t)
    latent_wg = dot_plain(latent_t_ref[...], both_back)
    col_total = weights_ref.shape[1]
    weights_grad_ref[0, :, :query_rows, :] = query_wg.astype(BF).reshape(col_total, query_rows, HEAD)
    weights_grad_ref[0, :, query_rows:, :] = latent_wg.astype(BF).reshape(col_total, -1, HEAD)

    @pl.when(head == pl.num_programs(0) - 1)
    def _():
        query_grad_ref[...] = query_acc[...]
        latent_grad_ref[...] = latent_acc[...]
        rope_grad_ref[...] = rope_acc[...]


def whole(shape):
    return pl.BlockSpec(shape, lambda head: (0,) * len(shape))


def attend(weights, query_t, latent, rope, cos_t, sin_t, bias_t, query_rows, block):
    _, col_total, pack_rows, pack_cols = weights.shape
    heads = pack_cols // HEAD
    length, local = bias_t.shape
    tile = math.gcd(length, 256)
    return pl.pallas_call(
        functools.partial(attend_kernel, query_rows, tile),
        grid=(heads,),
        in_specs=[
            pl.BlockSpec((1, col_total, pack_rows, HEAD), lambda head: (block, 0, 0, head)),
            whole(query_t.shape),
            whole(latent.shape),
            whole(rope.shape),
            whole(cos_t.shape),
            whole(sin_t.shape),
            whole(bias_t.shape),
        ],
        out_specs=[
            pl.BlockSpec((VDIM, local), lambda head: (head, 0)),
            pl.BlockSpec((1, 1, local), lambda head: (head, 0, 0)),
        ],
        out_shape=[
            jax.ShapeDtypeStruct((heads * VDIM, local), BF),
            jax.ShapeDtypeStruct((heads, 1, local), F32),
        ],
        scratch_shapes=[pltpu.VMEM((length, local), F32)],
        compiler_params=pltpu.CompilerParams(
            dimension_semantics=("arbitrary",), vmem_limit_bytes=48 * 1024 * 1024
        ),
        cost_estimate=pl.CostEstimate(
            flops=heads * 1_700_000_000,
            bytes_accessed=weights[0].size * 2,
            transcendentals=heads * local * length,
        ),
        name="attend",
    )(weights, query_t, latent, rope, cos_t, sin_t, bias_t)


def attend_back(
    weights, query_t, latent, latent_t, rope, cos_t, sin_t, bias_t, mixed_t, grad_t, lse,
    query_rows, block,
):
    _, col_total, pack_rows, pack_cols = weights.shape
    heads = pack_cols // HEAD
    length, local = bias_t.shape
    tile = math.gcd(length, 256)
    return pl.pallas_call(
        functools.partial(attend_back_kernel, query_rows, tile),
        grid=(heads,),
        in_specs=[
            pl.BlockSpec((1, col_total, pack_rows, HEAD), lambda head: (block, 0, 0, head)),
            whole(query_t.shape),
            whole(latent.shape),
            whole(latent_t.shape),
            whole(rope.shape),
            whole(cos_t.shape),
            whole(sin_t.shape),
            whole(bias_t.shape),
            pl.BlockSpec((VDIM, local), lambda head: (head, 0)),
            pl.BlockSpec((VDIM, local), lambda head: (block * heads + head, 0)),
            pl.BlockSpec((1, 1, local), lambda head: (head, 0, 0)),
        ],
        out_specs=[
            pl.BlockSpec((1, col_total, pack_rows, HEAD), lambda head: (0, 0, 0, head)),
            whole(query_t.shape),
            whole(latent.shape),
            whole(rope.shape),
        ],
        out_shape=[
            jax.ShapeDtypeStruct((1,) + weights.shape[1:], BF),
            jax.ShapeDtypeStruct(query_t.shape, F32),
            jax.ShapeDtypeStruct(latent.shape, F32),
            jax.ShapeDtypeStruct(rope.shape, F32),
        ],
        scratch_shapes=[
            pltpu.VMEM(query_t.shape, F32),
            pltpu.VMEM(latent.shape, F32),
            pltpu.VMEM(rope.shape, F32),
            pltpu.VMEM((length, HEAD), BF),
        ],
        compiler_params=pltpu.CompilerParams(
            dimension_semantics=("arbitrary",), vmem_limit_bytes=48 * 1024 * 1024
        ),
        cost_estimate=pl.CostEstimate(
            flops=heads * 4_200_000_000,
            bytes_accessed=weights[0].size * 4,
            transcendentals=heads * local * length,
        ),
        name="attend_back",
    )(weights, query_t, latent, latent_t, rope, cos_t, sin_t, bias_t, mixed_t, grad_t, lse)


def weight_grad_kernel(chunks, *refs):
    lefts, rights, out_ref = refs[:chunks], refs[chunks : 2 * chunks], refs[2 * chunks]
    total = None
    for left_ref, right_ref in zip(lefts, rights):
        term = dot_plain(left_ref[...].T, right_ref[...])
        total = term if total is None else total + term
    out_ref[...] = total.astype(out_ref.dtype)


def weight_grad(lefts, rights, name):
    chunks = len(lefts)
    rows, width = lefts[0].shape
    units = rights[0].shape[1]
    tile = math.gcd(width, 256)
    return pl.pallas_call(
        functools.partial(weight_grad_kernel, chunks),
        grid=(width // tile,),
        in_specs=[pl.BlockSpec((rows, tile), lambda step: (0, step))] * chunks
        + [pl.BlockSpec((rows, units), lambda step: (0, 0))] * chunks,
        out_specs=pl.BlockSpec((tile, units), lambda step: (step, 0)),
        out_shape=jax.ShapeDtypeStruct((width, units), BF),
        compiler_params=pltpu.CompilerParams(
            dimension_semantics=("arbitrary",), vmem_limit_bytes=48 * 1024 * 1024
        ),
        cost_estimate=pl.CostEstimate(
            flops=2 * chunks * rows * width * units,
            bytes_accessed=2 * (chunks * rows + units) * width,
            transcendentals=0,
        ),
        name=name,
    )(*lefts, *rights)


together = lax.optimization_barrier


class Task:
    def __init__(self, steps):
        self.steps, self.state, self.value, self.over = steps, None, None, False

    def advance(self):
        if not self.over:
            try:
                return self.steps.send(self.state)
            except StopIteration as stop:
                self.value, self.over = stop.value, True
        return ()

    def result(self):
        self.advance()
        assert self.over
        return self.value


def slot(*tasks):
    states = together(tuple(task.advance() for task in tasks))
    for task, state in zip(tasks, states):
        task.state = state


def slots(count, *tasks):
    for _ in range(count):
        slot(*tasks)


def gather_steps(values):
    total = lax.axis_size("row")
    up, down = [None], [None]
    ways = (values, values)
    for step in range(1, total):
        ways = yield (
            lax.ppermute(ways[0], "row", [(i, i + 1) for i in range(step - 1, total - 1)]),
            lax.ppermute(ways[1], "row", [(i, i - 1) for i in range(1, total - step + 1)]),
        )
        up.append(ways[0])
        down.append(ways[1])
    return jnp.concatenate([values] + [up[step] + down[total - step] for step in range(1, total)])


def add_parts(left_op, right_op):
    return (left_op.astype(F32) + right_op.astype(F32)).astype(BF)


def reduce_steps(parts):
    total = lax.axis_size("row")
    ways = None
    for step in range(total - 1):
        sends = (parts[step + 1], parts[total - 1 - step])
        if step > 0:
            sends = (add_parts(sends[0], ways[0]), add_parts(sends[1], ways[1]))
        ways = yield (
            lax.ppermute(sends[0], "row", [(i, i + 1) for i in range(step + 1)]),
            lax.ppermute(sends[1], "row", [(i, i - 1) for i in range(total - 1 - step, total)]),
        )
    return parts[0].astype(F32) + ways[0].astype(F32) + ways[1].astype(F32)


def reduce_row_steps(line):
    total = lax.axis_size("row")
    row_rank = lax.axis_index("row")
    parts = [pick(line, lax.rem(row_rank + total - step, total), 0) for step in range(total)]
    return (yield from reduce_steps(parts))


def product_steps(product):
    total = lax.axis_size("row")
    rows = product.shape[0] // total
    parts = [product[at * rows : (at + 1) * rows] for at in range(total)]
    return (yield from reduce_steps(parts))


def swap(values, bit):
    total = lax.axis_size("col")
    return lax.ppermute(values, "col", [(i, i ^ bit) for i in range(total)])


def pick(values, index, axis):
    return lax.dynamic_index_in_dim(values, index, axis, keepdims=False)


def far_bits():
    bits, bit = [], 2
    while bit < lax.axis_size("col"):
        bits.append(bit)
        bit *= 2
    return bits


def gather_col_steps(first, second):
    halves = [[(0, first)], [(0, second)]]
    orders = [far_bits()[::-1] + [1], far_bits() + [1]]
    for step in range(len(orders[0])):
        got = yield tuple(
            tuple(swap(part, order[step]) for _, part in half)
            for half, order in zip(halves, orders)
        )
        halves = [
            half + [(away + order[step], part) for (away, _), part in zip(half, parts)]
            for half, order, parts in zip(halves, orders, got)
        ]
    return halves


def reduce_col_steps(blocks):
    col_rank = lax.axis_index("col")
    bits = far_bits()
    dims = [bits[::-1] + [1] for _ in blocks]
    orders = [[1] + (bits if at % 2 == 0 else bits[::-1]) for at in range(len(blocks))]
    blocks = [block.reshape((2,) * len(dims[0]) + block.shape[1:]) for block in blocks]
    for step in range(len(dims[0])):
        keeps, sends = [], []
        for block, dim, order in zip(blocks, dims, orders):
            bit = order[step]
            axis, own = dim.index(bit), lax.rem(col_rank // bit, 2)
            keeps.append(pick(block, own, axis))
            sends.append(swap(pick(block, 1 - own, axis), bit))
            dim.remove(bit)
        sends = yield tuple(sends)
        blocks = [add_parts(keep, send) for keep, send in zip(keeps, sends)]
    return jnp.stack(blocks)


def reduce_all_steps(blocks):
    line = yield from reduce_col_steps(blocks)
    return (yield from reduce_row_steps(line))


def token_rows(values):
    return lax.all_gather(values, "row", axis=0, tiled=True)


def pad_to(values, width):
    return jnp.pad(values, ((0, 0), (0, width - values.shape[1])))


def body(
    inputs,
    segments,
    valid_mask,
    teacher,
    cotangent,
    query_down,
    latent_down,
    query_up,
    latent_up,
    output_weight,
    gate_weight,
    up_weight,
    down_weight,
    attn_gain,
    query_gain,
    latent_gain,
    mlp_gain,
):
    both_axes = ("row", "col")
    row_total = lax.axis_size("row")
    col_total = lax.axis_size("col")
    devices = row_total * col_total
    row_rank = lax.axis_index("row")
    local_rows, width = inputs.shape
    length = segments.shape[0]
    q_rank = query_down.shape[1]
    kv_wide = latent_down.shape[1]
    lat_wide = q_rank + kv_wide
    down_rows = query_down.shape[0]
    q_part, kv_part = query_gain.shape[0], latent_gain.shape[0]
    heads_here = output_weight.shape[0] // VDIM
    query_rows = query_up.shape[0]
    offset = row_rank * local_rows

    count = jnp.sum(valid_mask)
    count_parts = jnp.stack([count // 256, count % 256]).astype(F32)
    misc = jnp.concatenate(
        [query_gain.astype(F32), latent_gain.astype(F32), count_parts]
    )
    misc = jnp.pad(misc, (0, down_rows - misc.shape[0])).astype(BF)
    down_pack = jnp.concatenate(
        [query_down, latent_down, attn_gain[:, None], mlp_gain[:, None], misc[:, None]], axis=1
    )
    pack_wide = -(-(lat_wide + 3) // 128) * 128
    down_all = lax.all_gather(pad_to(down_pack, pack_wide), both_axes, axis=0, tiled=True)

    query_pack = jnp.pad(
        query_up.reshape(query_rows, heads_here, NOPE + ROPE),
        ((0, 0), (0, 0), (0, HEAD - NOPE - ROPE)),
    ).reshape(query_rows, heads_here * HEAD)
    up_pack = jnp.concatenate([query_pack, latent_up], axis=0)
    pack_rows = up_pack.shape[0]
    mlp_pack = jnp.concatenate([gate_weight, up_weight, down_weight.T], axis=0)
    part_rows = gate_weight.shape[0]
    half_rows = part_rows // 2
    down_all, mlp_pack = together((down_all, mlp_pack))
    mlp_w = Task(
        gather_col_steps(
            mlp_pack[: part_rows + half_rows], mlp_pack[part_rows + half_rows :]
        )
    )

    attn_g = down_all[:, lat_wide].astype(F32)
    mlp_g = down_all[:, lat_wide + 1].astype(F32)
    misc_all = down_all[:, lat_wide + 2].astype(F32).reshape(devices, down_rows)
    query_g = misc_all[:, :q_part].reshape(-1)
    latent_g = misc_all[:, q_part : q_part + kv_part].reshape(-1)
    counts = jnp.sum(misc_all[:, q_part + kv_part : q_part + kv_part + 2], axis=0)
    valid_total = counts[0] * 256.0 + counts[1]

    cosine, sine = rotary(segments)
    cos_here = lax.dynamic_slice_in_dim(cosine, offset, local_rows, 0)
    sin_here = lax.dynamic_slice_in_dim(sine, offset, local_rows, 0)
    tokens_f = inputs.astype(F32)
    normed, normed_unit = root_norm(tokens_f, attn_g)
    normed_b = normed.astype(BF)
    lat = dot_plain(normed_b, down_all)
    query_lat, kv_lat = lat[:, :q_rank], lat[:, q_rank:lat_wide]
    query_norm, query_unit = root_norm(query_lat, query_g)
    kv_norm, kv_unit = root_norm(kv_lat[:, :KV_RANK], latent_g)
    key_rope = rotate(kv_lat[:, KV_RANK:], cos_here, sin_here)
    query_nb = query_norm.astype(BF)
    latent_pack = jnp.concatenate(
        [
            kv_norm,
            jnp.zeros((local_rows, NOPE), F32),
            key_rope,
            jnp.zeros((local_rows, HEAD - NOPE - ROPE), F32),
        ],
        axis=1,
    ).astype(BF)
    latent_all = token_rows(latent_pack)
    got = mlp_w.advance()
    latent_all, up_pack, got = together((latent_all, up_pack, got))
    mlp_w.state = got
    head_w = lax.all_gather(up_pack, both_axes, axis=0, tiled=True)
    got = mlp_w.advance()
    head_w, out_here, got = together((head_w, output_weight.T, got))
    mlp_w.state = got
    head_w = head_w.reshape(row_total, col_total, pack_rows, heads_here * HEAD)
    out_all = lax.all_gather(out_here, both_axes, axis=0, tiled=True).reshape(
        row_total, width, heads_here * VDIM
    )
    kv_all = latent_all[:, :KV_RANK]
    rope_all = latent_all[:, KV_RANK:]

    query_at = offset + jnp.arange(local_rows, dtype=jnp.int32)
    query_seg = lax.dynamic_slice_in_dim(segments, offset, local_rows, 0)
    key_at = jnp.arange(length, dtype=jnp.int32)
    allowed_t = (key_at[:, None] <= query_at[None, :]) & (
        (segments[:, None] == 0) | (segments[:, None] == query_seg[None, :])
    )
    bias_t = jnp.where(allowed_t, 0.0, HIDE).astype(F32)
    query_t = query_nb.T
    cos_t, sin_t = cos_here.T, sin_here.T
    mixed = [
        attend(head_w, query_t, kv_all, rope_all, cos_t, sin_t, bias_t, query_rows, block)
        for block in range(row_total)
    ]
    while not mlp_w.over:
        mlp_w.state = mlp_w.advance()
    gate_full = jnp.zeros((col_total, part_rows, mlp_pack.shape[1]), BF)
    up_full, down_t = gate_full, gate_full
    col_rank = lax.axis_index("col")

    def put(array, part, away, row):
        return lax.dynamic_update_slice(
            array, part[None], (jnp.bitwise_xor(col_rank, away), row, 0)
        )

    for (away, one), (away_b, two) in zip(*[sorted(h, key=lambda p: p[0]) for h in mlp_w.value]):
        gate_full = put(gate_full, one[:part_rows], away, 0)
        up_full = put(up_full, one[part_rows:], away, 0)
        up_full = put(up_full, two[: part_rows - half_rows], away_b, half_rows)
        down_t = put(down_t, two[part_rows - half_rows :], away_b, 0)
    gate_full, up_full, down_t = (
        gate_full.reshape(width, -1), up_full.reshape(width, -1), down_t.reshape(width, -1)
    )
    mixed, out_all, gate_full, up_full, down_t = together(
        (mixed, out_all, gate_full, up_full, down_t)
    )
    attn_sum = None
    for block in range(row_total):
        term = dot_dims(mixed[block][0], out_all[block], (0,), (1,))
        attn_sum = term if attn_sum is None else attn_sum + term

    residual = tokens_f + RES * attn_sum
    mlp_in, mlp_unit = root_norm(residual, mlp_g)
    mlp_b = mlp_in.astype(BF)
    weight_v = valid_mask.astype(F32)[:, None]
    out_scale = local_rows * devices / valid_total
    rows = local_rows // 2
    parts = [slice(0, rows), slice(rows, 2 * rows)]

    def forward_steps(tokens):
        gate_act = yield dot_plain(tokens, gate_full)
        up_act = dot_plain(tokens, up_full)
        hidden = yield (gate_act * jax.nn.sigmoid(gate_act) * up_act).astype(BF)
        product = yield dot_trans_right(hidden, down_t).astype(BF)
        return (gate_act, up_act, hidden, product)

    def judge(part, down_sum):
        out_rows = residual[part] + RES * down_sum
        error_val = out_rows - teacher[part].astype(F32)
        squared = 0.5 * jnp.sum(weight_v[part] * error_val * error_val)
        grad_rows = cotangent[part].astype(F32) + out_scale * weight_v[part] * error_val
        return (out_rows.astype(BF), squared, grad_rows, (RES * grad_rows).astype(BF))

    def backward_steps(branch, gate_act, up_act):
        gate_sig = jax.nn.sigmoid(gate_act)
        hidden_grad = dot_plain(branch, down_t)
        gate_grad, up_grad = yield (
            (hidden_grad * up_act * gate_sig * (1.0 + gate_act * (1.0 - gate_sig))).astype(BF),
            (hidden_grad * gate_act * gate_sig).astype(BF),
        )
        product = yield dot_trans_right(gate_grad, gate_full)
        product = yield (product + dot_trans_right(up_grad, up_full)).astype(BF)
        return (gate_grad, up_grad, product)

    def weight_steps(work):
        got = []
        for lefts, rights, name in work:
            got.append((yield weight_grad(lefts, rights, name)))
        return got

    hops = row_total - 1
    mlp_b = mlp_in.astype(BF)
    give_0, give_1 = [Task(gather_steps(mlp_b[part])) for part in parts]
    slots(hops, give_0)
    tokens_0 = give_0.result()
    fore_0 = Task(forward_steps(tokens_0))
    slots(hops, give_1, fore_0)
    tokens_1 = give_1.result()
    fore_0 = fore_0.result()
    take_0 = Task(product_steps(fore_0[3]))
    fore_1 = Task(forward_steps(tokens_1))
    slots(hops, take_0, fore_1)
    judged_0 = judge(parts[0], take_0.result())
    fore_1 = fore_1.result()
    take_1 = Task(product_steps(fore_1[3]))
    give_0 = Task(gather_steps(judged_0[3]))
    slot(give_0)
    slots(hops - 1, give_0, take_1)
    branch_0 = give_0.result()
    back_0 = Task(backward_steps(branch_0, fore_0[0], fore_0[1]))
    slot(take_1, back_0)
    judged_1 = judge(parts[1], take_1.result())
    give_1 = Task(gather_steps(judged_1[3]))
    slots(hops - 1, give_1, back_0)
    back_0 = back_0.result()
    take_0 = Task(product_steps(back_0[2]))
    slot(give_1, take_0)
    branch_1 = give_1.result()
    back_1 = Task(backward_steps(branch_1, fore_1[0], fore_1[1]))
    slots(hops - 1, take_0, back_1)
    grad_0 = take_0.result()
    slot(back_1)
    back_1 = back_1.result()
    take_1 = Task(product_steps(back_1[2]))
    work = Task(
        weight_steps(
            [
                ([branch_0, branch_1], [fore_0[2], fore_1[2]], "down_wg"),
                ([tokens_0, tokens_1], [back_0[0], back_1[0]], "gate_wg"),
                ([tokens_0, tokens_1], [back_0[1], back_1[1]], "up_wg"),
            ]
        )
    )
    slots(max(hops, 3), take_1, work)
    grad_1 = take_1.result()
    down_wg, gate_wg, up_wg = work.result()
    outputs = jnp.concatenate([judged_0[0], judged_1[0]])
    squared = judged_0[1] + judged_1[1]
    out_grad = jnp.concatenate([judged_0[2], judged_1[2]])
    mlp_in_grad = jnp.concatenate([grad_0, grad_1])
    gate_wg, up_wg, down_wg = (
        lax.psum_scatter(gate_wg, "col", scatter_dimension=0, tiled=True).astype(F32),
        lax.psum_scatter(up_wg, "col", scatter_dimension=0, tiled=True).astype(F32),
        lax.psum_scatter(down_wg, "col", scatter_dimension=0, tiled=True).astype(F32).T,
    )
    residual_part, mlp_gain_grad = norm_back(mlp_in_grad, mlp_unit, residual, mlp_g)
    residual_grad = out_grad + residual_part

    attn_grad_in = (RES * residual_grad).astype(BF)
    grad_t = dot_dims(out_all, attn_grad_in, (1,), (1,)).astype(BF)
    out_wg = [
        dot_dims(attn_grad_in, mixed_t, (0,), (1,))
        .astype(BF)
        .reshape(col_total, -1, heads_here * VDIM)
        for mixed_t, _ in mixed
    ]
    latent_t = kv_all.T
    grad_t, out_wg = together((grad_t.reshape(-1, local_rows), out_wg))

    def back_steps():
        got = []
        for block in range(row_total):
            mixed_t, lse = mixed[block]
            wg, query_part, kv_part_back, rope_part = yield attend_back(
                head_w, query_t, kv_all, latent_t, rope_all, cos_t, sin_t, bias_t, mixed_t,
                grad_t, lse, query_rows, block,
            )
            got.append((wg[0], query_part, jnp.concatenate([kv_part_back, rope_part], axis=1)))
        return got

    steps = len(far_bits()) + 1
    backs = Task(back_steps())
    out_reduce = Task(reduce_all_steps(out_wg))
    slots(row_total, backs, out_reduce)
    backs = backs.result()
    query_back_t = sum(query_part for _, query_part, _ in backs)
    latent_back = sum(part for _, _, part in backs).astype(BF)
    latent_reduce = Task(reduce_row_steps(latent_back.reshape(row_total, local_rows, -1)))
    head_reduce = Task(reduce_all_steps([wg for wg, _, _ in backs]))
    slots(hops, latent_reduce, head_reduce, out_reduce)
    latent_back = latent_reduce.result()
    kv_norm_grad = latent_back[:, :KV_RANK]
    rope_grad = latent_back[:, KV_RANK + NOPE : KV_RANK + NOPE + ROPE]
    query_norm_grad = query_back_t.T
    query_lat_grad, query_gain_grad = norm_back(query_norm_grad, query_unit, query_lat, query_g)
    kv_lat_part, latent_gain_grad = norm_back(kv_norm_grad, kv_unit, kv_lat[:, :KV_RANK], latent_g)
    lat_grad = jnp.concatenate(
        [
            query_lat_grad,
            kv_lat_part,
            rotate(rope_grad, cos_here, -sin_here),
            jnp.zeros((local_rows, pack_wide - lat_wide), F32),
        ],
        axis=-1,
    ).astype(BF)
    lat_wg = dot_trans_left(normed_b, lat_grad)
    normed_grad = dot_trans_right(lat_grad, down_all)
    input_part, attention_gain_gradient = norm_back(normed_grad, normed_unit, tokens_f, attn_g)
    input_grad = residual_grad + input_part

    loss_high = squared.astype(BF).astype(F32)
    loss_low = squared - loss_high
    misc_grad = jnp.concatenate(
        [
            query_gain_grad.reshape(devices, q_part),
            latent_gain_grad.reshape(devices, kv_part),
            jnp.broadcast_to(loss_high, (devices, 1)),
            jnp.broadcast_to(loss_low, (devices, 1)),
        ],
        axis=1,
    )
    misc_grad = pad_to(misc_grad, down_rows).reshape(devices * down_rows, 1)
    lane = lax.broadcasted_iota(jnp.int32, lat_wg.shape, 1)
    small = jnp.where(lane == lat_wide, attention_gain_gradient[:, None], lat_wg)
    small = jnp.where(lane == lat_wide + 1, mlp_gain_grad[:, None], small)
    small = jnp.where(lane == lat_wide + 2, misc_grad, small).astype(BF)
    small = small.reshape(row_total, col_total, down_rows, pack_wide)
    small_reduce = Task(reduce_all_steps([small[block] for block in range(row_total)]))
    slots(steps + hops, small_reduce, head_reduce, out_reduce)
    small, head_wg, out_wg = small_reduce.result(), head_reduce.result(), out_reduce.result()
    out_wg = out_wg.T
    qu_wg = head_wg[:query_rows].reshape(query_rows, heads_here, HEAD)[:, :, : NOPE + ROPE]
    qu_wg = qu_wg.reshape(query_rows, heads_here * (NOPE + ROPE))
    kvu_wg = head_wg[query_rows:]
    misc_sum = small[:, lat_wide + 2]
    at = q_part + kv_part
    loss = (misc_sum[at] + misc_sum[at + 1]) / valid_total
    return (
        outputs,
        loss,
        input_grad,
        small[:, :q_rank],
        small[:, q_rank:lat_wide],
        qu_wg,
        kvu_wg,
        out_wg,
        gate_wg,
        up_wg,
        down_wg,
        small[:, lat_wide],
        misc_sum[:q_part],
        misc_sum[q_part : q_part + kv_part],
        small[:, lat_wide + 1],
    )


def solution(mesh):
    in_specs = (
        P(("col", "row"), None),
        P("col"),
        P(("col", "row")),
        P(("col", "row"), None),
        P(("col", "row"), None),
        P(("row", "col"), None),
        P(("row", "col"), None),
        P("col", "row"),
        P("col", "row"),
        P("row", "col"),
        P("col", "row"),
        P("col", "row"),
        P("row", "col"),
        P(("row", "col")),
        P(("row", "col")),
        P(("row", "col")),
        P(("row", "col")),
    )
    out_specs = (
        P(("col", "row"), None),
        P(),
        P(("col", "row"), None),
        P(("row", "col"), None),
        P(("row", "col"), None),
        P("col", "row"),
        P("col", "row"),
        P("row", "col"),
        P("col", "row"),
        P("col", "row"),
        P("row", "col"),
        P(("row", "col")),
        P(("row", "col")),
        P(("row", "col")),
        P(("row", "col")),
    )
    return jax.shard_map(body, mesh=mesh, in_specs=in_specs, out_specs=out_specs, check_vma=False)
```

```python
import functools
import math

import jax
import jax.numpy as jnp
from jax import lax
from jax.experimental import pallas as pl
from jax.experimental.pallas import tpu as pltpu
from jax.sharding import PartitionSpec as P

NOPE = 64
ROPE = 32
VDIM = 64
KV_RANK = 256
CONTS = 4
HEAD = 128

EPS = 1e-05
RES = 1.4 / math.sqrt(62.0)
BASE = 10000.0
SCALE = (NOPE + ROPE) ** (-0.5)
LOG2E = math.log2(math.e)
HIDE = -1e30
BF = jnp.bfloat16
F32 = jnp.float32


def dot_plain(left_op, right_op):
    return jnp.dot(left_op, right_op, preferred_element_type=F32)


def dot_dims(left_op, right_op, left_dims, right_dims):
    return lax.dot_general(
        left_op, right_op, ((left_dims, right_dims), ((), ())), preferred_element_type=F32
    )


def dot_trans_left(left_op, right_op):
    return dot_dims(left_op, right_op, (0,), (0,))


def dot_trans_right(left_op, right_op):
    return dot_dims(left_op, right_op, (1,), (1,))


def root_norm(values, gain):
    unit_rows = values * lax.rsqrt(jnp.mean(values * values, axis=-1, keepdims=True) + EPS)
    return (unit_rows * gain, unit_rows)


def norm_back(grad_rows, unit_rows, values, gain):
    factor = lax.rsqrt(jnp.mean(values * values, axis=-1, keepdims=True) + EPS)
    scaled = grad_rows * gain
    value_grad = factor * (
        scaled - unit_rows * jnp.mean(scaled * unit_rows, axis=-1, keepdims=True)
    )
    return (value_grad, jnp.sum(grad_rows * unit_rows, axis=0))


def rotary(segments):
    length = segments.shape[0]
    indices = jnp.arange(length, dtype=jnp.int32)
    labels = jnp.arange(CONTS + 1, dtype=jnp.int32)
    member = (segments[:, None] == labels[None, :]).astype(jnp.int32)
    counts = jnp.sum(member, axis=0)
    starts = jnp.cumsum(counts) - counts
    first_at = jnp.sum(member * starts[None, :], axis=1)
    places = jnp.where(segments == 0, indices, counts[0] + indices - first_at).astype(F32)
    freqs = BASE ** (-jnp.arange(ROPE // 2, dtype=F32) * 2.0 / ROPE)
    angles = places[:, None] * freqs[None, :]
    return (jnp.cos(angles), jnp.sin(angles))


def rotate(values, cosine, sine):
    half = values.shape[-1] // 2
    first_half = values[..., :half]
    second_half = values[..., half:]
    return jnp.concatenate(
        [first_half * cosine - second_half * sine, second_half * cosine + first_half * sine],
        axis=-1,
    )


def head_weights(weights_ref, query_rows):
    block = weights_ref[0]
    col_total = block.shape[0]
    query_w = block[:, :query_rows, :].reshape(col_total * query_rows, HEAD)
    latent_w = block[:, query_rows:, :].reshape(-1, HEAD)
    return (query_w, latent_w)


def head_vectors(weights_ref, query_t_ref, latent_ref, rope_ref, cos_ref, sin_ref, query_rows):
    query_w, latent_w = head_weights(weights_ref, query_rows)
    half = ROPE // 2
    proj_t = dot_plain(query_w.T, query_t_ref[...])
    first, second = proj_t[NOPE : NOPE + half], proj_t[NOPE + half : NOPE + ROPE]
    cosine, sine = cos_ref[...], sin_ref[...]
    query_t = jnp.concatenate(
        [
            proj_t[:NOPE],
            first * cosine - second * sine,
            second * cosine + first * sine,
            proj_t[NOPE + ROPE :],
        ],
        axis=0,
    ).astype(BF)
    both = dot_plain(latent_ref[...], latent_w).astype(BF)
    lane = lax.broadcasted_iota(jnp.int32, both.shape, 1)
    keys = jnp.where(lane < NOPE, both, rope_ref[...])
    return (query_w, latent_w, query_t, keys, both)


def attend_kernel(
    query_rows, tile, weights_ref, query_t_ref, latent_ref, rope_ref, cos_ref, sin_ref, bias_ref,
    mixed_ref, lse_ref, scores_ref,
):
    _, _, query_t, keys, both = head_vectors(
        weights_ref, query_t_ref, latent_ref, rope_ref, cos_ref, sin_ref, query_rows
    )
    values_t = both.T[NOPE:]
    length = keys.shape[0]
    top = None
    for begin in range(0, length, tile):
        part = dot_plain(keys[begin : begin + tile], query_t) * (SCALE * LOG2E)
        part = part + bias_ref[begin : begin + tile, :]
        scores_ref[begin : begin + tile, :] = part
        tile_top = jnp.max(part, axis=0, keepdims=True)
        top = tile_top if top is None else jnp.maximum(top, tile_top)
    total, out_t = None, None
    for begin in range(0, length, tile):
        expo = jnp.exp2(scores_ref[begin : begin + tile, :] - top)
        tile_sum = jnp.sum(expo, axis=0, keepdims=True)
        term = dot_plain(values_t[:, begin : begin + tile], expo.astype(BF))
        total = tile_sum if total is None else total + tile_sum
        out_t = term if out_t is None else out_t + term
    mixed_ref[...] = (out_t / total).astype(BF)
    lse_ref[0] = top + jnp.log2(total)


def attend_back_kernel(
    query_rows, tile, weights_ref, query_t_ref, latent_ref, latent_t_ref, rope_ref, cos_ref,
    sin_ref, bias_ref, mixed_ref, grad_ref, lse_ref, query_before_ref, latent_before_ref, *rest,
):
    weights_grad_ref, query_acc, latent_acc, both_scr = rest[-4:]
    head = pl.program_id(0)
    kv_rank = latent_ref.shape[1]
    query_w, latent_w, query_t, keys, both = head_vectors(
        weights_ref, query_t_ref, latent_ref, rope_ref, cos_ref, sin_ref, query_rows
    )

    @pl.when(head == 0)
    def _():
        query_acc[...] = query_before_ref[...]
        latent_acc[...] = latent_before_ref[...]

    keys_t = keys.T
    query = query_t.T
    grad_t = grad_ref[...]
    delta = jnp.sum(
        grad_t.astype(F32) * mixed_ref[...].astype(F32), axis=0, keepdims=True
    )
    grad_pad_t = jnp.concatenate([jnp.zeros_like(grad_t), grad_t], axis=0)
    grad_pad = grad_pad_t.T
    lse = lse_ref[0]
    length = keys.shape[0]
    query_back_t = None
    for begin in range(0, length, tile):
        rows = slice(begin, begin + tile)
        scores = dot_plain(keys[rows], query_t) * (SCALE * LOG2E)
        probs = jnp.exp2(scores + bias_ref[rows, :] - lse)
        prob_grad = dot_plain(both[rows], grad_pad_t)
        score_grad = (probs * (prob_grad - delta)).astype(BF)
        term = dot_plain(keys_t[:, rows], score_grad)
        query_back_t = term if query_back_t is None else query_back_t + term
        key_back = dot_plain(score_grad, query) * SCALE
        value_back = dot_plain(probs.astype(BF), grad_pad)
        lane = lax.broadcasted_iota(jnp.int32, key_back.shape, 1)
        latent_acc[rows, kv_rank:] += key_back
        both_scr[rows, :] = jnp.where(lane < NOPE, key_back, value_back).astype(BF)
    query_back_t = query_back_t * SCALE
    half = ROPE // 2
    first, second = query_back_t[NOPE : NOPE + half], query_back_t[NOPE + half : NOPE + ROPE]
    cosine, sine = cos_ref[...], sin_ref[...]
    query_back_t = jnp.concatenate(
        [
            query_back_t[:NOPE],
            first * cosine + second * sine,
            second * cosine - first * sine,
            jnp.zeros_like(query_back_t[NOPE + ROPE :]),
        ],
        axis=0,
    ).astype(BF)
    both_back = both_scr[...]
    query_acc[...] += dot_plain(query_w, query_back_t)
    latent_acc[:, :kv_rank] += dot_trans_right(both_back, latent_w)
    query_wg = dot_trans_right(query_t_ref[...], query_back_t)
    latent_wg = dot_plain(latent_t_ref[...], both_back)
    col_total = weights_ref.shape[1]
    weights_grad_ref[0, :, :query_rows, :] = query_wg.astype(BF).reshape(col_total, query_rows, HEAD)
    weights_grad_ref[0, :, query_rows:, :] = latent_wg.astype(BF).reshape(col_total, -1, HEAD)


def whole(shape):
    return pl.BlockSpec(shape, lambda head: (0,) * len(shape))


def attend(weights, query_t, latent, rope, cos_t, sin_t, bias_t, query_rows, block):
    _, col_total, _, pack_cols = weights.shape
    pack_rows = query_rows + latent.shape[1] // col_total
    heads = pack_cols // HEAD
    length, local = bias_t.shape
    tile = math.gcd(length, 256)
    return pl.pallas_call(
        functools.partial(attend_kernel, query_rows, tile),
        grid=(heads,),
        in_specs=[
            pl.BlockSpec((1, col_total, pack_rows, HEAD), lambda head: (block, 0, 0, head)),
            whole(query_t.shape),
            whole(latent.shape),
            whole(rope.shape),
            whole(cos_t.shape),
            whole(sin_t.shape),
            whole(bias_t.shape),
        ],
        out_specs=[
            pl.BlockSpec((VDIM, local), lambda head: (head, 0)),
            pl.BlockSpec((1, 1, local), lambda head: (head, 0, 0)),
        ],
        out_shape=[
            jax.ShapeDtypeStruct((heads * VDIM, local), BF),
            jax.ShapeDtypeStruct((heads, 1, local), F32),
        ],
        scratch_shapes=[pltpu.VMEM((length, local), F32)],
        compiler_params=pltpu.CompilerParams(
            dimension_semantics=("arbitrary",), vmem_limit_bytes=48 * 1024 * 1024
        ),
        cost_estimate=pl.CostEstimate(
            flops=heads * 1_700_000_000,
            bytes_accessed=weights[0].size * 2,
            transcendentals=heads * local * length,
        ),
        name="attend",
    )(weights, query_t, latent, rope, cos_t, sin_t, bias_t)


def attend_back(
    weights, query_t, latent, latent_t, rope, cos_t, sin_t, bias_t, mixed_t, grad_t, lse,
    query_before, latent_before, weights_before, query_rows, block,
):
    row_total, col_total, _, pack_cols = weights.shape
    more = [] if weights_before is None else [weights_before]
    pack_rows = query_rows + latent.shape[1] // col_total
    heads = pack_cols // HEAD
    length, local = bias_t.shape
    tile = math.gcd(length, 256)
    return pl.pallas_call(
        functools.partial(attend_back_kernel, query_rows, tile),
        grid=(heads,),
        in_specs=[
            pl.BlockSpec((1, col_total, pack_rows, HEAD), lambda head: (block, 0, 0, head)),
            whole(query_t.shape),
            whole(latent.shape),
            whole(latent_t.shape),
            whole(rope.shape),
            whole(cos_t.shape),
            whole(sin_t.shape),
            whole(bias_t.shape),
            pl.BlockSpec((VDIM, local), lambda head: (head, 0)),
            pl.BlockSpec((VDIM, local), lambda head: (block * heads + head, 0)),
            pl.BlockSpec((1, 1, local), lambda head: (head, 0, 0)),
            whole(query_before.shape),
            whole(latent_before.shape),
        ]
        + [pl.BlockSpec(memory_space=pl.ANY)] * len(more),
        out_specs=[
            pl.BlockSpec((1, col_total, pack_rows, HEAD), lambda head: (block, 0, 0, head)),
            whole(query_before.shape),
            whole(latent_before.shape),
        ],
        out_shape=[
            jax.ShapeDtypeStruct((row_total, col_total, pack_rows, pack_cols), BF),
            jax.ShapeDtypeStruct(query_before.shape, F32),
            jax.ShapeDtypeStruct(latent_before.shape, F32),
        ],
        input_output_aliases={13: 0} if more else {},
        scratch_shapes=[pltpu.VMEM((length, HEAD), BF)],
        compiler_params=pltpu.CompilerParams(
            dimension_semantics=("arbitrary",), vmem_limit_bytes=48 * 1024 * 1024
        ),
        cost_estimate=pl.CostEstimate(
            flops=heads * 4_200_000_000,
            bytes_accessed=weights[0].size * 4,
            transcendentals=heads * local * length,
        ),
        name="attend_back",
    )(weights, query_t, latent, latent_t, rope, cos_t, sin_t, bias_t, mixed_t, grad_t, lse,
      query_before, latent_before, *more)


def weight_grad_kernel(chunks, *refs):
    lefts, rights, out_ref = refs[:chunks], refs[chunks : 2 * chunks], refs[2 * chunks]
    total = None
    for left_ref, right_ref in zip(lefts, rights):
        term = dot_plain(left_ref[...].T, right_ref[...])
        total = term if total is None else total + term
    out_ref[...] = total.astype(out_ref.dtype)


def weight_grad(lefts, rights, name):
    chunks = len(lefts)
    rows, width = lefts[0].shape
    units = rights[0].shape[1]
    tile = math.gcd(width, 256)
    return pl.pallas_call(
        functools.partial(weight_grad_kernel, chunks),
        grid=(width // tile,),
        in_specs=[pl.BlockSpec((rows, tile), lambda step: (0, step))] * chunks
        + [pl.BlockSpec((rows, units), lambda step: (0, 0))] * chunks,
        out_specs=pl.BlockSpec((tile, units), lambda step: (step, 0)),
        out_shape=jax.ShapeDtypeStruct((width, units), BF),
        compiler_params=pltpu.CompilerParams(
            dimension_semantics=("arbitrary",), vmem_limit_bytes=48 * 1024 * 1024
        ),
        cost_estimate=pl.CostEstimate(
            flops=2 * chunks * rows * width * units,
            bytes_accessed=2 * (chunks * rows + units) * width,
            transcendentals=0,
        ),
        name=name,
    )(*lefts, *rights)


MESH = pl.DeviceIdType.MESH


def out_grad_kernel(tokens_ref, mixed_ref, out_ref):
    out_ref[0] = dot_trans_right(tokens_ref[...].T, mixed_ref[...]).astype(BF)


def out_weight_grad(tokens, mixed):
    rows, width = tokens.shape
    row_total, units, _ = mixed.shape
    tile = math.gcd(width, 512)
    return pl.pallas_call(
        out_grad_kernel,
        grid=(row_total, width // tile),
        in_specs=[
            pl.BlockSpec((rows, tile), lambda block, step: (0, step)),
            pl.BlockSpec((None, units, rows), lambda block, step: (block, 0, 0)),
        ],
        out_specs=pl.BlockSpec((1, tile, units), lambda block, step: (block, step, 0)),
        out_shape=jax.ShapeDtypeStruct((row_total, width, units), BF),
        cost_estimate=pl.CostEstimate(
            flops=2 * rows * width * units * row_total,
            bytes_accessed=2 * row_total * width * units,
            transcendentals=0,
        ),
        name="out_wg",
    )(tokens, mixed)


def flip(index, bit):
    return index + bit - 2 * bit * lax.rem(index // bit, 2)


def chip_bits(col_total):
    bits, bit = [], 2
    while bit < col_total:
        bits.append(bit)
        bit *= 2
    return bits


def turn_bit(bits, row, step, row_total):
    turn = lax.rem(step + (row * len(bits)) // row_total, len(bits))
    return sum(jnp.where(turn == at, bit, 0) for at, bit in enumerate(bits))


def greet(row_total, row_rank, col_rank, bits):
    barrier = pltpu.get_barrier_semaphore()
    for bit in [1] + bits:
        pl.semaphore_signal(
            barrier, inc=1, device_id=(row_rank, flip(col_rank, bit)), device_id_type=MESH
        )

    @pl.when(row_rank > 0)
    def _():
        pl.semaphore_signal(barrier, inc=1, device_id=(row_rank - 1, col_rank), device_id_type=MESH)

    @pl.when(row_rank < row_total - 1)
    def _():
        pl.semaphore_signal(barrier, inc=1, device_id=(row_rank + 1, col_rank), device_id_type=MESH)

    beside = lax.min(row_rank, 1) + lax.min(row_total - 1 - row_rank, 1)
    pl.semaphore_wait(barrier, 1 + len(bits) + beside)


def gather_kernel(
    row_total, col_total, own_ref, out_ref, own_sem, line_send, line_recv, chip_send, chip_recv,
    core_send, core_recv,
):
    row_rank, col_rank = lax.axis_index("row"), lax.axis_index("col")
    bits = chip_bits(col_total)
    masks = 2 ** len(bits)
    own = pltpu.make_async_copy(own_ref, out_ref.at[row_rank, col_rank], own_sem)
    own.start()
    greet(row_total, row_rank, col_rank, bits)
    own.wait()

    def block_col(row, mask):
        index = col_rank
        for step in range(len(bits)):
            if mask >> step & 1:
                index = flip(index, turn_bit(bits, row, step, row_total))
        return index

    def line_copy(way, row):
        ref = out_ref.at[row, col_rank]
        return pltpu.make_async_remote_copy(
            src_ref=ref, dst_ref=ref, send_sem=line_send.at[way, row], recv_sem=line_recv.at[row],
            device_id=(row_rank + 1 - 2 * way, col_rank), device_id_type=MESH,
        )

    def chip_copy(row, mask, step):
        ref = out_ref.at[row, block_col(row, mask)]
        to = mask + 2**step
        return pltpu.make_async_remote_copy(
            src_ref=ref, dst_ref=ref, send_sem=chip_send.at[row, to], recv_sem=chip_recv.at[row, to],
            device_id=(row_rank, flip(col_rank, turn_bit(bits, row, step, row_total))),
            device_id_type=MESH,
        )

    def core_copy(row, mask):
        ref = out_ref.at[row, block_col(row, mask)]
        return pltpu.make_async_remote_copy(
            src_ref=ref, dst_ref=ref, send_sem=core_send.at[row, mask],
            recv_sem=core_recv.at[row, mask], device_id=(row_rank, flip(col_rank, 1)),
            device_id_type=MESH,
        )

    def by_distance(act):
        for away in range(row_total):
            for side in (0,) if away == 0 else (-1, 1):
                row = row_rank + side * away

                @pl.when((row >= 0) & (row < row_total))
                def _():
                    act(row, away, side)

    def arrive(row, away, side):
        if away > 0:
            line_copy(0, row).wait_recv()
        if side <= 0:

            @pl.when(row_rank < row_total - 1)
            def _():
                line_copy(0, row).start()

        if side >= 0:

            @pl.when(row_rank > 0)
            def _():
                line_copy(1, row).start()

        for step in range(len(bits)):
            chip_copy(row, 0, step).start()
        core_copy(row, 0).start()

    by_distance(arrive)
    for mask in range(1, masks):
        top = mask.bit_length() - 1

        def forward(row, away, side):
            chip_copy(row, mask - 2**top, top).wait_recv()
            for step in range(top + 1, len(bits)):
                chip_copy(row, mask, step).start()
            core_copy(row, mask).start()

        by_distance(forward)
    for row in range(row_total):
        for mask in range(masks):
            core_copy(row, mask).wait()
            if mask > 0:
                top = mask.bit_length() - 1
                chip_copy(row, mask - 2**top, top).wait_send()

        @pl.when((row <= row_rank) & (row_rank < row_total - 1))
        def _():
            line_copy(0, row).wait_send()

        @pl.when((row >= row_rank) & (row_rank > 0))
        def _():
            line_copy(1, row).wait_send()


def gather_all(values, collective_id, name):
    row_total, col_total = lax.axis_size("row"), lax.axis_size("col")
    masks = 2 ** len(chip_bits(col_total))
    return pl.pallas_call(
        functools.partial(gather_kernel, row_total, col_total),
        in_specs=[pl.BlockSpec(memory_space=pl.ANY)],
        out_specs=pl.BlockSpec(memory_space=pl.ANY),
        out_shape=jax.ShapeDtypeStruct((row_total, col_total) + values.shape, values.dtype),
        scratch_shapes=[
            pltpu.SemaphoreType.DMA,
            pltpu.SemaphoreType.DMA((2, row_total)),
            pltpu.SemaphoreType.DMA((row_total,)),
            pltpu.SemaphoreType.DMA((row_total, masks)),
            pltpu.SemaphoreType.DMA((row_total, masks)),
            pltpu.SemaphoreType.DMA((row_total, masks)),
            pltpu.SemaphoreType.DMA((row_total, masks)),
        ],
        compiler_params=pltpu.CompilerParams(
            collective_id=collective_id, has_side_effects=True
        ),
        name=name,
    )(values)


def add_into(total_ref, other_ref):
    rows = total_ref.shape[0]
    tile = math.gcd(rows, 32)

    def one(step, carry):
        here = pl.ds(pl.multiple_of(step * tile, tile), tile)
        total = total_ref[here, :].astype(F32) + other_ref[here, :].astype(F32)
        total_ref[here, :] = total.astype(total_ref.dtype)
        return carry

    lax.fori_loop(0, rows // tile, one, 0)


class LineReduce:
    def __init__(self, row_total, row_rank, col_rank, block, landed, send, recv):
        self.row_total, self.row_rank, self.col_rank = row_total, row_rank, col_rank
        self.block, self.landed, self.send, self.recv = block, landed, send, recv

    def copy(self, way, row):
        return pltpu.make_async_remote_copy(
            src_ref=self.block(row), dst_ref=self.landed.at[way, row],
            send_sem=self.send.at[way, row], recv_sem=self.recv.at[way, row],
            device_id=(self.row_rank + 1 - 2 * way, self.col_rank), device_id_type=MESH,
        )

    def run(self):
        last = self.row_total - 1
        for step in range(last):
            for way, row in ((0, last - step), (1, step)):
                sends = self.row_rank < row if way == 0 else self.row_rank > row
                gets = self.row_rank > 0 if way == 0 else self.row_rank < last

                @pl.when(sends)
                def _():
                    @pl.when(gets)
                    def _():
                        self.copy(way, row).wait_recv()
                        add_into(self.block(row), self.landed.at[way, row])

                    self.copy(way, row).start()

        for way, gets in ((0, self.row_rank > 0), (1, self.row_rank < last)):

            @pl.when(gets)
            def _():
                self.copy(way, self.row_rank).wait_recv()
                add_into(self.block(self.row_rank), self.landed.at[way, self.row_rank])

    def finish(self, out_ref):
        rows = out_ref.shape[0]
        tile = math.gcd(rows, 32)
        own = self.block(self.row_rank)

        def one(step, carry):
            here = pl.ds(pl.multiple_of(step * tile, tile), tile)
            out_ref[here, :] = own[here, :].astype(out_ref.dtype)
            return carry

        lax.fori_loop(0, rows // tile, one, 0)
        for row in range(self.row_total):
            for way, sends in ((0, self.row_rank < row), (1, self.row_rank > row)):

                @pl.when(sends)
                def _():
                    self.copy(way, row).wait_send()


def reduce_kernel(
    row_total, col_total, part_ref, out_ref, sums, chip_buf, line_buf, core_send, core_recv,
    chip_send, chip_recv, line_send, line_recv,
):
    row_rank, col_rank = lax.axis_index("row"), lax.axis_index("col")
    bits = chip_bits(col_total)
    count = len(bits)
    masks = 2**count
    core = lax.rem(col_rank, 2)
    greet(row_total, row_rank, col_rank, bits)

    def order(row):
        turn = (row * count) // row_total
        return bits[turn:] + bits[:turn]

    def chip_at(row, mask):
        index = col_rank // 2
        for step, bit in enumerate(order(row)):
            if mask >> step & 1:
                index = flip(index, bit // 2)
        return index

    def core_copy(row, mask):
        return pltpu.make_async_remote_copy(
            src_ref=part_ref.at[row, chip_at(row, mask), 1 - core], dst_ref=sums.at[row, mask],
            send_sem=core_send.at[row, mask], recv_sem=core_recv.at[row, mask],
            device_id=(row_rank, flip(col_rank, 1)), device_id_type=MESH,
        )

    def chip_copy(row, mask, step):
        return pltpu.make_async_remote_copy(
            src_ref=sums.at[row, mask], dst_ref=chip_buf.at[row, mask],
            send_sem=chip_send.at[row, mask], recv_sem=chip_recv.at[row, mask],
            device_id=(row_rank, flip(col_rank, order(row)[step])), device_id_type=MESH,
        )

    for mask in range(masks - 1, -1, -1):
        for row in range(row_total):
            core_copy(row, mask).start()
    for mask in range(masks - 1, -1, -1):
        for row in range(row_total):
            core_copy(row, mask).wait_recv()
            add_into(sums.at[row, mask], part_ref.at[row, chip_at(row, mask), core])
            if mask >= masks // 2:
                chip_copy(row, mask, count - 1).start()
    for step in range(count - 1, -1, -1):
        half = 2**step
        for mask in range(half - 1, -1, -1):
            for row in range(row_total):
                chip_copy(row, mask + half, step).wait_recv()
                add_into(sums.at[row, mask], chip_buf.at[row, mask + half])
                if step > 0 and mask >= half // 2:
                    chip_copy(row, mask, step - 1).start()
    line = LineReduce(
        row_total, row_rank, col_rank, lambda row: sums.at[row, 0], line_buf, line_send, line_recv
    )
    line.run()
    line.finish(out_ref)
    for row in range(row_total):
        for mask in range(masks):
            core_copy(row, mask).wait_send()
            if mask > 0:
                chip_copy(row, mask, mask.bit_length() - 1).wait_send()


def reduce_all(parts, collective_id, name):
    row_total, col_total, own_rows, lanes = parts.shape
    rows = -(-own_rows // 16) * 16
    if rows != own_rows:
        parts = jnp.pad(parts, ((0, 0), (0, 0), (0, rows - own_rows), (0, 0)))
    parts = parts.reshape(row_total, col_total // 2, 2, rows, lanes)
    masks = col_total // 2
    sem = pltpu.SemaphoreType.DMA
    vmem = pl.BlockSpec(memory_space=pltpu.VMEM)
    return pl.pallas_call(
        functools.partial(reduce_kernel, row_total, col_total),
        in_specs=[vmem],
        out_specs=vmem,
        out_shape=jax.ShapeDtypeStruct((rows, lanes), F32),
        scratch_shapes=[
            pltpu.VMEM((row_total, masks, rows, lanes), BF),
            pltpu.VMEM((row_total, masks, rows, lanes), BF),
            pltpu.VMEM((2, row_total, rows, lanes), BF),
            sem((row_total, masks)),
            sem((row_total, masks)),
            sem((row_total, masks)),
            sem((row_total, masks)),
            sem((2, row_total)),
            sem((2, row_total)),
        ],
        compiler_params=pltpu.CompilerParams(
            collective_id=collective_id, has_side_effects=True, vmem_limit_bytes=48 * 1024 * 1024
        ),
        name=name,
    )(parts)[:own_rows]


together = lax.optimization_barrier


class Task:
    def __init__(self, steps):
        self.steps, self.state, self.value, self.over = steps, None, None, False

    def advance(self):
        if not self.over:
            try:
                return self.steps.send(self.state)
            except StopIteration as stop:
                self.value, self.over = stop.value, True
        return ()

    def advance_into(self):
        self.state = self.advance()
        return not self.over

    def result(self):
        self.advance()
        assert self.over
        return self.value


def slot(*tasks):
    states = together(tuple(task.advance() for task in tasks))
    for task, state in zip(tasks, states):
        task.state = state


def slots(count, *tasks):
    for _ in range(count):
        slot(*tasks)


def gather_steps(values):
    total = lax.axis_size("row")
    up, down = [None], [None]
    ways = (values, values)
    for step in range(1, total):
        ways = yield (
            lax.ppermute(ways[0], "row", [(i, i + 1) for i in range(step - 1, total - 1)]),
            lax.ppermute(ways[1], "row", [(i, i - 1) for i in range(1, total - step + 1)]),
        )
        up.append(ways[0])
        down.append(ways[1])
    return jnp.concatenate([values] + [up[step] + down[total - step] for step in range(1, total)])


def add_parts(left_op, right_op):
    return (left_op.astype(F32) + right_op.astype(F32)).astype(BF)


def reduce_steps(parts):
    total = lax.axis_size("row")
    ways = None
    for step in range(total - 1):
        sends = (parts[step + 1], parts[total - 1 - step])
        if step > 0:
            sends = (add_parts(sends[0], ways[0]), add_parts(sends[1], ways[1]))
        ways = yield (
            lax.ppermute(sends[0], "row", [(i, i + 1) for i in range(step + 1)]),
            lax.ppermute(sends[1], "row", [(i, i - 1) for i in range(total - 1 - step, total)]),
        )
    return parts[0].astype(F32) + ways[0].astype(F32) + ways[1].astype(F32)


def product_steps(product):
    total = lax.axis_size("row")
    rows = product.shape[0] // total
    parts = [product[at * rows : (at + 1) * rows] for at in range(total)]
    return (yield from reduce_steps(parts))


def pad_to(values, width):
    return jnp.pad(values, ((0, 0), (0, width - values.shape[1])))


def body(
    inputs,
    segments,
    valid_mask,
    teacher,
    cotangent,
    query_down,
    latent_down,
    query_up,
    latent_up,
    output_weight,
    gate_weight,
    up_weight,
    down_weight,
    attn_gain,
    query_gain,
    latent_gain,
    mlp_gain,
):
    both_axes = ("row", "col")
    row_total = lax.axis_size("row")
    col_total = lax.axis_size("col")
    devices = row_total * col_total
    row_rank = lax.axis_index("row")
    local_rows, width = inputs.shape
    length = segments.shape[0]
    q_rank = query_down.shape[1]
    kv_wide = latent_down.shape[1]
    lat_wide = q_rank + kv_wide
    down_rows = query_down.shape[0]
    q_part, kv_part = query_gain.shape[0], latent_gain.shape[0]
    heads_here = output_weight.shape[0] // VDIM
    query_rows = query_up.shape[0]
    offset = row_rank * local_rows

    count = jnp.sum(valid_mask)
    count_parts = jnp.stack([count // 256, count % 256]).astype(F32)
    misc = jnp.concatenate(
        [query_gain.astype(F32), latent_gain.astype(F32), count_parts]
    )
    misc = jnp.pad(misc, (0, down_rows - misc.shape[0])).astype(BF)
    down_pack = jnp.concatenate(
        [query_down, latent_down, attn_gain[:, None], mlp_gain[:, None], misc[:, None]], axis=1
    )
    pack_wide = -(-(lat_wide + 3) // 128) * 128
    down_pack = pad_to(down_pack, pack_wide)

    query_pack = jnp.pad(
        query_up.reshape(query_rows, heads_here, NOPE + ROPE),
        ((0, 0), (0, 0), (0, HEAD - NOPE - ROPE)),
    ).reshape(query_rows, heads_here * HEAD)
    up_pack = jnp.concatenate([query_pack, latent_up], axis=0)
    pack_rows = up_pack.shape[0]
    if up_pack.shape[1] >= pack_wide:
        head_w = gather_all(
            jnp.concatenate([up_pack, pad_to(down_pack, up_pack.shape[1])]), 1, "gather_pack"
        )
        down_all = head_w[:, :, pack_rows:, :pack_wide]
    else:
        head_w = gather_all(up_pack, 1, "gather_up")
        down_all = gather_all(down_pack, 2, "gather_down")
    down_all = down_all.reshape(devices * down_rows, pack_wide)
    down_all, out_here = together((down_all, output_weight.T))
    out_all = lax.all_gather(out_here, both_axes, axis=0, tiled=True).reshape(
        row_total, width, heads_here * VDIM
    )
    attn_g = down_all[:, lat_wide].astype(F32)
    mlp_g = down_all[:, lat_wide + 1].astype(F32)
    misc_all = down_all[:, lat_wide + 2].astype(F32).reshape(devices, down_rows)
    query_g = misc_all[:, :q_part].reshape(-1)
    latent_g = misc_all[:, q_part : q_part + kv_part].reshape(-1)
    counts = jnp.sum(misc_all[:, q_part + kv_part : q_part + kv_part + 2], axis=0)
    valid_total = counts[0] * 256.0 + counts[1]

    cosine, sine = rotary(segments)
    cos_here = lax.dynamic_slice_in_dim(cosine, offset, local_rows, 0)
    sin_here = lax.dynamic_slice_in_dim(sine, offset, local_rows, 0)
    tokens_f = inputs.astype(F32)
    normed, normed_unit = root_norm(tokens_f, attn_g)
    normed_b = normed.astype(BF)
    lat = dot_plain(normed_b, down_all)
    query_lat, kv_lat = lat[:, :q_rank], lat[:, q_rank:lat_wide]
    query_norm, query_unit = root_norm(query_lat, query_g)
    kv_norm, kv_unit = root_norm(kv_lat[:, :KV_RANK], latent_g)
    key_rope = rotate(kv_lat[:, KV_RANK:], cos_here, sin_here)
    query_nb = query_norm.astype(BF)
    latent_pack = jnp.concatenate(
        [
            kv_norm,
            jnp.zeros((local_rows, NOPE), F32),
            key_rope,
            jnp.zeros((local_rows, HEAD - NOPE - ROPE), F32),
        ],
        axis=1,
    ).astype(BF)
    latent_give = Task(gather_steps(latent_pack))
    while latent_give.advance_into():
        pass
    latent_all = together(latent_give.value)
    kv_all = latent_all[:, :KV_RANK]
    rope_all = latent_all[:, KV_RANK:]

    query_at = offset + jnp.arange(local_rows, dtype=jnp.int32)
    query_seg = lax.dynamic_slice_in_dim(segments, offset, local_rows, 0)
    begins = [
        lax.rem(row_rank + row_total - step, row_total) * local_rows for step in range(row_total)
    ]
    key_at = jnp.concatenate([begin + jnp.arange(local_rows, dtype=jnp.int32) for begin in begins])
    key_seg = jnp.concatenate(
        [lax.dynamic_slice_in_dim(segments, begin, local_rows, 0) for begin in begins]
    )
    allowed_t = (key_at[:, None] <= query_at[None, :]) & (
        (key_seg[:, None] == 0) | (key_seg[:, None] == query_seg[None, :])
    )
    bias_t = jnp.where(allowed_t, 0.0, HIDE).astype(F32)
    query_t = query_nb.T
    cos_t, sin_t = cos_here.T, sin_here.T
    cut = row_total // 2
    mixed = [
        attend(head_w, query_t, kv_all, rope_all, cos_t, sin_t, bias_t, query_rows, block)
        for block in range(cut)
    ]
    mixed, out_all, query_t, gate_here, up_here, down_here = together(
        (mixed, out_all, query_t, gate_weight, up_weight, down_weight.T)
    )
    gate_full, up_full, down_t = (
        lax.all_gather(gate_here, "col", axis=0, tiled=True),
        lax.all_gather(up_here, "col", axis=0, tiled=True),
        lax.all_gather(down_here, "col", axis=0, tiled=True),
    )
    mixed += [
        attend(head_w, query_t, kv_all, rope_all, cos_t, sin_t, bias_t, query_rows, block)
        for block in range(cut, row_total)
    ]
    attn_sum = None
    for block in range(row_total):
        term = dot_dims(mixed[block][0], out_all[block], (0,), (1,))
        attn_sum = term if attn_sum is None else attn_sum + term

    residual = tokens_f + RES * attn_sum
    mlp_in, mlp_unit = root_norm(residual, mlp_g)
    mlp_b = mlp_in.astype(BF)
    weight_v = valid_mask.astype(F32)[:, None]
    out_scale = local_rows * devices / valid_total
    rows = local_rows // 2
    parts = [slice(0, rows), slice(rows, 2 * rows)]

    def forward_steps(tokens):
        gate_act = yield dot_plain(tokens, gate_full).astype(BF)
        gate_f = gate_act.astype(F32)
        up_act = dot_plain(tokens, up_full)
        hidden = yield (gate_f * jax.nn.sigmoid(gate_f) * up_act).astype(BF)
        up_act = up_act.astype(BF)
        product = yield dot_trans_right(hidden, down_t).astype(BF)
        return (gate_act, up_act, hidden, product)

    def judge(part, down_sum):
        out_rows = residual[part] + RES * down_sum
        error_val = out_rows - teacher[part].astype(F32)
        squared = 0.5 * jnp.sum(weight_v[part] * error_val * error_val)
        grad_rows = cotangent[part].astype(F32) + out_scale * weight_v[part] * error_val
        return (out_rows.astype(BF), squared, grad_rows, (RES * grad_rows).astype(BF))

    def backward_steps(branch, gate_act, up_act):
        gate_act, up_act = gate_act.astype(F32), up_act.astype(F32)
        gate_sig = jax.nn.sigmoid(gate_act)
        hidden_grad = dot_plain(branch, down_t)
        gate_grad, up_grad = yield (
            (hidden_grad * up_act * gate_sig * (1.0 + gate_act * (1.0 - gate_sig))).astype(BF),
            (hidden_grad * gate_act * gate_sig).astype(BF),
        )
        product = yield dot_trans_right(gate_grad, gate_full)
        product = yield (product + dot_trans_right(up_grad, up_full)).astype(BF)
        return (gate_grad, up_grad, product)

    def weight_steps(work):
        got = []
        for lefts, rights, name in work:
            got.append((yield weight_grad(lefts, rights, name)))
        return got

    hops = row_total - 1
    mlp_b = mlp_in.astype(BF)
    give_0, give_1 = [Task(gather_steps(mlp_b[part])) for part in parts]
    slots(hops, give_0)
    tokens_0, gate_full, up_full = together((give_0.result(), gate_full, up_full))
    fore_0 = Task(forward_steps(tokens_0))
    slots(hops, give_1, fore_0)
    tokens_1 = give_1.result()
    fore_0 = fore_0.result()
    take_0 = Task(product_steps(fore_0[3]))
    fore_1 = Task(forward_steps(tokens_1))
    slots(hops, take_0, fore_1)
    judged_0 = judge(parts[0], take_0.result())
    fore_1 = fore_1.result()
    take_1 = Task(product_steps(fore_1[3]))
    give_0 = Task(gather_steps(judged_0[3]))
    slot(give_0)
    slots(hops - 1, give_0, take_1)
    branch_0 = give_0.result()
    back_0 = Task(backward_steps(branch_0, fore_0[0], fore_0[1]))
    slot(take_1, back_0)
    judged_1 = judge(parts[1], take_1.result())
    give_1 = Task(gather_steps(judged_1[3]))
    slots(hops - 1, give_1, back_0)
    back_0 = back_0.result()
    take_0 = Task(product_steps(back_0[2]))
    slot(give_1, take_0)
    branch_1 = give_1.result()
    back_1 = Task(backward_steps(branch_1, fore_1[0], fore_1[1]))
    down_work = Task(weight_steps([([branch_0, branch_1], [fore_0[2], fore_1[2]], "down_wg")]))
    slot(take_0, down_work)
    slots(hops - 2, take_0, back_1)
    grad_0 = take_0.result()
    (down_wg,) = down_work.result()
    while back_1.advance_into():
        pass
    back_1 = back_1.value
    take_1 = Task(product_steps(back_1[2]))
    work = Task(
        weight_steps(
            [
                ([tokens_0, tokens_1], [back_0[0], back_1[0]], "gate_wg"),
                ([tokens_0, tokens_1], [back_0[1], back_1[1]], "up_wg"),
            ]
        )
    )
    slots(max(hops, 2), take_1, work)
    grad_1 = take_1.result()
    gate_wg, up_wg = work.result()
    outputs = jnp.concatenate([judged_0[0], judged_1[0]])
    squared = judged_0[1] + judged_1[1]
    out_grad = jnp.concatenate([judged_0[2], judged_1[2]])
    mlp_in_grad = jnp.concatenate([grad_0, grad_1])
    gate_wg, up_wg, down_wg = (
        lax.psum_scatter(gate_wg, "col", scatter_dimension=0, tiled=True),
        lax.psum_scatter(up_wg, "col", scatter_dimension=0, tiled=True),
        lax.psum_scatter(down_wg, "col", scatter_dimension=0, tiled=True),
    )
    residual_part, mlp_gain_grad = norm_back(mlp_in_grad, mlp_unit, residual, mlp_g)
    residual_grad = out_grad + residual_part

    attn_grad_in = (RES * residual_grad).astype(BF)
    grad_t = dot_dims(out_all, attn_grad_in, (1,), (1,)).astype(BF)
    latent_t = kv_all.T
    out_wg = out_weight_grad(attn_grad_in, jnp.stack([mixed_t for mixed_t, _ in mixed]))
    grad_t, out_wg = together((grad_t.reshape(-1, local_rows), out_wg))
    out_wg = lax.psum_scatter(
        out_wg.reshape(row_total * width, heads_here * VDIM),
        both_axes, scatter_dimension=0, tiled=True,
    )
    query_back_t = jnp.zeros(query_t.shape, F32)
    latent_back = jnp.zeros(latent_all.shape, F32)
    head_wg = None
    for block, (mixed_t, lse) in enumerate(mixed):
        if block == cut:
            query_back_t, gate_wg, up_wg, down_wg = together((query_back_t, gate_wg, up_wg, down_wg))
        head_wg, query_back_t, latent_back = attend_back(
            head_w, query_t, kv_all, latent_t, rope_all, cos_t, sin_t, bias_t, mixed_t,
            grad_t, lse, query_back_t, latent_back, head_wg, query_rows, block,
        )
    head_wg, out_wg = together((head_wg, out_wg))
    out_wg = out_wg.astype(F32).T
    head_wg = lax.psum_scatter(
        head_wg.reshape(devices * pack_rows, heads_here * HEAD),
        both_axes, scatter_dimension=0, tiled=True,
    ).astype(F32)
    latent_rows = latent_back.astype(BF)
    latent_reduce = Task(
        reduce_steps(
            [latent_rows[at * local_rows : (at + 1) * local_rows] for at in range(row_total)]
        )
    )
    while latent_reduce.advance_into():
        pass
    latent_back = latent_reduce.value
    kv_norm_grad = latent_back[:, :KV_RANK]
    rope_grad = latent_back[:, KV_RANK + NOPE : KV_RANK + NOPE + ROPE]
    query_norm_grad = query_back_t.T
    query_lat_grad, query_gain_grad = norm_back(query_norm_grad, query_unit, query_lat, query_g)
    kv_lat_part, latent_gain_grad = norm_back(kv_norm_grad, kv_unit, kv_lat[:, :KV_RANK], latent_g)
    lat_grad = jnp.concatenate(
        [
            query_lat_grad,
            kv_lat_part,
            rotate(rope_grad, cos_here, -sin_here),
            jnp.zeros((local_rows, pack_wide - lat_wide), F32),
        ],
        axis=-1,
    ).astype(BF)
    lat_wg = dot_trans_left(normed_b, lat_grad)
    normed_grad = dot_trans_right(lat_grad, down_all)
    input_part, attention_gain_gradient = norm_back(normed_grad, normed_unit, tokens_f, attn_g)
    input_grad = residual_grad + input_part

    loss_high = squared.astype(BF).astype(F32)
    loss_low = squared - loss_high
    misc_grad = jnp.concatenate(
        [
            query_gain_grad.reshape(devices, q_part),
            latent_gain_grad.reshape(devices, kv_part),
            jnp.broadcast_to(loss_high, (devices, 1)),
            jnp.broadcast_to(loss_low, (devices, 1)),
        ],
        axis=1,
    )
    misc_grad = pad_to(misc_grad, down_rows).reshape(devices * down_rows, 1)
    lane = lax.broadcasted_iota(jnp.int32, lat_wg.shape, 1)
    small = jnp.where(lane == lat_wide, attention_gain_gradient[:, None], lat_wg)
    small = jnp.where(lane == lat_wide + 1, mlp_gain_grad[:, None], small)
    small = jnp.where(lane == lat_wide + 2, misc_grad, small).astype(BF)
    small = small.reshape(row_total, col_total, down_rows, pack_wide)
    small = reduce_all(small, 3, "reduce_down")
    qu_wg = head_wg[:query_rows].reshape(query_rows, heads_here, HEAD)[:, :, : NOPE + ROPE]
    qu_wg = qu_wg.reshape(query_rows, heads_here * (NOPE + ROPE))
    kvu_wg = head_wg[query_rows:]
    misc_sum = small[:, lat_wide + 2]
    at = q_part + kv_part
    loss = (misc_sum[at] + misc_sum[at + 1]) / valid_total
    return (
        outputs,
        loss,
        input_grad,
        small[:, :q_rank],
        small[:, q_rank:lat_wide],
        qu_wg,
        kvu_wg,
        out_wg,
        gate_wg.astype(F32),
        up_wg.astype(F32),
        down_wg.astype(F32).T,
        small[:, lat_wide],
        misc_sum[:q_part],
        misc_sum[q_part : q_part + kv_part],
        small[:, lat_wide + 1],
    )


def solution(mesh):
    in_specs = (
        P(("col", "row"), None),
        P("col"),
        P(("col", "row")),
        P(("col", "row"), None),
        P(("col", "row"), None),
        P(("row", "col"), None),
        P(("row", "col"), None),
        P("col", "row"),
        P("col", "row"),
        P("row", "col"),
        P("col", "row"),
        P("col", "row"),
        P("row", "col"),
        P(("row", "col")),
        P(("row", "col")),
        P(("row", "col")),
        P(("row", "col")),
    )
    out_specs = (
        P(("col", "row"), None),
        P(),
        P(("col", "row"), None),
        P(("row", "col"), None),
        P(("row", "col"), None),
        P("col", "row"),
        P("col", "row"),
        P("row", "col"),
        P("col", "row"),
        P("col", "row"),
        P("row", "col"),
        P(("row", "col")),
        P(("row", "col")),
        P(("row", "col")),
        P(("row", "col")),
    )
    return jax.shard_map(body, mesh=mesh, in_specs=in_specs, out_specs=out_specs, check_vma=False)
```

```python
import functools
import math

import jax
import jax.numpy as jnp
from jax import lax
from jax.experimental import pallas as pl
from jax.experimental.pallas import tpu as pltpu
from jax.sharding import PartitionSpec as P

NOPE = 64
ROPE = 32
VDIM = 64
KV_RANK = 256
CONTS = 4
CONT_LEN = 256
HEAD = 128

EPS = 1e-05
RES = 1.4 / math.sqrt(62.0)
BASE = 10000.0
SCALE = (NOPE + ROPE) ** (-0.5)
LOG2E = math.log2(math.e)
HIDE = -1e30
BF = jnp.bfloat16
F32 = jnp.float32


def dot_plain(left_op, right_op):
    return jnp.dot(left_op, right_op, preferred_element_type=F32)


def dot_dims(left_op, right_op, left_dims, right_dims):
    return lax.dot_general(
        left_op, right_op, ((left_dims, right_dims), ((), ())), preferred_element_type=F32
    )


def dot_trans_left(left_op, right_op):
    return dot_dims(left_op, right_op, (0,), (0,))


def dot_trans_right(left_op, right_op):
    return dot_dims(left_op, right_op, (1,), (1,))


def root_norm(values, gain):
    unit_rows = values * lax.rsqrt(jnp.mean(values * values, axis=-1, keepdims=True) + EPS)
    return (unit_rows * gain, unit_rows)


def norm_back(grad_rows, unit_rows, values, gain):
    factor = lax.rsqrt(jnp.mean(values * values, axis=-1, keepdims=True) + EPS)
    scaled = grad_rows * gain
    value_grad = factor * (
        scaled - unit_rows * jnp.mean(scaled * unit_rows, axis=-1, keepdims=True)
    )
    return (value_grad, jnp.sum(grad_rows * unit_rows, axis=0))


def rotary(segments):
    length = segments.shape[0]
    indices = jnp.arange(length, dtype=jnp.int32)
    labels = jnp.arange(CONTS + 1, dtype=jnp.int32)
    member = (segments[:, None] == labels[None, :]).astype(jnp.int32)
    counts = jnp.sum(member, axis=0)
    starts = jnp.cumsum(counts) - counts
    first_at = jnp.sum(member * starts[None, :], axis=1)
    places = jnp.where(segments == 0, indices, counts[0] + indices - first_at).astype(F32)
    freqs = BASE ** (-jnp.arange(ROPE // 2, dtype=F32) * 2.0 / ROPE)
    angles = places[:, None] * freqs[None, :]
    return (jnp.cos(angles), jnp.sin(angles))


def rotate(values, cosine, sine):
    half = values.shape[-1] // 2
    first_half = values[..., :half]
    second_half = values[..., half:]
    return jnp.concatenate(
        [first_half * cosine - second_half * sine, second_half * cosine + first_half * sine],
        axis=-1,
    )


def head_weights(weights_ref, query_rows):
    block = weights_ref[0]
    col_total, _, lanes = block.shape
    query_w = block[:, :query_rows, :].reshape(col_total * query_rows, lanes)
    latent_w = block[:, query_rows:, :].reshape(-1, lanes)
    return (query_w, latent_w)


def head_queries(query_w, query_t_ref, cos_ref, sin_ref):
    half = ROPE // 2
    proj_t = dot_plain(query_w.T, query_t_ref[...])
    cosine, sine = cos_ref[...], sin_ref[...]
    queries = []
    for begin in range(0, proj_t.shape[0], HEAD):
        head_t = proj_t[begin : begin + HEAD]
        first, second = head_t[NOPE : NOPE + half], head_t[NOPE + half : NOPE + ROPE]
        queries.append(
            jnp.concatenate(
                [
                    head_t[:NOPE],
                    first * cosine - second * sine,
                    second * cosine + first * sine,
                    head_t[NOPE + ROPE :],
                ],
                axis=0,
            ).astype(BF)
        )
    return queries


def head_tile(both, rope_rows, index):
    both = both[:, index * HEAD : (index + 1) * HEAD]
    lane = lax.broadcasted_iota(jnp.int32, both.shape, 1)
    return (jnp.where(lane < NOPE, both, rope_rows), both)


def attend_kernel(
    query_rows, tile, weights_ref, query_t_ref, latent_ref, rope_ref, cos_ref, sin_ref, bias_ref,
    mixed_ref, lse_ref, scores_ref,
):
    query_w, latent_w = head_weights(weights_ref, query_rows)
    queries = head_queries(query_w, query_t_ref, cos_ref, sin_ref)
    projected = dot_plain(latent_ref[...], latent_w).astype(BF)
    length = projected.shape[0]
    for index, query_t in enumerate(queries):
        keys, both = head_tile(projected, rope_ref[...], index)
        values_t = both.T[NOPE:]
        top = None
        for begin in range(0, length, tile):
            rows = slice(begin, begin + tile)
            part = dot_plain(keys[rows], query_t) * (SCALE * LOG2E) + bias_ref[rows, :]
            scores_ref[index, rows, :] = part
            tile_top = jnp.max(part, axis=0, keepdims=True)
            top = tile_top if top is None else jnp.maximum(top, tile_top)
        total, out_t = None, None
        for begin in range(0, length, tile):
            rows = slice(begin, begin + tile)
            expo = jnp.exp2(scores_ref[index, rows, :] - top)
            tile_sum = jnp.sum(expo, axis=0, keepdims=True)
            term = dot_plain(values_t[:, rows], expo.astype(BF))
            total = tile_sum if total is None else total + tile_sum
            out_t = term if out_t is None else out_t + term
        mixed_ref[index * VDIM : (index + 1) * VDIM, :] = (out_t / total).astype(BF)
        lse_ref[index] = top + jnp.log2(total)


def attend_back_kernel(
    query_rows, tile, weights_ref, query_t_ref, latent_ref, latent_t_ref, rope_ref,
    cos_ref, sin_ref, bias_ref, mixed_ref, grad_ref, lse_ref, query_before_ref, latent_before_ref,
    *rest,
):
    weights_grad_ref, query_acc, latent_acc, both_scr = rest[-4:]
    kv_rank = latent_ref.shape[1]
    query_w, latent_w = head_weights(weights_ref, query_rows)
    queries = head_queries(query_w, query_t_ref, cos_ref, sin_ref)
    projected = dot_plain(latent_ref[...], latent_w).astype(BF)
    length = projected.shape[0]

    @pl.when(pl.program_id(0) == 0)
    def _():
        query_acc[...] = query_before_ref[...]
        latent_acc[...] = latent_before_ref[...]

    half = ROPE // 2
    cosine, sine = cos_ref[...], sin_ref[...]
    backs = []
    for index, query_t in enumerate(queries):
        part = slice(index * VDIM, (index + 1) * VDIM)
        lanes = slice(index * HEAD, (index + 1) * HEAD)
        keys, both = head_tile(projected, rope_ref[...], index)
        keys_t, query = keys.T, query_t.T
        grad_t = grad_ref[part, :]
        delta = jnp.sum(
            grad_t.astype(F32) * mixed_ref[part, :].astype(F32), axis=0, keepdims=True
        )
        grad_pad_t = jnp.concatenate([jnp.zeros_like(grad_t), grad_t], axis=0)
        grad_pad = grad_pad_t.T
        lse = lse_ref[index]
        back_t = None
        for begin in range(0, length, tile):
            rows = slice(begin, begin + tile)
            scores = dot_plain(keys[rows], query_t) * (SCALE * LOG2E)
            probs = jnp.exp2(scores + bias_ref[rows, :] - lse)
            prob_grad = dot_plain(both[rows], grad_pad_t)
            score_grad = (probs * (prob_grad - delta)).astype(BF)
            term = dot_plain(keys_t[:, rows], score_grad)
            back_t = term if back_t is None else back_t + term
            key_back = dot_plain(score_grad, query) * SCALE
            value_back = dot_plain(probs.astype(BF), grad_pad)
            latent_acc[rows, kv_rank:] += key_back
            lane = lax.broadcasted_iota(jnp.int32, key_back.shape, 1)
            both_scr[rows, lanes] = jnp.where(lane < NOPE, key_back, value_back).astype(BF)
        back_t = back_t * SCALE
        first, second = back_t[NOPE : NOPE + half], back_t[NOPE + half : NOPE + ROPE]
        backs += [
            back_t[:NOPE],
            first * cosine + second * sine,
            second * cosine - first * sine,
            jnp.zeros_like(back_t[NOPE + ROPE :]),
        ]
    both_back = both_scr[...]
    latent_acc[:, :kv_rank] += dot_trans_right(both_back, latent_w)
    query_back_t = jnp.concatenate(backs, axis=0).astype(BF)
    query_acc[...] += dot_plain(query_w, query_back_t)
    query_wg = dot_trans_right(query_t_ref[...], query_back_t).astype(BF)
    latent_wg = dot_plain(latent_t_ref[...], both_back).astype(BF)
    col_total, lanes = weights_ref.shape[1], weights_ref.shape[3]
    weights_grad_ref[:, 0, :query_rows, :] = query_wg.reshape(col_total, query_rows, lanes)
    weights_grad_ref[:, 0, query_rows:, :] = latent_wg.reshape(col_total, -1, lanes)


def whole(shape):
    return pl.BlockSpec(shape, lambda step: (0,) * len(shape))


def attend(weights, query_t, latent, rope, cos_t, sin_t, bias_t, query_rows, block):
    _, col_total, _, pack_cols = weights.shape
    pack_rows = query_rows + latent.shape[1] // col_total
    heads = pack_cols // HEAD
    group = math.gcd(heads, 2)
    length, local = bias_t.shape
    tile = math.gcd(length, 256)
    return pl.pallas_call(
        functools.partial(attend_kernel, query_rows, tile),
        grid=(heads // group,),
        in_specs=[
            pl.BlockSpec(
                (1, col_total, pack_rows, group * HEAD), lambda step: (block, 0, 0, step)
            ),
            whole(query_t.shape),
            whole(latent.shape),
            whole(rope.shape),
            whole(cos_t.shape),
            whole(sin_t.shape),
            whole(bias_t.shape),
        ],
        out_specs=[
            pl.BlockSpec((group * VDIM, local), lambda step: (step, 0)),
            pl.BlockSpec((group, 1, local), lambda step: (step, 0, 0)),
        ],
        out_shape=[
            jax.ShapeDtypeStruct((heads * VDIM, local), BF),
            jax.ShapeDtypeStruct((heads, 1, local), F32),
        ],
        scratch_shapes=[
            pltpu.VMEM((group, length, local), F32),
        ],
        compiler_params=pltpu.CompilerParams(
            dimension_semantics=("arbitrary",), vmem_limit_bytes=48 * 1024 * 1024
        ),
        cost_estimate=pl.CostEstimate(
            flops=heads * 1_200_000_000,
            bytes_accessed=weights[0].size * 2,
            transcendentals=heads * local * length,
        ),
        name="attend",
    )(weights, query_t, latent, rope, cos_t, sin_t, bias_t)


def attend_back(
    weights, query_t, latent, latent_t, rope, cos_t, sin_t, bias_t, mixed_t, grad_t, lse,
    query_before, latent_before, weights_before, query_rows, block,
):
    row_total, col_total, _, pack_cols = weights.shape
    more = [] if weights_before is None else [weights_before]
    pack_rows = query_rows + latent.shape[1] // col_total
    heads = pack_cols // HEAD
    group = math.gcd(heads, 2)
    steps = heads // group
    length, local = bias_t.shape
    tile = math.gcd(length, 256)
    return pl.pallas_call(
        functools.partial(attend_back_kernel, query_rows, tile),
        grid=(steps,),
        in_specs=[
            pl.BlockSpec(
                (1, col_total, pack_rows, group * HEAD), lambda step: (block, 0, 0, step)
            ),
            whole(query_t.shape),
            whole(latent.shape),
            whole(latent_t.shape),
            whole(rope.shape),
            whole(cos_t.shape),
            whole(sin_t.shape),
            whole(bias_t.shape),
            pl.BlockSpec((group * VDIM, local), lambda step: (step, 0)),
            pl.BlockSpec((group * VDIM, local), lambda step: (block * steps + step, 0)),
            pl.BlockSpec((group, 1, local), lambda step: (step, 0, 0)),
            whole(query_before.shape),
            whole(latent_before.shape),
        ]
        + [pl.BlockSpec(memory_space=pl.ANY)] * len(more),
        out_specs=[
            pl.BlockSpec(
                (col_total, 1, pack_rows, group * HEAD), lambda step: (0, block, 0, step)
            ),
            whole(query_before.shape),
            whole(latent_before.shape),
        ],
        out_shape=[
            jax.ShapeDtypeStruct((col_total, row_total, pack_rows, pack_cols), BF),
            jax.ShapeDtypeStruct(query_before.shape, F32),
            jax.ShapeDtypeStruct(latent_before.shape, F32),
        ],
        input_output_aliases={13: 0} if more else {},
        scratch_shapes=[
            pltpu.VMEM((length, group * HEAD), BF),
        ],
        compiler_params=pltpu.CompilerParams(
            dimension_semantics=("arbitrary",), vmem_limit_bytes=48 * 1024 * 1024
        ),
        cost_estimate=pl.CostEstimate(
            flops=heads * 2_500_000_000,
            bytes_accessed=weights[0].size * 4,
            transcendentals=heads * local * length,
        ),
        name="attend_back",
    )(weights, query_t, latent, latent_t, rope, cos_t, sin_t, bias_t, mixed_t, grad_t, lse,
      query_before, latent_before, *more)


def weight_grad_kernel(chunks, *refs):
    lefts, rights, out_ref = refs[:chunks], refs[chunks : 2 * chunks], refs[2 * chunks]
    total = None
    for left_ref, right_ref in zip(lefts, rights):
        term = dot_plain(left_ref[...].T, right_ref[...])
        total = term if total is None else total + term
    out_ref[...] = total.astype(out_ref.dtype)


def weight_grad(lefts, rights, name):
    chunks = len(lefts)
    rows, width = lefts[0].shape
    units = rights[0].shape[1]
    tile = math.gcd(width, 256)
    return pl.pallas_call(
        functools.partial(weight_grad_kernel, chunks),
        grid=(width // tile,),
        in_specs=[pl.BlockSpec((rows, tile), lambda step: (0, step))] * chunks
        + [pl.BlockSpec((rows, units), lambda step: (0, 0))] * chunks,
        out_specs=pl.BlockSpec((tile, units), lambda step: (step, 0)),
        out_shape=jax.ShapeDtypeStruct((width, units), BF),
        compiler_params=pltpu.CompilerParams(
            dimension_semantics=("arbitrary",), vmem_limit_bytes=48 * 1024 * 1024
        ),
        cost_estimate=pl.CostEstimate(
            flops=2 * chunks * rows * width * units,
            bytes_accessed=2 * (chunks * rows + units) * width,
            transcendentals=0,
        ),
        name=name,
    )(*lefts, *rights)


MESH = pl.DeviceIdType.MESH


def out_grad_kernel(tokens_ref, mixed_ref, out_ref):
    out_ref[...] = dot_trans_right(tokens_ref[...].T, mixed_ref[...]).astype(BF)


def out_weight_grad(tokens, mixed):
    rows, width = tokens.shape
    units = mixed.shape[0]
    tile = math.gcd(width, 256)
    return pl.pallas_call(
        out_grad_kernel,
        grid=(width // tile,),
        in_specs=[
            pl.BlockSpec((rows, tile), lambda step: (0, step)),
            pl.BlockSpec((units, rows), lambda step: (0, 0)),
        ],
        out_specs=pl.BlockSpec((tile, units), lambda step: (step, 0)),
        out_shape=jax.ShapeDtypeStruct((width, units), BF),
        cost_estimate=pl.CostEstimate(
            flops=2 * rows * width * units,
            bytes_accessed=2 * width * units,
            transcendentals=0,
        ),
        name="out_wg",
    )(tokens, mixed)


def flip(index, bit):
    return index + bit - 2 * bit * lax.rem(index // bit, 2)


def chip_bits(col_total):
    bits, bit = [], 2
    while bit < col_total:
        bits.append(bit)
        bit *= 2
    return bits


def turn_bit(bits, row, step, row_total):
    turn = lax.rem(step + (row * len(bits)) // row_total, len(bits))
    return sum(jnp.where(turn == at, bit, 0) for at, bit in enumerate(bits))


def greet(row_total, row_rank, col_rank, bits):
    barrier = pltpu.get_barrier_semaphore()
    for bit in [1] + bits:
        pl.semaphore_signal(
            barrier, inc=1, device_id=(row_rank, flip(col_rank, bit)), device_id_type=MESH
        )

    @pl.when(row_rank > 0)
    def _():
        pl.semaphore_signal(barrier, inc=1, device_id=(row_rank - 1, col_rank), device_id_type=MESH)

    @pl.when(row_rank < row_total - 1)
    def _():
        pl.semaphore_signal(barrier, inc=1, device_id=(row_rank + 1, col_rank), device_id_type=MESH)

    beside = lax.min(row_rank, 1) + lax.min(row_total - 1 - row_rank, 1)
    pl.semaphore_wait(barrier, 1 + len(bits) + beside)


def gather_kernel(
    row_total, col_total, arrays, *refs,
):
    own_refs, out_refs = refs[:arrays], refs[arrays : 2 * arrays]
    own_sem, line_send, line_recv, chip_send, chip_recv, core_send, core_recv = refs[2 * arrays :]
    row_rank, col_rank = lax.axis_index("row"), lax.axis_index("col")
    bits = chip_bits(col_total)
    masks = 2 ** len(bits)
    owns = [
        pltpu.make_async_copy(own_ref, out_ref.at[row_rank, col_rank], own_sem.at[at])
        for at, (own_ref, out_ref) in enumerate(zip(own_refs, out_refs))
    ]
    for own in owns:
        own.start()
    greet(row_total, row_rank, col_rank, bits)
    for own in owns:
        own.wait()

    def block_col(row, mask):
        index = col_rank
        for step in range(len(bits)):
            if mask >> step & 1:
                index = flip(index, turn_bit(bits, row, step, row_total))
        return index

    def line_copy(at, way, row):
        ref = out_refs[at].at[row, col_rank]
        return pltpu.make_async_remote_copy(
            src_ref=ref, dst_ref=ref, send_sem=line_send.at[at, way, row],
            recv_sem=line_recv.at[at, row],
            device_id=(row_rank + 1 - 2 * way, col_rank), device_id_type=MESH,
        )

    def chip_copy(at, row, mask, step):
        ref = out_refs[at].at[row, block_col(row, mask)]
        to = mask + 2**step
        return pltpu.make_async_remote_copy(
            src_ref=ref, dst_ref=ref, send_sem=chip_send.at[at, row, to],
            recv_sem=chip_recv.at[at, row, to],
            device_id=(row_rank, flip(col_rank, turn_bit(bits, row, step, row_total))),
            device_id_type=MESH,
        )

    def core_copy(at, row, mask):
        ref = out_refs[at].at[row, block_col(row, mask)]
        return pltpu.make_async_remote_copy(
            src_ref=ref, dst_ref=ref, send_sem=core_send.at[at, row, mask],
            recv_sem=core_recv.at[at, row, mask], device_id=(row_rank, flip(col_rank, 1)),
            device_id_type=MESH,
        )

    def by_distance(act):
        for away in range(row_total):
            for side in (0,) if away == 0 else (-1, 1):
                row = row_rank + side * away

                @pl.when((row >= 0) & (row < row_total))
                def _():
                    act(row, away, side)

    def arrive(row, away, side):
        for at in range(arrays):
            if away > 0:
                line_copy(at, 0, row).wait_recv()
            if side <= 0:

                @pl.when(row_rank < row_total - 1)
                def _():
                    line_copy(at, 0, row).start()

            if side >= 0:

                @pl.when(row_rank > 0)
                def _():
                    line_copy(at, 1, row).start()

            for step in range(len(bits)):
                chip_copy(at, row, 0, step).start()
            core_copy(at, row, 0).start()

    by_distance(arrive)
    for mask in range(1, masks):
        top = mask.bit_length() - 1

        def forward(row, away, side):
            for at in range(arrays):
                chip_copy(at, row, mask - 2**top, top).wait_recv()
                for step in range(top + 1, len(bits)):
                    chip_copy(at, row, mask, step).start()
                core_copy(at, row, mask).start()

        by_distance(forward)
    for at in range(arrays):
        for row in range(row_total):
            for mask in range(masks):
                core_copy(at, row, mask).wait()
                if mask > 0:
                    top = mask.bit_length() - 1
                    chip_copy(at, row, mask - 2**top, top).wait_send()

            @pl.when((row <= row_rank) & (row_rank < row_total - 1))
            def _():
                line_copy(at, 0, row).wait_send()

            @pl.when((row >= row_rank) & (row_rank > 0))
            def _():
                line_copy(at, 1, row).wait_send()


def gather_all(values, collective_id, name):
    row_total, col_total = lax.axis_size("row"), lax.axis_size("col")
    masks = 2 ** len(chip_bits(col_total))
    arrays = len(values)
    sem = pltpu.SemaphoreType.DMA
    anywhere = pl.BlockSpec(memory_space=pl.ANY)
    return pl.pallas_call(
        functools.partial(gather_kernel, row_total, col_total, arrays),
        in_specs=[anywhere] * arrays,
        out_specs=[anywhere] * arrays,
        out_shape=[
            jax.ShapeDtypeStruct((row_total, col_total) + array.shape, array.dtype)
            for array in values
        ],
        scratch_shapes=[
            sem((arrays,)),
            sem((arrays, 2, row_total)),
            sem((arrays, row_total)),
            sem((arrays, row_total, masks)),
            sem((arrays, row_total, masks)),
            sem((arrays, row_total, masks)),
            sem((arrays, row_total, masks)),
        ],
        compiler_params=pltpu.CompilerParams(
            collective_id=collective_id, has_side_effects=True
        ),
        name=name,
    )(*values)


def add_into(total_ref, other_ref):
    rows = total_ref.shape[0]
    tile = math.gcd(rows, 32)

    def one(step, carry):
        here = pl.ds(pl.multiple_of(step * tile, tile), tile)
        total = total_ref[here, :].astype(F32) + other_ref[here, :].astype(F32)
        total_ref[here, :] = total.astype(total_ref.dtype)
        return carry

    lax.fori_loop(0, rows // tile, one, 0)


class LineReduce:
    def __init__(self, row_total, row_rank, col_rank, block, landed, send, recv):
        self.row_total, self.row_rank, self.col_rank = row_total, row_rank, col_rank
        self.block, self.landed, self.send, self.recv = block, landed, send, recv

    def copy(self, way, row):
        return pltpu.make_async_remote_copy(
            src_ref=self.block(row), dst_ref=self.landed.at[way, row],
            send_sem=self.send.at[way, row], recv_sem=self.recv.at[way, row],
            device_id=(self.row_rank + 1 - 2 * way, self.col_rank), device_id_type=MESH,
        )

    def run(self):
        last = self.row_total - 1
        for step in range(last):
            for way, row in ((0, last - step), (1, step)):
                sends = self.row_rank < row if way == 0 else self.row_rank > row
                gets = self.row_rank > 0 if way == 0 else self.row_rank < last

                @pl.when(sends)
                def _():
                    @pl.when(gets)
                    def _():
                        self.copy(way, row).wait_recv()
                        add_into(self.block(row), self.landed.at[way, row])

                    self.copy(way, row).start()

        for way, gets in ((0, self.row_rank > 0), (1, self.row_rank < last)):

            @pl.when(gets)
            def _():
                self.copy(way, self.row_rank).wait_recv()
                add_into(self.block(self.row_rank), self.landed.at[way, self.row_rank])

    def load(self, from_ref, row):
        rows = from_ref.shape[1]
        tile = math.gcd(rows, 32)

        def one(step, carry):
            here = pl.ds(pl.multiple_of(step * tile, tile), tile)
            self.block(row)[here, :] = from_ref[row, here, :]
            return carry

        lax.fori_loop(0, rows // tile, one, 0)

    def finish(self, out_ref):
        rows = out_ref.shape[0]
        tile = math.gcd(rows, 32)
        own = self.block(self.row_rank)

        def one(step, carry):
            here = pl.ds(pl.multiple_of(step * tile, tile), tile)
            out_ref[here, :] = own[here, :].astype(out_ref.dtype)
            return carry

        lax.fori_loop(0, rows // tile, one, 0)
        for row in range(self.row_total):
            for way, sends in ((0, self.row_rank < row), (1, self.row_rank > row)):

                @pl.when(sends)
                def _():
                    self.copy(way, row).wait_send()


def reduce_kernel(row_total, col_total, part_ref, side_ref, out_ref, side_out_ref, *scratch):
    sums, chip_buf, line_buf, side_sums, side_buf = scratch[:5]
    core_send, core_recv, chip_send, chip_recv = scratch[5:9]
    line_send, line_recv, side_send, side_recv = scratch[9:]
    row_rank, col_rank = lax.axis_index("row"), lax.axis_index("col")
    bits = chip_bits(col_total)
    count = len(bits)
    masks = 2**count
    core = lax.rem(col_rank, 2)
    greet(row_total, row_rank, col_rank, bits)

    def order(row):
        turn = (row * count) // row_total
        return bits[turn:] + bits[:turn]

    def chip_at(row, mask):
        index = col_rank // 2
        for step, bit in enumerate(order(row)):
            if mask >> step & 1:
                index = flip(index, bit // 2)
        return index

    def core_copy(row, mask):
        return pltpu.make_async_remote_copy(
            src_ref=part_ref.at[row, chip_at(row, mask), 1 - core], dst_ref=sums.at[row, mask],
            send_sem=core_send.at[row, mask], recv_sem=core_recv.at[row, mask],
            device_id=(row_rank, flip(col_rank, 1)), device_id_type=MESH,
        )

    def chip_copy(row, mask, step):
        return pltpu.make_async_remote_copy(
            src_ref=sums.at[row, mask], dst_ref=chip_buf.at[row, mask],
            send_sem=chip_send.at[row, mask], recv_sem=chip_recv.at[row, mask],
            device_id=(row_rank, flip(col_rank, order(row)[step])), device_id_type=MESH,
        )

    for mask in range(masks - 1, -1, -1):
        for row in range(row_total):
            core_copy(row, mask).start()
    for mask in range(masks - 1, -1, -1):
        for row in range(row_total):
            core_copy(row, mask).wait_recv()
            add_into(sums.at[row, mask], part_ref.at[row, chip_at(row, mask), core])
            if mask >= masks // 2:
                chip_copy(row, mask, count - 1).start()
    side = LineReduce(
        row_total, row_rank, col_rank, lambda row: side_sums.at[row], side_buf, side_send, side_recv
    )
    for row in range(row_total):
        side.load(side_ref, row)
    side.run()
    for step in range(count - 1, -1, -1):
        half = 2**step
        for mask in range(half - 1, -1, -1):
            for row in range(row_total):
                chip_copy(row, mask + half, step).wait_recv()
                add_into(sums.at[row, mask], chip_buf.at[row, mask + half])
                if step > 0 and mask >= half // 2:
                    chip_copy(row, mask, step - 1).start()
    line = LineReduce(
        row_total, row_rank, col_rank, lambda row: sums.at[row, 0], line_buf, line_send, line_recv
    )
    line.run()
    line.finish(out_ref)
    side.finish(side_out_ref)
    for row in range(row_total):
        for mask in range(masks):
            core_copy(row, mask).wait_send()
            if mask > 0:
                chip_copy(row, mask, mask.bit_length() - 1).wait_send()


def whole_tiles(values):
    rows = values.shape[-2]
    more = -rows % 16
    return jnp.pad(values, ((0, 0),) * (values.ndim - 2) + ((0, more), (0, 0))) if more else values


def reduce_all(parts, side, collective_id, name):
    row_total, col_total, own_rows, lanes = parts.shape
    own_side = side.shape[1]
    parts, side = whole_tiles(parts), whole_tiles(side)
    rows = parts.shape[2]
    parts = parts.reshape(row_total, col_total // 2, 2, rows, lanes)
    masks = col_total // 2
    sem = pltpu.SemaphoreType.DMA
    vmem = pl.BlockSpec(memory_space=pltpu.VMEM)
    out, side_out = pl.pallas_call(
        functools.partial(reduce_kernel, row_total, col_total),
        in_specs=[vmem, vmem],
        out_specs=[vmem, vmem],
        out_shape=[
            jax.ShapeDtypeStruct((rows, lanes), F32),
            jax.ShapeDtypeStruct(side.shape[1:], F32),
        ],
        scratch_shapes=[
            pltpu.VMEM((row_total, masks, rows, lanes), BF),
            pltpu.VMEM((row_total, masks, rows, lanes), BF),
            pltpu.VMEM((2, row_total, rows, lanes), BF),
            pltpu.VMEM(side.shape, BF),
            pltpu.VMEM((2,) + side.shape, BF),
            sem((row_total, masks)),
            sem((row_total, masks)),
            sem((row_total, masks)),
            sem((row_total, masks)),
            sem((2, row_total)),
            sem((2, row_total)),
            sem((2, row_total)),
            sem((2, row_total)),
        ],
        compiler_params=pltpu.CompilerParams(
            collective_id=collective_id, has_side_effects=True, vmem_limit_bytes=48 * 1024 * 1024
        ),
        name=name,
    )(parts, side)
    return (out[:own_rows], side_out[:own_side])


together = lax.optimization_barrier


class Task:
    def __init__(self, steps):
        self.steps, self.state, self.value, self.over = steps, None, None, False

    def advance(self):
        if not self.over:
            try:
                return self.steps.send(self.state)
            except StopIteration as stop:
                self.value, self.over = stop.value, True
        return ()

    def advance_into(self):
        self.state = self.advance()
        return not self.over

    def result(self):
        self.advance()
        assert self.over
        return self.value


def slot(*tasks):
    states = together(tuple(task.advance() for task in tasks))
    for task, state in zip(tasks, states):
        task.state = state


def slots(count, *tasks):
    for _ in range(count):
        slot(*tasks)


def gather_steps(values):
    total = lax.axis_size("row")
    up, down = [None], [None]
    ways = (values, values)
    for step in range(1, total):
        ways = yield (
            lax.ppermute(ways[0], "row", [(i, i + 1) for i in range(step - 1, total - 1)]),
            lax.ppermute(ways[1], "row", [(i, i - 1) for i in range(1, total - step + 1)]),
        )
        up.append(ways[0])
        down.append(ways[1])
    return jnp.concatenate([values] + [up[step] + down[total - step] for step in range(1, total)])


def add_parts(left_op, right_op):
    return (left_op.astype(F32) + right_op.astype(F32)).astype(BF)


def reduce_steps(parts):
    total = lax.axis_size("row")
    ways = None
    for step in range(total - 1):
        sends = (parts[step + 1], parts[total - 1 - step])
        if step > 0:
            sends = (add_parts(sends[0], ways[0]), add_parts(sends[1], ways[1]))
        ways = yield (
            lax.ppermute(sends[0], "row", [(i, i + 1) for i in range(step + 1)]),
            lax.ppermute(sends[1], "row", [(i, i - 1) for i in range(total - 1 - step, total)]),
        )
    return parts[0].astype(F32) + ways[0].astype(F32) + ways[1].astype(F32)


def product_steps(product):
    total = lax.axis_size("row")
    rows = product.shape[0] // total
    parts = [product[at * rows : (at + 1) * rows] for at in range(total)]
    return (yield from reduce_steps(parts))


def pad_to(values, width):
    return jnp.pad(values, ((0, 0), (0, width - values.shape[1])))


def body(
    inputs,
    segments,
    valid_mask,
    teacher,
    cotangent,
    query_down,
    latent_down,
    query_up,
    latent_up,
    output_weight,
    gate_weight,
    up_weight,
    down_weight,
    attn_gain,
    query_gain,
    latent_gain,
    mlp_gain,
):
    both_axes = ("row", "col")
    row_total = lax.axis_size("row")
    col_total = lax.axis_size("col")
    devices = row_total * col_total
    row_rank = lax.axis_index("row")
    local_rows, width = inputs.shape
    length = segments.shape[0]
    q_rank = query_down.shape[1]
    kv_wide = latent_down.shape[1]
    lat_wide = q_rank + kv_wide
    down_rows = query_down.shape[0]
    q_part, kv_part = query_gain.shape[0], latent_gain.shape[0]
    heads_here = output_weight.shape[0] // VDIM
    query_rows = query_up.shape[0]
    offset = row_rank * local_rows

    count = jnp.sum(valid_mask)
    count_parts = jnp.stack([count // 256, count % 256]).astype(F32)
    misc = jnp.concatenate(
        [query_gain.astype(F32), latent_gain.astype(F32), count_parts]
    )
    misc = jnp.pad(misc, (0, down_rows - misc.shape[0])).astype(BF)
    down_pack = jnp.concatenate(
        [query_down, latent_down, attn_gain[:, None], mlp_gain[:, None], misc[:, None]], axis=1
    )
    pack_wide = -(-(lat_wide + 3) // 128) * 128
    down_pack = pad_to(down_pack, pack_wide)

    query_pack = jnp.pad(
        query_up.reshape(query_rows, heads_here, NOPE + ROPE),
        ((0, 0), (0, 0), (0, HEAD - NOPE - ROPE)),
    ).reshape(query_rows, heads_here * HEAD)
    up_pack = jnp.concatenate([query_pack, latent_up], axis=0)
    pack_rows = up_pack.shape[0]
    down_all, head_w = gather_all([down_pack, up_pack], 1, "gather_pack")
    down_all = down_all.reshape(devices * down_rows, pack_wide)
    attn_g = down_all[:, lat_wide].astype(F32)
    mlp_g = down_all[:, lat_wide + 1].astype(F32)
    misc_all = down_all[:, lat_wide + 2].astype(F32).reshape(devices, down_rows)
    query_g = misc_all[:, :q_part].reshape(-1)
    latent_g = misc_all[:, q_part : q_part + kv_part].reshape(-1)
    query_g, out_here = together((query_g, output_weight.T))
    out_all = lax.all_gather(out_here, both_axes, axis=0, tiled=True).reshape(
        row_total, width, heads_here * VDIM
    )
    counts = jnp.sum(misc_all[:, q_part + kv_part : q_part + kv_part + 2], axis=0)
    valid_total = counts[0] * 256.0 + counts[1]

    cosine, sine = rotary(segments)
    cos_here = lax.dynamic_slice_in_dim(cosine, offset, local_rows, 0)
    sin_here = lax.dynamic_slice_in_dim(sine, offset, local_rows, 0)
    tokens_f = inputs.astype(F32)
    normed, normed_unit = root_norm(tokens_f, attn_g)
    normed_b = normed.astype(BF)
    lat = dot_plain(normed_b, down_all)
    query_lat, kv_lat = lat[:, :q_rank], lat[:, q_rank:lat_wide]
    query_norm, query_unit = root_norm(query_lat, query_g)
    kv_norm, kv_unit = root_norm(kv_lat[:, :KV_RANK], latent_g)
    key_rope = rotate(kv_lat[:, KV_RANK:], cos_here, sin_here)
    query_nb = query_norm.astype(BF)
    latent_pack = jnp.concatenate(
        [
            kv_norm,
            jnp.zeros((local_rows, NOPE), F32),
            key_rope,
            jnp.zeros((local_rows, HEAD - NOPE - ROPE), F32),
        ],
        axis=1,
    ).astype(BF)
    latent_give = Task(gather_steps(latent_pack))
    while latent_give.advance_into():
        pass
    latent_all = together(latent_give.value)
    blocks = latent_all.reshape(row_total, local_rows, -1)
    froms = [lax.rem(row_rank + row_total - step, row_total) for step in range(row_total)]
    latent_all = jnp.concatenate(
        [lax.dynamic_index_in_dim(blocks, at, 0, keepdims=False) for at in froms]
    )

    kept = 0
    for block in range(row_total):
        begin = block * local_rows
        ahead = [CONTS - at for at in range(1, CONTS + 1) if begin < length - (CONTS - at) * CONT_LEN]
        passed = CONTS - 1 - max(ahead)
        kept = max(kept, begin + local_rows - passed * CONT_LEN)
    kept = min(length, -(-kept // 256) * 256)
    query_at = offset + jnp.arange(local_rows, dtype=jnp.int32)
    query_seg = lax.dynamic_slice_in_dim(segments, offset, local_rows, 0)
    prompt = jnp.sum((segments == 0).astype(jnp.int32))
    shift = jnp.maximum(jnp.sum((segments < query_seg[0]).astype(jnp.int32)) - prompt, 0)

    def keep(values):
        far = jnp.pad(values, ((0, kept),) + ((0, 0),) * (values.ndim - 1))
        far = lax.dynamic_slice_in_dim(far, shift, kept, 0)
        near = jnp.arange(kept, dtype=jnp.int32) < prompt
        return jnp.where(near.reshape((kept,) + (1,) * (values.ndim - 1)), values[:kept], far)

    def spread(values):
        places = jnp.arange(length, dtype=jnp.int32)[:, None]
        near = jnp.pad(values, ((0, length - kept), (0, 0)))
        far = jnp.pad(values, ((length, length - kept), (0, 0)))
        far = lax.dynamic_slice_in_dim(far, length - shift, length, 0)
        return jnp.where(places < prompt, near, jnp.where(places < prompt + shift, 0.0, far))

    kept_all = keep(latent_all)
    kv_all = kept_all[:, :KV_RANK]
    rope_all = kept_all[:, KV_RANK:]
    key_at = jnp.arange(kept, dtype=jnp.int32)
    key_at = jnp.where(key_at < prompt, key_at, key_at + shift)
    key_seg = keep(segments)
    allowed_t = (key_at[:, None] <= query_at[None, :]) & (
        (key_seg[:, None] == 0) | (key_seg[:, None] == query_seg[None, :])
    )
    bias_t = jnp.where(allowed_t, 0.0, HIDE).astype(F32)
    query_t = query_nb.T
    cos_t, sin_t = cos_here.T, sin_here.T
    cut = row_total // 2
    mixed = [
        attend(head_w, query_t, kv_all, rope_all, cos_t, sin_t, bias_t, query_rows, block)
        for block in range(cut)
    ]
    mixed, out_all, query_t, gate_here, up_here, down_here = together(
        (mixed, out_all, query_t, gate_weight, up_weight, down_weight.T)
    )
    gate_full, up_full, down_t = (
        lax.all_gather(gate_here, "col", axis=0, tiled=True),
        lax.all_gather(up_here, "col", axis=0, tiled=True),
        lax.all_gather(down_here, "col", axis=0, tiled=True),
    )
    mixed += [
        attend(head_w, query_t, kv_all, rope_all, cos_t, sin_t, bias_t, query_rows, block)
        for block in range(cut, row_total)
    ]
    attn_sum = None
    for block in range(row_total):
        term = dot_dims(mixed[block][0], out_all[block], (0,), (1,))
        attn_sum = term if attn_sum is None else attn_sum + term

    residual = tokens_f + RES * attn_sum
    mlp_in, mlp_unit = root_norm(residual, mlp_g)
    mlp_b = mlp_in.astype(BF)
    weight_v = valid_mask.astype(F32)[:, None]
    out_scale = local_rows * devices / valid_total
    rows = local_rows // 2
    parts = [slice(0, rows), slice(rows, 2 * rows)]

    def forward_steps(tokens):
        gate_act = yield dot_plain(tokens, gate_full).astype(BF)
        gate_f = gate_act.astype(F32)
        up_act = dot_plain(tokens, up_full)
        hidden = yield (gate_f * jax.nn.sigmoid(gate_f) * up_act).astype(BF)
        up_act = up_act.astype(BF)
        product = yield dot_trans_right(hidden, down_t).astype(BF)
        return (gate_act, up_act, hidden, product)

    def judge(part, down_sum):
        out_rows = residual[part] + RES * down_sum
        error_val = out_rows - teacher[part].astype(F32)
        squared = 0.5 * jnp.sum(weight_v[part] * error_val * error_val)
        grad_rows = cotangent[part].astype(F32) + out_scale * weight_v[part] * error_val
        return (out_rows.astype(BF), squared, grad_rows, (RES * grad_rows).astype(BF))

    def backward_steps(branch, gate_act, up_act):
        gate_act, up_act = gate_act.astype(F32), up_act.astype(F32)
        gate_sig = jax.nn.sigmoid(gate_act)
        hidden_grad = dot_plain(branch, down_t)
        gate_grad, up_grad = yield (
            (hidden_grad * up_act * gate_sig * (1.0 + gate_act * (1.0 - gate_sig))).astype(BF),
            (hidden_grad * gate_act * gate_sig).astype(BF),
        )
        product = yield dot_trans_right(gate_grad, gate_full)
        product = yield (product + dot_trans_right(up_grad, up_full)).astype(BF)
        return (gate_grad, up_grad, product)

    def weight_steps(work):
        got = []
        for lefts, rights, name in work:
            got.append((yield weight_grad(lefts, rights, name)))
        return got

    hops = row_total - 1
    mlp_b = mlp_in.astype(BF)
    give_0, give_1 = [Task(gather_steps(mlp_b[part])) for part in parts]
    slots(hops, give_0)
    tokens_0, gate_full, up_full = together((give_0.result(), gate_full, up_full))
    fore_0 = Task(forward_steps(tokens_0))
    slots(hops, give_1, fore_0)
    tokens_1 = give_1.result()
    fore_0 = fore_0.result()
    take_0 = Task(product_steps(fore_0[3]))
    fore_1 = Task(forward_steps(tokens_1))
    slots(hops, take_0, fore_1)
    judged_0 = judge(parts[0], take_0.result())
    fore_1 = fore_1.result()
    take_1 = Task(product_steps(fore_1[3]))
    give_0 = Task(gather_steps(judged_0[3]))
    slot(give_0)
    slots(hops - 1, give_0, take_1)
    branch_0 = give_0.result()
    back_0 = Task(backward_steps(branch_0, fore_0[0], fore_0[1]))
    slot(take_1, back_0)
    judged_1 = judge(parts[1], take_1.result())
    give_1 = Task(gather_steps(judged_1[3]))
    slots(hops - 1, give_1, back_0)
    back_0 = back_0.result()
    take_0 = Task(product_steps(back_0[2]))
    slot(give_1, take_0)
    branch_1 = give_1.result()
    back_1 = Task(backward_steps(branch_1, fore_1[0], fore_1[1]))
    down_work = Task(weight_steps([([branch_0, branch_1], [fore_0[2], fore_1[2]], "down_wg")]))
    slot(take_0, down_work)
    slots(hops - 2, take_0, back_1)
    grad_0 = take_0.result()
    (down_wg,) = down_work.result()
    while back_1.advance_into():
        pass
    back_1 = back_1.value
    take_1 = Task(product_steps(back_1[2]))
    work = Task(
        weight_steps(
            [
                ([tokens_0, tokens_1], [back_0[0], back_1[0]], "gate_wg"),
                ([tokens_0, tokens_1], [back_0[1], back_1[1]], "up_wg"),
            ]
        )
    )
    slots(max(hops, 2), take_1, work)
    grad_1 = take_1.result()
    gate_wg, up_wg = work.result()
    outputs = jnp.concatenate([judged_0[0], judged_1[0]])
    squared = judged_0[1] + judged_1[1]
    out_grad = jnp.concatenate([judged_0[2], judged_1[2]])
    mlp_in_grad = jnp.concatenate([grad_0, grad_1])
    gate_wg, up_wg, down_wg = (
        lax.psum_scatter(gate_wg, "col", scatter_dimension=0, tiled=True),
        lax.psum_scatter(up_wg, "col", scatter_dimension=0, tiled=True),
        lax.psum_scatter(down_wg, "col", scatter_dimension=0, tiled=True),
    )
    residual_part, mlp_gain_grad = norm_back(mlp_in_grad, mlp_unit, residual, mlp_g)
    residual_grad = out_grad + residual_part

    attn_grad_in = (RES * residual_grad).astype(BF)
    grad_t = dot_dims(out_all, attn_grad_in, (1,), (1,)).astype(BF)
    latent_t = kv_all.T
    out_wg = out_weight_grad(attn_grad_in, jnp.concatenate([mixed_t for mixed_t, _ in mixed]))
    grad_t, out_wg = together((grad_t.reshape(-1, local_rows), out_wg))
    out_wg = lax.psum_scatter(out_wg, "col", scatter_dimension=0, tiled=True)
    query_back_t = jnp.zeros(query_t.shape, F32)
    latent_back = jnp.zeros(kept_all.shape, F32)
    head_wg = None
    for block, (mixed_t, lse) in enumerate(mixed):
        if block == cut:
            query_back_t, gate_wg, up_wg, down_wg = together((query_back_t, gate_wg, up_wg, down_wg))
        head_wg, query_back_t, latent_back = attend_back(
            head_w, query_t, kv_all, latent_t, rope_all, cos_t, sin_t, bias_t, mixed_t,
            grad_t, lse, query_back_t, latent_back, head_wg, query_rows, block,
        )
    head_wg = lax.psum_scatter(
        head_wg.reshape(devices * pack_rows, heads_here * HEAD), "col",
        scatter_dimension=0, tiled=True,
    ).reshape(row_total, pack_rows, heads_here * HEAD)
    latent_rows = spread(latent_back).astype(BF).reshape(blocks.shape)
    latent_reduce = Task(
        reduce_steps(
            [lax.dynamic_index_in_dim(latent_rows, at, 0, keepdims=False) for at in froms]
        )
    )
    while latent_reduce.advance_into():
        pass
    latent_back = latent_reduce.value
    kv_norm_grad = latent_back[:, :KV_RANK]
    rope_grad = latent_back[:, KV_RANK + NOPE : KV_RANK + NOPE + ROPE]
    query_norm_grad = query_back_t.T
    query_lat_grad, query_gain_grad = norm_back(query_norm_grad, query_unit, query_lat, query_g)
    kv_lat_part, latent_gain_grad = norm_back(kv_norm_grad, kv_unit, kv_lat[:, :KV_RANK], latent_g)
    lat_grad = jnp.concatenate(
        [
            query_lat_grad,
            kv_lat_part,
            rotate(rope_grad, cos_here, -sin_here),
            jnp.zeros((local_rows, pack_wide - lat_wide), F32),
        ],
        axis=-1,
    ).astype(BF)
    lat_wg = dot_trans_left(normed_b, lat_grad)
    normed_grad = dot_trans_right(lat_grad, down_all)
    input_part, attention_gain_gradient = norm_back(normed_grad, normed_unit, tokens_f, attn_g)
    input_grad = residual_grad + input_part

    loss_high = squared.astype(BF).astype(F32)
    loss_low = squared - loss_high
    misc_grad = jnp.concatenate(
        [
            query_gain_grad.reshape(devices, q_part),
            latent_gain_grad.reshape(devices, kv_part),
            jnp.broadcast_to(loss_high, (devices, 1)),
            jnp.broadcast_to(loss_low, (devices, 1)),
        ],
        axis=1,
    )
    misc_grad = pad_to(misc_grad, down_rows).reshape(devices * down_rows, 1)
    lane = lax.broadcasted_iota(jnp.int32, lat_wg.shape, 1)
    small = jnp.where(lane == lat_wide, attention_gain_gradient[:, None], lat_wg)
    small = jnp.where(lane == lat_wide + 1, mlp_gain_grad[:, None], small)
    small = jnp.where(lane == lat_wide + 2, misc_grad, small).astype(BF)
    small = small.reshape(row_total, col_total, down_rows, pack_wide)
    units = heads_here * VDIM
    out_wg = jnp.stack(
        [out_wg[:, at * units : (at + 1) * units] for at in range(row_total)]
    )
    small, out_wg = reduce_all(small, out_wg, 3, "reduce_down")
    out_wg = out_wg.T
    small, head_wg = together((small, head_wg))
    head_reduce = Task(
        reduce_steps([lax.dynamic_index_in_dim(head_wg, at, 0, keepdims=False) for at in froms])
    )
    slots(hops, head_reduce)
    head_wg = head_reduce.result()
    qu_wg = head_wg[:query_rows].reshape(query_rows, heads_here, HEAD)[:, :, : NOPE + ROPE]
    qu_wg = qu_wg.reshape(query_rows, heads_here * (NOPE + ROPE))
    kvu_wg = head_wg[query_rows:]
    misc_sum = small[:, lat_wide + 2]
    at = q_part + kv_part
    loss = (misc_sum[at] + misc_sum[at + 1]) / valid_total
    return (
        outputs,
        loss,
        input_grad,
        small[:, :q_rank],
        small[:, q_rank:lat_wide],
        qu_wg,
        kvu_wg,
        out_wg,
        gate_wg.astype(F32),
        up_wg.astype(F32),
        down_wg.astype(F32).T,
        small[:, lat_wide],
        misc_sum[:q_part],
        misc_sum[q_part : q_part + kv_part],
        small[:, lat_wide + 1],
    )


def solution(mesh):
    in_specs = (
        P(("col", "row"), None),
        P("col"),
        P(("col", "row")),
        P(("col", "row"), None),
        P(("col", "row"), None),
        P(("row", "col"), None),
        P(("row", "col"), None),
        P("col", "row"),
        P("col", "row"),
        P("row", "col"),
        P("col", "row"),
        P("col", "row"),
        P("row", "col"),
        P(("row", "col")),
        P(("row", "col")),
        P(("row", "col")),
        P(("row", "col")),
    )
    out_specs = (
        P(("col", "row"), None),
        P(),
        P(("col", "row"), None),
        P(("row", "col"), None),
        P(("row", "col"), None),
        P("col", "row"),
        P("col", "row"),
        P("row", "col"),
        P("col", "row"),
        P("col", "row"),
        P("row", "col"),
        P(("row", "col")),
        P(("row", "col")),
        P(("row", "col")),
        P(("row", "col")),
    )
    return jax.shard_map(body, mesh=mesh, in_specs=in_specs, out_specs=out_specs, check_vma=False)
```

```python
import functools
import math

import jax
import jax.numpy as jnp
from jax import lax
from jax.experimental import pallas as pl
from jax.experimental.pallas import tpu as pltpu
from jax.sharding import PartitionSpec as P

NOPE = 64
ROPE = 32
VDIM = 64
KV_RANK = 256
CONTS = 4
CONT_LEN = 256
HEAD = 128

EPS = 1e-05
RES = 1.4 / math.sqrt(62.0)
BASE = 10000.0
SCALE = (NOPE + ROPE) ** (-0.5)
LOG2E = math.log2(math.e)
HIDE = -1e30
BF = jnp.bfloat16
F32 = jnp.float32


def dot_plain(left_op, right_op):
    return jnp.dot(left_op, right_op, preferred_element_type=F32)


def dot_dims(left_op, right_op, left_dims, right_dims):
    return lax.dot_general(
        left_op, right_op, ((left_dims, right_dims), ((), ())), preferred_element_type=F32
    )


def dot_trans_left(left_op, right_op):
    return dot_dims(left_op, right_op, (0,), (0,))


def dot_trans_right(left_op, right_op):
    return dot_dims(left_op, right_op, (1,), (1,))


def root_norm(values, gain):
    unit_rows = values * lax.rsqrt(jnp.mean(values * values, axis=-1, keepdims=True) + EPS)
    return (unit_rows * gain, unit_rows)


def norm_back(grad_rows, unit_rows, values, gain):
    factor = lax.rsqrt(jnp.mean(values * values, axis=-1, keepdims=True) + EPS)
    scaled = grad_rows * gain
    value_grad = factor * (
        scaled - unit_rows * jnp.mean(scaled * unit_rows, axis=-1, keepdims=True)
    )
    return (value_grad, jnp.sum(grad_rows * unit_rows, axis=0))


def rotary(segments):
    length = segments.shape[0]
    indices = jnp.arange(length, dtype=jnp.int32)
    labels = jnp.arange(CONTS + 1, dtype=jnp.int32)
    member = (segments[:, None] == labels[None, :]).astype(jnp.int32)
    counts = jnp.sum(member, axis=0)
    starts = jnp.cumsum(counts) - counts
    first_at = jnp.sum(member * starts[None, :], axis=1)
    places = jnp.where(segments == 0, indices, counts[0] + indices - first_at).astype(F32)
    freqs = BASE ** (-jnp.arange(ROPE // 2, dtype=F32) * 2.0 / ROPE)
    angles = places[:, None] * freqs[None, :]
    return (jnp.cos(angles), jnp.sin(angles))


def rotate(values, cosine, sine):
    half = values.shape[-1] // 2
    first_half = values[..., :half]
    second_half = values[..., half:]
    return jnp.concatenate(
        [first_half * cosine - second_half * sine, second_half * cosine + first_half * sine],
        axis=-1,
    )


def head_weights(weights_ref, query_rows):
    block = weights_ref[0]
    col_total, _, lanes = block.shape
    query_w = block[:, :query_rows, :].reshape(col_total * query_rows, lanes)
    latent_w = block[:, query_rows:, :].reshape(-1, lanes)
    return (query_w, latent_w)


def head_queries(query_w, query_t_ref, cos_ref, sin_ref):
    half = ROPE // 2
    proj_t = dot_plain(query_w.T, query_t_ref[...])
    cosine, sine = cos_ref[...], sin_ref[...]
    queries = []
    for begin in range(0, proj_t.shape[0], HEAD):
        head_t = proj_t[begin : begin + HEAD]
        first, second = head_t[NOPE : NOPE + half], head_t[NOPE + half : NOPE + ROPE]
        queries.append(
            jnp.concatenate(
                [
                    head_t[:NOPE],
                    first * cosine - second * sine,
                    second * cosine + first * sine,
                    head_t[NOPE + ROPE :],
                ],
                axis=0,
            ).astype(BF)
        )
    return queries


def head_tile(both, rope_rows, index):
    both = both[:, index * HEAD : (index + 1) * HEAD]
    lane = lax.broadcasted_iota(jnp.int32, both.shape, 1)
    return (jnp.where(lane < NOPE, both, rope_rows), both)


def attend_kernel(
    query_rows, tile, weights_ref, query_t_ref, latent_ref, rope_ref, cos_ref, sin_ref, bias_ref,
    mixed_ref, lse_ref, scores_ref,
):
    query_w, latent_w = head_weights(weights_ref, query_rows)
    queries = head_queries(query_w, query_t_ref, cos_ref, sin_ref)
    projected = dot_plain(latent_ref[...], latent_w).astype(BF)
    length = projected.shape[0]
    for index, query_t in enumerate(queries):
        keys, both = head_tile(projected, rope_ref[...], index)
        values_t = both.T[NOPE:]
        top = None
        for begin in range(0, length, tile):
            rows = slice(begin, begin + tile)
            part = dot_plain(keys[rows], query_t) * (SCALE * LOG2E) + bias_ref[rows, :]
            scores_ref[index, rows, :] = part
            tile_top = jnp.max(part, axis=0, keepdims=True)
            top = tile_top if top is None else jnp.maximum(top, tile_top)
        total, out_t = None, None
        for begin in range(0, length, tile):
            rows = slice(begin, begin + tile)
            expo = jnp.exp2(scores_ref[index, rows, :] - top)
            tile_sum = jnp.sum(expo, axis=0, keepdims=True)
            term = dot_plain(values_t[:, rows], expo.astype(BF))
            total = tile_sum if total is None else total + tile_sum
            out_t = term if out_t is None else out_t + term
        mixed_ref[index * VDIM : (index + 1) * VDIM, :] = (out_t / total).astype(BF)
        lse_ref[index] = top + jnp.log2(total)


def attend_back_kernel(
    query_rows, tile, weights_ref, query_t_ref, latent_ref, latent_t_ref, rope_ref,
    cos_ref, sin_ref, bias_ref, mixed_ref, grad_ref, lse_ref, query_before_ref, latent_before_ref,
    *rest,
):
    weights_grad_ref, query_acc, latent_acc, both_scr = rest[-4:]
    kv_rank = latent_ref.shape[1]
    query_w, latent_w = head_weights(weights_ref, query_rows)
    queries = head_queries(query_w, query_t_ref, cos_ref, sin_ref)
    projected = dot_plain(latent_ref[...], latent_w).astype(BF)
    length = projected.shape[0]

    @pl.when(pl.program_id(0) == 0)
    def _():
        query_acc[...] = query_before_ref[...]
        latent_acc[...] = latent_before_ref[...]

    half = ROPE // 2
    cosine, sine = cos_ref[...], sin_ref[...]
    backs = []
    for index, query_t in enumerate(queries):
        part = slice(index * VDIM, (index + 1) * VDIM)
        lanes = slice(index * HEAD, (index + 1) * HEAD)
        keys, both = head_tile(projected, rope_ref[...], index)
        keys_t, query = keys.T, query_t.T
        grad_t = grad_ref[part, :]
        delta = jnp.sum(
            grad_t.astype(F32) * mixed_ref[part, :].astype(F32), axis=0, keepdims=True
        )
        grad_pad_t = jnp.concatenate([jnp.zeros_like(grad_t), grad_t], axis=0)
        grad_pad = grad_pad_t.T
        lse = lse_ref[index]
        back_t = None
        for begin in range(0, length, tile):
            rows = slice(begin, begin + tile)
            scores = dot_plain(keys[rows], query_t) * (SCALE * LOG2E)
            probs = jnp.exp2(scores + bias_ref[rows, :] - lse)
            prob_grad = dot_plain(both[rows], grad_pad_t)
            score_grad = (probs * (prob_grad - delta)).astype(BF)
            term = dot_plain(keys_t[:, rows], score_grad)
            back_t = term if back_t is None else back_t + term
            key_back = dot_plain(score_grad, query) * SCALE
            value_back = dot_plain(probs.astype(BF), grad_pad)
            latent_acc[rows, kv_rank:] += key_back
            lane = lax.broadcasted_iota(jnp.int32, key_back.shape, 1)
            both_scr[rows, lanes] = jnp.where(lane < NOPE, key_back, value_back).astype(BF)
        back_t = back_t * SCALE
        first, second = back_t[NOPE : NOPE + half], back_t[NOPE + half : NOPE + ROPE]
        backs += [
            back_t[:NOPE],
            first * cosine + second * sine,
            second * cosine - first * sine,
            jnp.zeros_like(back_t[NOPE + ROPE :]),
        ]
    both_back = both_scr[...]
    latent_acc[:, :kv_rank] += dot_trans_right(both_back, latent_w)
    query_back_t = jnp.concatenate(backs, axis=0).astype(BF)
    query_acc[...] += dot_plain(query_w, query_back_t)
    query_wg = dot_trans_right(query_t_ref[...], query_back_t).astype(BF)
    latent_wg = dot_plain(latent_t_ref[...], both_back).astype(BF)
    col_total, lanes = weights_ref.shape[1], weights_ref.shape[3]
    weights_grad_ref[:, 0, :query_rows, :] = query_wg.reshape(col_total, query_rows, lanes)
    weights_grad_ref[:, 0, query_rows:, :] = latent_wg.reshape(col_total, -1, lanes)


def whole(shape):
    return pl.BlockSpec(shape, lambda step: (0,) * len(shape))


def attend(weights, query_t, latent, rope, cos_t, sin_t, bias_t, query_rows, block):
    _, col_total, _, pack_cols = weights.shape
    pack_rows = query_rows + latent.shape[1] // col_total
    heads = pack_cols // HEAD
    group = math.gcd(heads, 2)
    length, local = bias_t.shape
    tile = math.gcd(length, 256)
    return pl.pallas_call(
        functools.partial(attend_kernel, query_rows, tile),
        grid=(heads // group,),
        in_specs=[
            pl.BlockSpec(
                (1, col_total, pack_rows, group * HEAD), lambda step: (block, 0, 0, step)
            ),
            whole(query_t.shape),
            whole(latent.shape),
            whole(rope.shape),
            whole(cos_t.shape),
            whole(sin_t.shape),
            whole(bias_t.shape),
        ],
        out_specs=[
            pl.BlockSpec((group * VDIM, local), lambda step: (step, 0)),
            pl.BlockSpec((group, 1, local), lambda step: (step, 0, 0)),
        ],
        out_shape=[
            jax.ShapeDtypeStruct((heads * VDIM, local), BF),
            jax.ShapeDtypeStruct((heads, 1, local), F32),
        ],
        scratch_shapes=[
            pltpu.VMEM((group, length, local), F32),
        ],
        compiler_params=pltpu.CompilerParams(
            dimension_semantics=("arbitrary",), vmem_limit_bytes=48 * 1024 * 1024
        ),
        cost_estimate=pl.CostEstimate(
            flops=heads * 1_200_000_000,
            bytes_accessed=weights[0].size * 2,
            transcendentals=heads * local * length,
        ),
        name="attend",
    )(weights, query_t, latent, rope, cos_t, sin_t, bias_t)


def attend_back(
    weights, query_t, latent, latent_t, rope, cos_t, sin_t, bias_t, mixed_t, grad_t, lse,
    query_before, latent_before, weights_before, query_rows, block,
):
    row_total, col_total, _, pack_cols = weights.shape
    more = [] if weights_before is None else [weights_before]
    pack_rows = query_rows + latent.shape[1] // col_total
    heads = pack_cols // HEAD
    group = math.gcd(heads, 2)
    steps = heads // group
    length, local = bias_t.shape
    tile = math.gcd(length, 256)
    return pl.pallas_call(
        functools.partial(attend_back_kernel, query_rows, tile),
        grid=(steps,),
        in_specs=[
            pl.BlockSpec(
                (1, col_total, pack_rows, group * HEAD), lambda step: (block, 0, 0, step)
            ),
            whole(query_t.shape),
            whole(latent.shape),
            whole(latent_t.shape),
            whole(rope.shape),
            whole(cos_t.shape),
            whole(sin_t.shape),
            whole(bias_t.shape),
            pl.BlockSpec((group * VDIM, local), lambda step: (step, 0)),
            pl.BlockSpec((group * VDIM, local), lambda step: (block * steps + step, 0)),
            pl.BlockSpec((group, 1, local), lambda step: (step, 0, 0)),
            whole(query_before.shape),
            whole(latent_before.shape),
        ]
        + [pl.BlockSpec(memory_space=pl.ANY)] * len(more),
        out_specs=[
            pl.BlockSpec(
                (col_total, 1, pack_rows, group * HEAD), lambda step: (0, block, 0, step)
            ),
            whole(query_before.shape),
            whole(latent_before.shape),
        ],
        out_shape=[
            jax.ShapeDtypeStruct((col_total, row_total, pack_rows, pack_cols), BF),
            jax.ShapeDtypeStruct(query_before.shape, F32),
            jax.ShapeDtypeStruct(latent_before.shape, F32),
        ],
        input_output_aliases={13: 0} if more else {},
        scratch_shapes=[
            pltpu.VMEM((length, group * HEAD), BF),
        ],
        compiler_params=pltpu.CompilerParams(
            dimension_semantics=("arbitrary",), vmem_limit_bytes=48 * 1024 * 1024
        ),
        cost_estimate=pl.CostEstimate(
            flops=heads * 2_500_000_000,
            bytes_accessed=weights[0].size * 4,
            transcendentals=heads * local * length,
        ),
        name="attend_back",
    )(weights, query_t, latent, latent_t, rope, cos_t, sin_t, bias_t, mixed_t, grad_t, lse,
      query_before, latent_before, *more)


def weight_grad_kernel(chunks, *refs):
    lefts, rights, out_ref = refs[:chunks], refs[chunks : 2 * chunks], refs[2 * chunks]
    total = None
    for left_ref, right_ref in zip(lefts, rights):
        term = dot_plain(left_ref[...].T, right_ref[...])
        total = term if total is None else total + term
    out_ref[...] = total.astype(out_ref.dtype)


def weight_grad(lefts, rights, name):
    chunks = len(lefts)
    rows, width = lefts[0].shape
    units = rights[0].shape[1]
    tile = math.gcd(width, 256)
    return pl.pallas_call(
        functools.partial(weight_grad_kernel, chunks),
        grid=(width // tile,),
        in_specs=[pl.BlockSpec((rows, tile), lambda step: (0, step))] * chunks
        + [pl.BlockSpec((rows, units), lambda step: (0, 0))] * chunks,
        out_specs=pl.BlockSpec((tile, units), lambda step: (step, 0)),
        out_shape=jax.ShapeDtypeStruct((width, units), BF),
        compiler_params=pltpu.CompilerParams(
            dimension_semantics=("arbitrary",), vmem_limit_bytes=48 * 1024 * 1024
        ),
        cost_estimate=pl.CostEstimate(
            flops=2 * chunks * rows * width * units,
            bytes_accessed=2 * (chunks * rows + units) * width,
            transcendentals=0,
        ),
        name=name,
    )(*lefts, *rights)


MESH = pl.DeviceIdType.MESH


def out_grad_kernel(tokens_ref, mixed_ref, out_ref):
    out_ref[...] = dot_trans_right(tokens_ref[...].T, mixed_ref[...]).astype(BF)


def out_weight_grad(tokens, mixed):
    rows, width = tokens.shape
    units = mixed.shape[0]
    tile = math.gcd(width, 256)
    return pl.pallas_call(
        out_grad_kernel,
        grid=(width // tile,),
        in_specs=[
            pl.BlockSpec((rows, tile), lambda step: (0, step)),
            pl.BlockSpec((units, rows), lambda step: (0, 0)),
        ],
        out_specs=pl.BlockSpec((tile, units), lambda step: (step, 0)),
        out_shape=jax.ShapeDtypeStruct((width, units), BF),
        cost_estimate=pl.CostEstimate(
            flops=2 * rows * width * units,
            bytes_accessed=2 * width * units,
            transcendentals=0,
        ),
        name="out_wg",
    )(tokens, mixed)


def flip(index, bit):
    return index + bit - 2 * bit * lax.rem(index // bit, 2)


def chip_bits(col_total):
    bits, bit = [], 2
    while bit < col_total:
        bits.append(bit)
        bit *= 2
    return bits


def turn_bit(bits, row, step, row_total):
    turn = lax.rem(step + (row * len(bits)) // row_total, len(bits))
    return sum(jnp.where(turn == at, bit, 0) for at, bit in enumerate(bits))


def greet(row_total, row_rank, col_rank, bits):
    barrier = pltpu.get_barrier_semaphore()
    for bit in [1] + bits:
        pl.semaphore_signal(
            barrier, inc=1, device_id=(row_rank, flip(col_rank, bit)), device_id_type=MESH
        )

    @pl.when(row_rank > 0)
    def _():
        pl.semaphore_signal(barrier, inc=1, device_id=(row_rank - 1, col_rank), device_id_type=MESH)

    @pl.when(row_rank < row_total - 1)
    def _():
        pl.semaphore_signal(barrier, inc=1, device_id=(row_rank + 1, col_rank), device_id_type=MESH)

    beside = lax.min(row_rank, 1) + lax.min(row_total - 1 - row_rank, 1)
    pl.semaphore_wait(barrier, 1 + len(bits) + beside)


def gather_kernel(
    row_total, col_total, arrays, *refs,
):
    own_refs, out_refs = refs[:arrays], refs[arrays : 2 * arrays]
    own_sem, line_send, line_recv, chip_send, chip_recv, core_send, core_recv = refs[2 * arrays :]
    row_rank, col_rank = lax.axis_index("row"), lax.axis_index("col")
    bits = chip_bits(col_total)
    masks = 2 ** len(bits)
    owns = [
        pltpu.make_async_copy(own_ref, out_ref.at[row_rank, col_rank], own_sem.at[at])
        for at, (own_ref, out_ref) in enumerate(zip(own_refs, out_refs))
    ]
    for own in owns:
        own.start()
    greet(row_total, row_rank, col_rank, bits)

    def block_col(row, mask):
        index = col_rank
        for step in range(len(bits)):
            if mask >> step & 1:
                index = flip(index, turn_bit(bits, row, step, row_total))
        return index

    def line_copy(at, way, row, own=False):
        ref = out_refs[at].at[row, col_rank]
        return pltpu.make_async_remote_copy(
            src_ref=own_refs[at] if own else ref, dst_ref=ref, send_sem=line_send.at[at, way, row],
            recv_sem=line_recv.at[at, row],
            device_id=(row_rank + 1 - 2 * way, col_rank), device_id_type=MESH,
        )

    def chip_copy(at, row, mask, step, own=False):
        ref = out_refs[at].at[row, block_col(row, mask)]
        to = mask + 2**step
        return pltpu.make_async_remote_copy(
            src_ref=own_refs[at] if own else ref, dst_ref=ref, send_sem=chip_send.at[at, row, to],
            recv_sem=chip_recv.at[at, row, to],
            device_id=(row_rank, flip(col_rank, turn_bit(bits, row, step, row_total))),
            device_id_type=MESH,
        )

    def core_copy(at, row, mask, own=False):
        ref = out_refs[at].at[row, block_col(row, mask)]
        return pltpu.make_async_remote_copy(
            src_ref=own_refs[at] if own else ref, dst_ref=ref, send_sem=core_send.at[at, row, mask],
            recv_sem=core_recv.at[at, row, mask], device_id=(row_rank, flip(col_rank, 1)),
            device_id_type=MESH,
        )

    def by_distance(act):
        for away in range(row_total):
            for side in (0,) if away == 0 else (-1, 1):
                row = row_rank + side * away

                @pl.when((row >= 0) & (row < row_total))
                def _():
                    act(row, away, side)

    def arrive(row, away, side):
        for at in range(arrays):
            if away > 0:
                line_copy(at, 0, row).wait_recv()
            if side <= 0:

                @pl.when(row_rank < row_total - 1)
                def _():
                    line_copy(at, 0, row, away == 0).start()

            if side >= 0:

                @pl.when(row_rank > 0)
                def _():
                    line_copy(at, 1, row, away == 0).start()

            for step in range(len(bits)):
                chip_copy(at, row, 0, step, away == 0).start()
            core_copy(at, row, 0, away == 0).start()

    by_distance(arrive)
    for mask in range(1, masks):
        top = mask.bit_length() - 1

        def forward(row, away, side):
            for at in range(arrays):
                chip_copy(at, row, mask - 2**top, top).wait_recv()
                for step in range(top + 1, len(bits)):
                    chip_copy(at, row, mask, step).start()
                core_copy(at, row, mask).start()

        by_distance(forward)
    for own in owns:
        own.wait()
    for at in range(arrays):
        for row in range(row_total):
            for mask in range(masks):
                core_copy(at, row, mask).wait()
                if mask > 0:
                    top = mask.bit_length() - 1
                    chip_copy(at, row, mask - 2**top, top).wait_send()

            @pl.when((row <= row_rank) & (row_rank < row_total - 1))
            def _():
                line_copy(at, 0, row).wait_send()

            @pl.when((row >= row_rank) & (row_rank > 0))
            def _():
                line_copy(at, 1, row).wait_send()


def gather_all(values, collective_id, name):
    row_total, col_total = lax.axis_size("row"), lax.axis_size("col")
    masks = 2 ** len(chip_bits(col_total))
    arrays = len(values)
    sem = pltpu.SemaphoreType.DMA
    anywhere = pl.BlockSpec(memory_space=pl.ANY)
    return pl.pallas_call(
        functools.partial(gather_kernel, row_total, col_total, arrays),
        in_specs=[anywhere] * arrays,
        out_specs=[anywhere] * arrays,
        out_shape=[
            jax.ShapeDtypeStruct((row_total, col_total) + array.shape, array.dtype)
            for array in values
        ],
        scratch_shapes=[
            sem((arrays,)),
            sem((arrays, 2, row_total)),
            sem((arrays, row_total)),
            sem((arrays, row_total, masks)),
            sem((arrays, row_total, masks)),
            sem((arrays, row_total, masks)),
            sem((arrays, row_total, masks)),
        ],
        compiler_params=pltpu.CompilerParams(
            collective_id=collective_id, has_side_effects=True
        ),
        name=name,
    )(*values)


def add_into(total_ref, other_ref):
    rows = total_ref.shape[0]
    tile = math.gcd(rows, 32)

    def one(step, carry):
        here = pl.ds(pl.multiple_of(step * tile, tile), tile)
        total = total_ref[here, :].astype(F32) + other_ref[here, :].astype(F32)
        total_ref[here, :] = total.astype(total_ref.dtype)
        return carry

    lax.fori_loop(0, rows // tile, one, 0)


class LineReduce:
    def __init__(self, row_total, row_rank, col_rank, block, landed, send, recv):
        self.row_total, self.row_rank, self.col_rank = row_total, row_rank, col_rank
        self.block, self.landed, self.send, self.recv = block, landed, send, recv

    def copy(self, way, row):
        return pltpu.make_async_remote_copy(
            src_ref=self.block(row), dst_ref=self.landed.at[way, row],
            send_sem=self.send.at[way, row], recv_sem=self.recv.at[way, row],
            device_id=(self.row_rank + 1 - 2 * way, self.col_rank), device_id_type=MESH,
        )

    def run(self):
        last = self.row_total - 1
        for step in range(last):
            for way, row in ((0, last - step), (1, step)):
                sends = self.row_rank < row if way == 0 else self.row_rank > row
                gets = self.row_rank > 0 if way == 0 else self.row_rank < last

                @pl.when(sends)
                def _():
                    @pl.when(gets)
                    def _():
                        self.copy(way, row).wait_recv()
                        add_into(self.block(row), self.landed.at[way, row])

                    self.copy(way, row).start()

        for way, gets in ((0, self.row_rank > 0), (1, self.row_rank < last)):

            @pl.when(gets)
            def _():
                self.copy(way, self.row_rank).wait_recv()
                add_into(self.block(self.row_rank), self.landed.at[way, self.row_rank])

    def load(self, from_ref, row):
        rows = from_ref.shape[1]
        tile = math.gcd(rows, 32)

        def one(step, carry):
            here = pl.ds(pl.multiple_of(step * tile, tile), tile)
            self.block(row)[here, :] = from_ref[row, here, :]
            return carry

        lax.fori_loop(0, rows // tile, one, 0)

    def finish(self, out_ref):
        rows = out_ref.shape[0]
        tile = math.gcd(rows, 32)
        own = self.block(self.row_rank)

        def one(step, carry):
            here = pl.ds(pl.multiple_of(step * tile, tile), tile)
            out_ref[here, :] = own[here, :].astype(out_ref.dtype)
            return carry

        lax.fori_loop(0, rows // tile, one, 0)
        for row in range(self.row_total):
            for way, sends in ((0, self.row_rank < row), (1, self.row_rank > row)):

                @pl.when(sends)
                def _():
                    self.copy(way, row).wait_send()


def reduce_kernel(row_total, col_total, part_ref, side_ref, out_ref, side_out_ref, *scratch):
    sums, chip_buf, line_buf, side_sums, side_buf = scratch[:5]
    core_send, core_recv, chip_send, chip_recv = scratch[5:9]
    line_send, line_recv, side_send, side_recv = scratch[9:]
    row_rank, col_rank = lax.axis_index("row"), lax.axis_index("col")
    bits = chip_bits(col_total)
    count = len(bits)
    masks = 2**count
    core = lax.rem(col_rank, 2)
    greet(row_total, row_rank, col_rank, bits)

    def order(row):
        turn = (row * count) // row_total
        return bits[turn:] + bits[:turn]

    def chip_at(row, mask):
        index = col_rank // 2
        for step, bit in enumerate(order(row)):
            if mask >> step & 1:
                index = flip(index, bit // 2)
        return index

    def core_copy(row, mask):
        return pltpu.make_async_remote_copy(
            src_ref=part_ref.at[row, chip_at(row, mask), 1 - core], dst_ref=sums.at[row, mask],
            send_sem=core_send.at[row, mask], recv_sem=core_recv.at[row, mask],
            device_id=(row_rank, flip(col_rank, 1)), device_id_type=MESH,
        )

    def chip_copy(row, mask, step):
        return pltpu.make_async_remote_copy(
            src_ref=sums.at[row, mask], dst_ref=chip_buf.at[row, mask],
            send_sem=chip_send.at[row, mask], recv_sem=chip_recv.at[row, mask],
            device_id=(row_rank, flip(col_rank, order(row)[step])), device_id_type=MESH,
        )

    for mask in range(masks - 1, -1, -1):
        for row in range(row_total):
            core_copy(row, mask).start()
    for mask in range(masks - 1, -1, -1):
        for row in range(row_total):
            core_copy(row, mask).wait_recv()
            add_into(sums.at[row, mask], part_ref.at[row, chip_at(row, mask), core])
            if mask >= masks // 2:
                chip_copy(row, mask, count - 1).start()
    side = LineReduce(
        row_total, row_rank, col_rank, lambda row: side_sums.at[row], side_buf, side_send, side_recv
    )
    for row in range(row_total):
        side.load(side_ref, row)
    side.run()
    for step in range(count - 1, -1, -1):
        half = 2**step
        for mask in range(half - 1, -1, -1):
            for row in range(row_total):
                chip_copy(row, mask + half, step).wait_recv()
                add_into(sums.at[row, mask], chip_buf.at[row, mask + half])
                if step > 0 and mask >= half // 2:
                    chip_copy(row, mask, step - 1).start()
    line = LineReduce(
        row_total, row_rank, col_rank, lambda row: sums.at[row, 0], line_buf, line_send, line_recv
    )
    line.run()
    line.finish(out_ref)
    side.finish(side_out_ref)
    for row in range(row_total):
        for mask in range(masks):
            core_copy(row, mask).wait_send()
            if mask > 0:
                chip_copy(row, mask, mask.bit_length() - 1).wait_send()


def whole_tiles(values):
    rows = values.shape[-2]
    more = -rows % 16
    return jnp.pad(values, ((0, 0),) * (values.ndim - 2) + ((0, more), (0, 0))) if more else values


def reduce_all(parts, side, collective_id, name):
    row_total, col_total, own_rows, lanes = parts.shape
    own_side = side.shape[1]
    parts, side = whole_tiles(parts), whole_tiles(side)
    rows = parts.shape[2]
    parts = parts.reshape(row_total, col_total // 2, 2, rows, lanes)
    masks = col_total // 2
    sem = pltpu.SemaphoreType.DMA
    vmem = pl.BlockSpec(memory_space=pltpu.VMEM)
    out, side_out = pl.pallas_call(
        functools.partial(reduce_kernel, row_total, col_total),
        in_specs=[vmem, vmem],
        out_specs=[vmem, vmem],
        out_shape=[
            jax.ShapeDtypeStruct((rows, lanes), F32),
            jax.ShapeDtypeStruct(side.shape[1:], F32),
        ],
        scratch_shapes=[
            pltpu.VMEM((row_total, masks, rows, lanes), BF),
            pltpu.VMEM((row_total, masks, rows, lanes), BF),
            pltpu.VMEM((2, row_total, rows, lanes), BF),
            pltpu.VMEM(side.shape, BF),
            pltpu.VMEM((2,) + side.shape, BF),
            sem((row_total, masks)),
            sem((row_total, masks)),
            sem((row_total, masks)),
            sem((row_total, masks)),
            sem((2, row_total)),
            sem((2, row_total)),
            sem((2, row_total)),
            sem((2, row_total)),
        ],
        compiler_params=pltpu.CompilerParams(
            collective_id=collective_id, has_side_effects=True, vmem_limit_bytes=48 * 1024 * 1024
        ),
        name=name,
    )(parts, side)
    return (out[:own_rows], side_out[:own_side])


together = lax.optimization_barrier


class Task:
    def __init__(self, steps):
        self.steps, self.state, self.value, self.over = steps, None, None, False

    def advance(self):
        if not self.over:
            try:
                return self.steps.send(self.state)
            except StopIteration as stop:
                self.value, self.over = stop.value, True
        return ()

    def advance_into(self):
        self.state = self.advance()
        return not self.over

    def result(self):
        self.advance()
        assert self.over
        return self.value


def slot(*tasks):
    states = together(tuple(task.advance() for task in tasks))
    for task, state in zip(tasks, states):
        task.state = state


def slots(count, *tasks):
    for _ in range(count):
        slot(*tasks)


def gather_steps(values):
    total = lax.axis_size("row")
    up, down = [None], [None]
    ways = (values, values)
    for step in range(1, total):
        ways = yield (
            lax.ppermute(ways[0], "row", [(i, i + 1) for i in range(step - 1, total - 1)]),
            lax.ppermute(ways[1], "row", [(i, i - 1) for i in range(1, total - step + 1)]),
        )
        up.append(ways[0])
        down.append(ways[1])
    return jnp.concatenate([values] + [up[step] + down[total - step] for step in range(1, total)])


def add_parts(left_op, right_op):
    return (left_op.astype(F32) + right_op.astype(F32)).astype(BF)


def reduce_steps(parts):
    total = lax.axis_size("row")
    ways = None
    for step in range(total - 1):
        sends = (parts[step + 1], parts[total - 1 - step])
        if step > 0:
            sends = (add_parts(sends[0], ways[0]), add_parts(sends[1], ways[1]))
        ways = yield (
            lax.ppermute(sends[0], "row", [(i, i + 1) for i in range(step + 1)]),
            lax.ppermute(sends[1], "row", [(i, i - 1) for i in range(total - 1 - step, total)]),
        )
    return parts[0].astype(F32) + ways[0].astype(F32) + ways[1].astype(F32)


def product_steps(product):
    total = lax.axis_size("row")
    rows = product.shape[0] // total
    parts = [product[at * rows : (at + 1) * rows] for at in range(total)]
    return (yield from reduce_steps(parts))


def pad_to(values, width):
    return jnp.pad(values, ((0, 0), (0, width - values.shape[1])))


def body(
    inputs,
    segments,
    valid_mask,
    teacher,
    cotangent,
    query_down,
    latent_down,
    query_up,
    latent_up,
    output_weight,
    gate_weight,
    up_weight,
    down_weight,
    attn_gain,
    query_gain,
    latent_gain,
    mlp_gain,
):
    both_axes = ("row", "col")
    row_total = lax.axis_size("row")
    col_total = lax.axis_size("col")
    devices = row_total * col_total
    row_rank = lax.axis_index("row")
    local_rows, width = inputs.shape
    length = segments.shape[0]
    q_rank = query_down.shape[1]
    kv_wide = latent_down.shape[1]
    lat_wide = q_rank + kv_wide
    down_rows = query_down.shape[0]
    q_part, kv_part = query_gain.shape[0], latent_gain.shape[0]
    heads_here = output_weight.shape[0] // VDIM
    query_rows = query_up.shape[0]
    offset = row_rank * local_rows

    count = jnp.sum(valid_mask)
    count_parts = jnp.stack([count // 256, count % 256]).astype(F32)
    misc = jnp.concatenate(
        [query_gain.astype(F32), latent_gain.astype(F32), count_parts]
    )
    misc = jnp.pad(misc, (0, down_rows - misc.shape[0])).astype(BF)
    down_pack = jnp.concatenate(
        [query_down, latent_down, attn_gain[:, None], mlp_gain[:, None], misc[:, None]], axis=1
    )
    pack_wide = -(-(lat_wide + 3) // 128) * 128
    down_pack = pad_to(down_pack, pack_wide)

    query_pack = jnp.pad(
        query_up.reshape(query_rows, heads_here, NOPE + ROPE),
        ((0, 0), (0, 0), (0, HEAD - NOPE - ROPE)),
    ).reshape(query_rows, heads_here * HEAD)
    up_pack = jnp.concatenate([query_pack, latent_up], axis=0)
    pack_rows = up_pack.shape[0]
    down_all, head_w = gather_all([down_pack, up_pack], 1, "gather_pack")
    down_all = down_all.reshape(devices * down_rows, pack_wide)
    attn_g = down_all[:, lat_wide].astype(F32)
    mlp_g = down_all[:, lat_wide + 1].astype(F32)
    misc_all = down_all[:, lat_wide + 2].astype(F32).reshape(devices, down_rows)
    query_g = misc_all[:, :q_part].reshape(-1)
    latent_g = misc_all[:, q_part : q_part + kv_part].reshape(-1)
    query_g, out_here = together((query_g, output_weight.T))
    out_all = lax.all_gather(out_here, both_axes, axis=0, tiled=True).reshape(
        row_total, width, heads_here * VDIM
    )
    counts = jnp.sum(misc_all[:, q_part + kv_part : q_part + kv_part + 2], axis=0)
    valid_total = counts[0] * 256.0 + counts[1]

    cosine, sine = rotary(segments)
    cos_here = lax.dynamic_slice_in_dim(cosine, offset, local_rows, 0)
    sin_here = lax.dynamic_slice_in_dim(sine, offset, local_rows, 0)
    tokens_f = inputs.astype(F32)
    normed, normed_unit = root_norm(tokens_f, attn_g)
    normed_b = normed.astype(BF)
    lat = dot_plain(normed_b, down_all)
    query_lat, kv_lat = lat[:, :q_rank], lat[:, q_rank:lat_wide]
    query_norm, query_unit = root_norm(query_lat, query_g)
    kv_norm, kv_unit = root_norm(kv_lat[:, :KV_RANK], latent_g)
    key_rope = rotate(kv_lat[:, KV_RANK:], cos_here, sin_here)
    query_nb = query_norm.astype(BF)
    latent_pack = jnp.concatenate(
        [
            kv_norm,
            jnp.zeros((local_rows, NOPE), F32),
            key_rope,
            jnp.zeros((local_rows, HEAD - NOPE - ROPE), F32),
        ],
        axis=1,
    ).astype(BF)
    latent_give = Task(gather_steps(latent_pack))
    while latent_give.advance_into():
        pass
    latent_blocks, gate_here, up_here, down_here = together(
        (latent_give.value, gate_weight, up_weight, down_weight.T)
    )
    gate_full, up_full, down_t = (
        lax.all_gather(gate_here, "col", axis=0, tiled=True),
        lax.all_gather(up_here, "col", axis=0, tiled=True),
        lax.all_gather(down_here, "col", axis=0, tiled=True),
    )
    froms = [lax.rem(row_rank + row_total - step, row_total) for step in range(row_total)]

    kept = 0
    for block in range(row_total):
        begin = block * local_rows
        ahead = [CONTS - at for at in range(1, CONTS + 1) if begin < length - (CONTS - at) * CONT_LEN]
        passed = CONTS - 1 - max(ahead)
        kept = max(kept, begin + local_rows - passed * CONT_LEN)
    kept = min(length, -(-kept // 256) * 256)
    query_at = offset + jnp.arange(local_rows, dtype=jnp.int32)
    query_seg = lax.dynamic_slice_in_dim(segments, offset, local_rows, 0)
    prompt = jnp.sum((segments == 0).astype(jnp.int32))
    shift = jnp.maximum(jnp.sum((segments < query_seg[0]).astype(jnp.int32)) - prompt, 0)

    def keep(values):
        far = lax.dynamic_slice_in_dim(values, shift, kept, 0)
        near = jnp.arange(kept, dtype=jnp.int32) < prompt
        return jnp.where(near.reshape((kept,) + (1,) * (values.ndim - 1)), values[:kept], far)

    def spread(values):
        places = jnp.arange(length, dtype=jnp.int32)[:, None]
        near = jnp.pad(values, ((0, length - kept), (0, 0)))
        far = jnp.pad(values, ((length, length - kept), (0, 0)))
        far = lax.dynamic_slice_in_dim(far, length - shift, length, 0)
        return jnp.where(places < prompt, near, jnp.where(places < prompt + shift, 0.0, far))

    latent_all = jnp.zeros((length + kept, latent_pack.shape[1]), BF)
    for step, at in enumerate(froms):
        latent_all = lax.dynamic_update_slice_in_dim(
            latent_all, latent_blocks[step * local_rows : (step + 1) * local_rows],
            at * local_rows, 0,
        )
    kept_all = keep(latent_all)
    kv_all = kept_all[:, :KV_RANK]
    rope_all = kept_all[:, KV_RANK:]
    key_at = jnp.arange(kept, dtype=jnp.int32)
    key_at = jnp.where(key_at < prompt, key_at, key_at + shift)
    key_seg = keep(jnp.pad(segments, (0, kept)))
    allowed_t = (key_at[:, None] <= query_at[None, :]) & (
        (key_seg[:, None] == 0) | (key_seg[:, None] == query_seg[None, :])
    )
    bias_t = jnp.where(allowed_t, 0.0, HIDE).astype(F32)
    query_t = query_nb.T
    cos_t, sin_t = cos_here.T, sin_here.T
    cut = row_total // 2
    mixed = [
        attend(head_w, query_t, kv_all, rope_all, cos_t, sin_t, bias_t, query_rows, block)
        for block in range(cut)
    ]
    mixed, out_all, query_t = together((mixed, out_all, query_t))
    mixed += [
        attend(head_w, query_t, kv_all, rope_all, cos_t, sin_t, bias_t, query_rows, block)
        for block in range(cut, row_total)
    ]
    attn_sum = None
    for block in range(row_total):
        term = dot_dims(mixed[block][0], out_all[block], (0,), (1,))
        attn_sum = term if attn_sum is None else attn_sum + term

    residual = tokens_f + RES * attn_sum
    mlp_in, mlp_unit = root_norm(residual, mlp_g)
    mlp_b = mlp_in.astype(BF)
    weight_v = valid_mask.astype(F32)[:, None]
    out_scale = local_rows * devices / valid_total
    rows = local_rows // 2
    parts = [slice(0, rows), slice(rows, 2 * rows)]

    def forward_steps(tokens):
        gate_act = yield dot_plain(tokens, gate_full).astype(BF)
        gate_f = gate_act.astype(F32)
        up_act = dot_plain(tokens, up_full)
        hidden = yield (gate_f * jax.nn.sigmoid(gate_f) * up_act).astype(BF)
        up_act = up_act.astype(BF)
        product = yield dot_trans_right(hidden, down_t).astype(BF)
        return (gate_act, up_act, hidden, product)

    def judge(part, down_sum):
        out_rows = residual[part] + RES * down_sum
        error_val = out_rows - teacher[part].astype(F32)
        squared = 0.5 * jnp.sum(weight_v[part] * error_val * error_val)
        grad_rows = cotangent[part].astype(F32) + out_scale * weight_v[part] * error_val
        return (out_rows.astype(BF), squared, grad_rows, (RES * grad_rows).astype(BF))

    def backward_steps(branch, gate_act, up_act):
        gate_act, up_act = gate_act.astype(F32), up_act.astype(F32)
        gate_sig = jax.nn.sigmoid(gate_act)
        hidden_grad = dot_plain(branch, down_t)
        gate_grad, up_grad = yield (
            (hidden_grad * up_act * gate_sig * (1.0 + gate_act * (1.0 - gate_sig))).astype(BF),
            (hidden_grad * gate_act * gate_sig).astype(BF),
        )
        product = yield dot_trans_right(gate_grad, gate_full)
        product = yield (product + dot_trans_right(up_grad, up_full)).astype(BF)
        return (gate_grad, up_grad, product)

    def weight_steps(work):
        got = []
        for lefts, rights, name in work:
            got.append((yield weight_grad(lefts, rights, name)))
        return got

    hops = row_total - 1
    mlp_b = mlp_in.astype(BF)
    give_0, give_1 = [Task(gather_steps(mlp_b[part])) for part in parts]
    slots(hops, give_0)
    tokens_0, gate_full, up_full = together((give_0.result(), gate_full, up_full))
    fore_0 = Task(forward_steps(tokens_0))
    slots(hops, give_1, fore_0)
    tokens_1 = give_1.result()
    fore_0 = fore_0.result()
    take_0 = Task(product_steps(fore_0[3]))
    fore_1 = Task(forward_steps(tokens_1))
    slots(hops, take_0, fore_1)
    judged_0 = judge(parts[0], take_0.result())
    fore_1 = fore_1.result()
    take_1 = Task(product_steps(fore_1[3]))
    give_0 = Task(gather_steps(judged_0[3]))
    slot(give_0)
    slots(hops - 1, give_0, take_1)
    branch_0 = give_0.result()
    back_0 = Task(backward_steps(branch_0, fore_0[0], fore_0[1]))
    slot(take_1, back_0)
    judged_1 = judge(parts[1], take_1.result())
    give_1 = Task(gather_steps(judged_1[3]))
    slots(hops - 1, give_1, back_0)
    back_0 = back_0.result()
    take_0 = Task(product_steps(back_0[2]))
    slot(give_1, take_0)
    branch_1 = give_1.result()
    back_1 = Task(backward_steps(branch_1, fore_1[0], fore_1[1]))
    down_work = Task(weight_steps([([branch_0, branch_1], [fore_0[2], fore_1[2]], "down_wg")]))
    slot(take_0, down_work)
    slots(hops - 2, take_0, back_1)
    grad_0 = take_0.result()
    (down_wg,) = down_work.result()
    while back_1.advance_into():
        pass
    back_1 = back_1.value
    take_1 = Task(product_steps(back_1[2]))
    work = Task(
        weight_steps(
            [
                ([tokens_0, tokens_1], [back_0[0], back_1[0]], "gate_wg"),
                ([tokens_0, tokens_1], [back_0[1], back_1[1]], "up_wg"),
            ]
        )
    )
    slots(max(hops, 2), take_1, work)
    grad_1 = take_1.result()
    gate_wg, up_wg = work.result()
    outputs = jnp.concatenate([judged_0[0], judged_1[0]])
    squared = judged_0[1] + judged_1[1]
    out_grad = jnp.concatenate([judged_0[2], judged_1[2]])
    mlp_in_grad = jnp.concatenate([grad_0, grad_1])
    gate_wg, up_wg, down_wg = (
        lax.psum_scatter(gate_wg, "col", scatter_dimension=0, tiled=True),
        lax.psum_scatter(up_wg, "col", scatter_dimension=0, tiled=True),
        lax.psum_scatter(down_wg, "col", scatter_dimension=0, tiled=True),
    )
    residual_part, mlp_gain_grad = norm_back(mlp_in_grad, mlp_unit, residual, mlp_g)
    residual_grad = out_grad + residual_part

    attn_grad_in = (RES * residual_grad).astype(BF)
    grad_t = dot_dims(out_all, attn_grad_in, (1,), (1,)).astype(BF)
    latent_t = kv_all.T
    out_wg = out_weight_grad(attn_grad_in, jnp.concatenate([mixed_t for mixed_t, _ in mixed]))
    grad_t, out_wg = together((grad_t.reshape(-1, local_rows), out_wg))
    out_wg = lax.psum_scatter(out_wg, "col", scatter_dimension=0, tiled=True)
    query_back_t = jnp.zeros(query_t.shape, F32)
    latent_back = jnp.zeros(kept_all.shape, F32)
    head_wg = None
    for block, (mixed_t, lse) in enumerate(mixed):
        if block == cut:
            query_back_t, gate_wg, up_wg, down_wg = together((query_back_t, gate_wg, up_wg, down_wg))
        head_wg, query_back_t, latent_back = attend_back(
            head_w, query_t, kv_all, latent_t, rope_all, cos_t, sin_t, bias_t, mixed_t,
            grad_t, lse, query_back_t, latent_back, head_wg, query_rows, block,
        )
    head_wg = lax.psum_scatter(
        head_wg.reshape(devices * pack_rows, heads_here * HEAD), "col",
        scatter_dimension=0, tiled=True,
    ).reshape(row_total, pack_rows, heads_here * HEAD)
    latent_rows = spread(latent_back).astype(BF).reshape(row_total, local_rows, -1)
    latent_reduce = Task(
        reduce_steps(
            [lax.dynamic_index_in_dim(latent_rows, at, 0, keepdims=False) for at in froms]
        )
    )
    while latent_reduce.advance_into():
        pass
    latent_back = latent_reduce.value
    kv_norm_grad = latent_back[:, :KV_RANK]
    rope_grad = latent_back[:, KV_RANK + NOPE : KV_RANK + NOPE + ROPE]
    query_norm_grad = query_back_t.T
    query_lat_grad, query_gain_grad = norm_back(query_norm_grad, query_unit, query_lat, query_g)
    kv_lat_part, latent_gain_grad = norm_back(kv_norm_grad, kv_unit, kv_lat[:, :KV_RANK], latent_g)
    lat_grad = jnp.concatenate(
        [
            query_lat_grad,
            kv_lat_part,
            rotate(rope_grad, cos_here, -sin_here),
            jnp.zeros((local_rows, pack_wide - lat_wide), F32),
        ],
        axis=-1,
    ).astype(BF)
    lat_wg = dot_trans_left(normed_b, lat_grad)
    normed_grad = dot_trans_right(lat_grad, down_all)
    input_part, attention_gain_gradient = norm_back(normed_grad, normed_unit, tokens_f, attn_g)
    input_grad = residual_grad + input_part

    loss_high = squared.astype(BF).astype(F32)
    loss_low = squared - loss_high
    misc_grad = jnp.concatenate(
        [
            query_gain_grad.reshape(devices, q_part),
            latent_gain_grad.reshape(devices, kv_part),
            jnp.broadcast_to(loss_high, (devices, 1)),
            jnp.broadcast_to(loss_low, (devices, 1)),
        ],
        axis=1,
    )
    misc_grad = pad_to(misc_grad, down_rows).reshape(devices * down_rows, 1)
    lane = lax.broadcasted_iota(jnp.int32, lat_wg.shape, 1)
    small = jnp.where(lane == lat_wide, attention_gain_gradient[:, None], lat_wg)
    small = jnp.where(lane == lat_wide + 1, mlp_gain_grad[:, None], small)
    small = jnp.where(lane == lat_wide + 2, misc_grad, small).astype(BF)
    small = small.reshape(row_total, col_total, down_rows, pack_wide)
    units = heads_here * VDIM
    out_wg = jnp.stack(
        [out_wg[:, at * units : (at + 1) * units] for at in range(row_total)]
    )
    small, out_wg = reduce_all(small, out_wg, 3, "reduce_down")
    out_wg = out_wg.T
    small, head_wg = together((small, head_wg))
    head_reduce = Task(
        reduce_steps([lax.dynamic_index_in_dim(head_wg, at, 0, keepdims=False) for at in froms])
    )
    slots(hops, head_reduce)
    head_wg = head_reduce.result()
    qu_wg = head_wg[:query_rows].reshape(query_rows, heads_here, HEAD)[:, :, : NOPE + ROPE]
    qu_wg = qu_wg.reshape(query_rows, heads_here * (NOPE + ROPE))
    kvu_wg = head_wg[query_rows:]
    misc_sum = small[:, lat_wide + 2]
    at = q_part + kv_part
    loss = (misc_sum[at] + misc_sum[at + 1]) / valid_total
    return (
        outputs,
        loss,
        input_grad,
        small[:, :q_rank],
        small[:, q_rank:lat_wide],
        qu_wg,
        kvu_wg,
        out_wg,
        gate_wg.astype(F32),
        up_wg.astype(F32),
        down_wg.astype(F32).T,
        small[:, lat_wide],
        misc_sum[:q_part],
        misc_sum[q_part : q_part + kv_part],
        small[:, lat_wide + 1],
    )


def solution(mesh):
    in_specs = (
        P(("col", "row"), None),
        P("col"),
        P(("col", "row")),
        P(("col", "row"), None),
        P(("col", "row"), None),
        P(("row", "col"), None),
        P(("row", "col"), None),
        P("col", "row"),
        P("col", "row"),
        P("row", "col"),
        P("col", "row"),
        P("col", "row"),
        P("row", "col"),
        P(("row", "col")),
        P(("row", "col")),
        P(("row", "col")),
        P(("row", "col")),
    )
    out_specs = (
        P(("col", "row"), None),
        P(),
        P(("col", "row"), None),
        P(("row", "col"), None),
        P(("row", "col"), None),
        P("col", "row"),
        P("col", "row"),
        P("row", "col"),
        P("col", "row"),
        P("col", "row"),
        P("row", "col"),
        P(("row", "col")),
        P(("row", "col")),
        P(("row", "col")),
        P(("row", "col")),
    )
    return jax.shard_map(body, mesh=mesh, in_specs=in_specs, out_specs=out_specs, check_vma=False)
```

```python
import functools
import math

import jax
import jax.numpy as jnp
from jax import lax
from jax.experimental import pallas as pl
from jax.experimental.pallas import tpu as pltpu
from jax.sharding import PartitionSpec as P

NOPE = 64
ROPE = 32
VDIM = 64
KV_RANK = 256
CONTS = 4
CONT_LEN = 256
HEAD = 128

EPS = 1e-05
RES = 1.4 / math.sqrt(62.0)
BASE = 10000.0
SCALE = (NOPE + ROPE) ** (-0.5)
LOG2E = math.log2(math.e)
HIDE = -1e30
BF = jnp.bfloat16
F32 = jnp.float32


def dot_plain(left_op, right_op):
    return jnp.dot(left_op, right_op, preferred_element_type=F32)


def dot_dims(left_op, right_op, left_dims, right_dims):
    return lax.dot_general(
        left_op, right_op, ((left_dims, right_dims), ((), ())), preferred_element_type=F32
    )


def dot_trans_left(left_op, right_op):
    return dot_dims(left_op, right_op, (0,), (0,))


def dot_trans_right(left_op, right_op):
    return dot_dims(left_op, right_op, (1,), (1,))


def root_norm(values, gain):
    unit_rows = values * lax.rsqrt(jnp.mean(values * values, axis=-1, keepdims=True) + EPS)
    return (unit_rows * gain, unit_rows)


def norm_back(grad_rows, unit_rows, values, gain):
    factor = lax.rsqrt(jnp.mean(values * values, axis=-1, keepdims=True) + EPS)
    scaled = grad_rows * gain
    value_grad = factor * (
        scaled - unit_rows * jnp.mean(scaled * unit_rows, axis=-1, keepdims=True)
    )
    return (value_grad, jnp.sum(grad_rows * unit_rows, axis=0))


def rotary(segments):
    length = segments.shape[0]
    indices = jnp.arange(length, dtype=jnp.int32)
    labels = jnp.arange(CONTS + 1, dtype=jnp.int32)
    member = (segments[:, None] == labels[None, :]).astype(jnp.int32)
    counts = jnp.sum(member, axis=0)
    starts = jnp.cumsum(counts) - counts
    first_at = jnp.sum(member * starts[None, :], axis=1)
    places = jnp.where(segments == 0, indices, counts[0] + indices - first_at).astype(F32)
    freqs = BASE ** (-jnp.arange(ROPE // 2, dtype=F32) * 2.0 / ROPE)
    angles = places[:, None] * freqs[None, :]
    return (jnp.cos(angles), jnp.sin(angles))


def rotate(values, cosine, sine):
    half = values.shape[-1] // 2
    first_half = values[..., :half]
    second_half = values[..., half:]
    return jnp.concatenate(
        [first_half * cosine - second_half * sine, second_half * cosine + first_half * sine],
        axis=-1,
    )


def head_weights(weights_ref, query_rows):
    block = weights_ref[0]
    col_total, _, lanes = block.shape
    query_w = block[:, :query_rows, :].reshape(col_total * query_rows, lanes)
    latent_w = block[:, query_rows:, :].reshape(-1, lanes)
    return (query_w, latent_w)


def head_queries(query_w, query_t_ref, cos_ref, sin_ref):
    half = ROPE // 2
    proj_t = dot_plain(query_w.T, query_t_ref[...])
    cosine, sine = cos_ref[...], sin_ref[...]
    queries = []
    for begin in range(0, proj_t.shape[0], HEAD):
        head_t = proj_t[begin : begin + HEAD]
        first, second = head_t[NOPE : NOPE + half], head_t[NOPE + half : NOPE + ROPE]
        queries.append(
            jnp.concatenate(
                [
                    head_t[:NOPE],
                    first * cosine - second * sine,
                    second * cosine + first * sine,
                    head_t[NOPE + ROPE :],
                ],
                axis=0,
            ).astype(BF)
        )
    return queries


def head_tile(both, rope_rows, index):
    both = both[:, index * HEAD : (index + 1) * HEAD]
    lane = lax.broadcasted_iota(jnp.int32, both.shape, 1)
    return (jnp.where(lane < NOPE, both, rope_rows), both)


def attend_kernel(
    query_rows, tile, weights_ref, query_t_ref, latent_ref, rope_ref, cos_ref, sin_ref, bias_ref,
    mixed_ref, lse_ref, scores_ref,
):
    query_w, latent_w = head_weights(weights_ref, query_rows)
    queries = head_queries(query_w, query_t_ref, cos_ref, sin_ref)
    projected = dot_plain(latent_ref[...], latent_w).astype(BF)
    length = projected.shape[0]
    for index, query_t in enumerate(queries):
        keys, both = head_tile(projected, rope_ref[...], index)
        values_t = both.T[NOPE:]
        top = None
        for begin in range(0, length, tile):
            rows = slice(begin, begin + tile)
            part = dot_plain(keys[rows], query_t) * (SCALE * LOG2E) + bias_ref[rows, :]
            scores_ref[index, rows, :] = part
            tile_top = jnp.max(part, axis=0, keepdims=True)
            top = tile_top if top is None else jnp.maximum(top, tile_top)
        total, out_t = None, None
        for begin in range(0, length, tile):
            rows = slice(begin, begin + tile)
            expo = jnp.exp2(scores_ref[index, rows, :] - top)
            tile_sum = jnp.sum(expo, axis=0, keepdims=True)
            term = dot_plain(values_t[:, rows], expo.astype(BF))
            total = tile_sum if total is None else total + tile_sum
            out_t = term if out_t is None else out_t + term
        mixed_ref[index * VDIM : (index + 1) * VDIM, :] = (out_t / total).astype(BF)
        lse_ref[index] = top + jnp.log2(total)


def attend_back_kernel(
    query_rows, tile, weights_ref, query_t_ref, latent_ref, latent_t_ref, rope_ref,
    cos_ref, sin_ref, bias_ref, mixed_ref, grad_ref, lse_ref, query_before_ref, latent_before_ref,
    *rest,
):
    weights_grad_ref, query_acc, latent_acc, both_scr = rest[-4:]
    kv_rank = latent_ref.shape[1]
    query_w, latent_w = head_weights(weights_ref, query_rows)
    queries = head_queries(query_w, query_t_ref, cos_ref, sin_ref)
    projected = dot_plain(latent_ref[...], latent_w).astype(BF)
    length = projected.shape[0]

    @pl.when(pl.program_id(0) == 0)
    def _():
        query_acc[...] = query_before_ref[...]
        latent_acc[...] = latent_before_ref[...]

    half = ROPE // 2
    cosine, sine = cos_ref[...], sin_ref[...]
    backs = []
    for index, query_t in enumerate(queries):
        part = slice(index * VDIM, (index + 1) * VDIM)
        lanes = slice(index * HEAD, (index + 1) * HEAD)
        keys, both = head_tile(projected, rope_ref[...], index)
        keys_t, query = keys.T, query_t.T
        grad_t = grad_ref[part, :]
        delta = jnp.sum(
            grad_t.astype(F32) * mixed_ref[part, :].astype(F32), axis=0, keepdims=True
        )
        grad_pad_t = jnp.concatenate([jnp.zeros_like(grad_t), grad_t], axis=0)
        grad_pad = grad_pad_t.T
        lse = lse_ref[index]
        back_t = None
        for begin in range(0, length, tile):
            rows = slice(begin, begin + tile)
            scores = dot_plain(keys[rows], query_t) * (SCALE * LOG2E)
            probs = jnp.exp2(scores + bias_ref[rows, :] - lse)
            prob_grad = dot_plain(both[rows], grad_pad_t)
            score_grad = (probs * (prob_grad - delta)).astype(BF)
            term = dot_plain(keys_t[:, rows], score_grad)
            back_t = term if back_t is None else back_t + term
            key_back = dot_plain(score_grad, query) * SCALE
            value_back = dot_plain(probs.astype(BF), grad_pad)
            latent_acc[rows, kv_rank:] += key_back
            lane = lax.broadcasted_iota(jnp.int32, key_back.shape, 1)
            both_scr[rows, lanes] = jnp.where(lane < NOPE, key_back, value_back).astype(BF)
        back_t = back_t * SCALE
        first, second = back_t[NOPE : NOPE + half], back_t[NOPE + half : NOPE + ROPE]
        backs += [
            back_t[:NOPE],
            first * cosine + second * sine,
            second * cosine - first * sine,
            jnp.zeros_like(back_t[NOPE + ROPE :]),
        ]
    both_back = both_scr[...]
    latent_acc[:, :kv_rank] += dot_trans_right(both_back, latent_w)
    query_back_t = jnp.concatenate(backs, axis=0).astype(BF)
    query_acc[...] += dot_plain(query_w, query_back_t)
    query_wg = dot_trans_right(query_t_ref[...], query_back_t).astype(BF)
    latent_wg = dot_plain(latent_t_ref[...], both_back).astype(BF)
    col_total, lanes = weights_ref.shape[1], weights_ref.shape[3]
    weights_grad_ref[:, 0, :query_rows, :] = query_wg.reshape(col_total, query_rows, lanes)
    weights_grad_ref[:, 0, query_rows:, :] = latent_wg.reshape(col_total, -1, lanes)


def whole(shape):
    return pl.BlockSpec(shape, lambda step: (0,) * len(shape))


def attend(weights, query_t, latent, rope, cos_t, sin_t, bias_t, query_rows, block):
    _, col_total, _, pack_cols = weights.shape
    pack_rows = query_rows + latent.shape[1] // col_total
    heads = pack_cols // HEAD
    group = math.gcd(heads, 2)
    length, local = bias_t.shape
    tile = math.gcd(length, 256)
    return pl.pallas_call(
        functools.partial(attend_kernel, query_rows, tile),
        grid=(heads // group,),
        in_specs=[
            pl.BlockSpec(
                (1, col_total, pack_rows, group * HEAD), lambda step: (block, 0, 0, step)
            ),
            whole(query_t.shape),
            whole(latent.shape),
            whole(rope.shape),
            whole(cos_t.shape),
            whole(sin_t.shape),
            whole(bias_t.shape),
        ],
        out_specs=[
            pl.BlockSpec((group * VDIM, local), lambda step: (step, 0)),
            pl.BlockSpec((group, 1, local), lambda step: (step, 0, 0)),
        ],
        out_shape=[
            jax.ShapeDtypeStruct((heads * VDIM, local), BF),
            jax.ShapeDtypeStruct((heads, 1, local), F32),
        ],
        scratch_shapes=[
            pltpu.VMEM((group, length, local), F32),
        ],
        compiler_params=pltpu.CompilerParams(
            dimension_semantics=("arbitrary",), vmem_limit_bytes=48 * 1024 * 1024
        ),
        cost_estimate=pl.CostEstimate(
            flops=heads * 1_200_000_000,
            bytes_accessed=weights[0].size * 2,
            transcendentals=heads * local * length,
        ),
        name="attend",
    )(weights, query_t, latent, rope, cos_t, sin_t, bias_t)


def attend_back(
    weights, query_t, latent, latent_t, rope, cos_t, sin_t, bias_t, mixed_t, grad_t, lse,
    query_before, latent_before, weights_before, query_rows, block,
):
    row_total, col_total, _, pack_cols = weights.shape
    more = [] if weights_before is None else [weights_before]
    pack_rows = query_rows + latent.shape[1] // col_total
    heads = pack_cols // HEAD
    group = math.gcd(heads, 2)
    steps = heads // group
    length, local = bias_t.shape
    tile = math.gcd(length, 512)
    return pl.pallas_call(
        functools.partial(attend_back_kernel, query_rows, tile),
        grid=(steps,),
        in_specs=[
            pl.BlockSpec(
                (1, col_total, pack_rows, group * HEAD), lambda step: (block, 0, 0, step)
            ),
            whole(query_t.shape),
            whole(latent.shape),
            whole(latent_t.shape),
            whole(rope.shape),
            whole(cos_t.shape),
            whole(sin_t.shape),
            whole(bias_t.shape),
            pl.BlockSpec((group * VDIM, local), lambda step: (step, 0)),
            pl.BlockSpec((group * VDIM, local), lambda step: (block * steps + step, 0)),
            pl.BlockSpec((group, 1, local), lambda step: (step, 0, 0)),
            whole(query_before.shape),
            whole(latent_before.shape),
        ]
        + [pl.BlockSpec(memory_space=pl.ANY)] * len(more),
        out_specs=[
            pl.BlockSpec(
                (col_total, 1, pack_rows, group * HEAD), lambda step: (0, block, 0, step)
            ),
            whole(query_before.shape),
            whole(latent_before.shape),
        ],
        out_shape=[
            jax.ShapeDtypeStruct((col_total, row_total, pack_rows, pack_cols), BF),
            jax.ShapeDtypeStruct(query_before.shape, F32),
            jax.ShapeDtypeStruct(latent_before.shape, F32),
        ],
        input_output_aliases={13: 0} if more else {},
        scratch_shapes=[
            pltpu.VMEM((length, group * HEAD), BF),
        ],
        compiler_params=pltpu.CompilerParams(
            dimension_semantics=("arbitrary",), vmem_limit_bytes=48 * 1024 * 1024
        ),
        cost_estimate=pl.CostEstimate(
            flops=heads * 2_500_000_000,
            bytes_accessed=weights[0].size * 4,
            transcendentals=heads * local * length,
        ),
        name="attend_back",
    )(weights, query_t, latent, latent_t, rope, cos_t, sin_t, bias_t, mixed_t, grad_t, lse,
      query_before, latent_before, *more)


def weight_grad_kernel(chunks, *refs):
    lefts, rights, out_ref = refs[:chunks], refs[chunks : 2 * chunks], refs[2 * chunks]
    total = None
    for left_ref, right_ref in zip(lefts, rights):
        term = dot_plain(left_ref[...].T, right_ref[...])
        total = term if total is None else total + term
    out_ref[...] = total.astype(out_ref.dtype)


def weight_grad(lefts, rights, name):
    chunks = len(lefts)
    rows, width = lefts[0].shape
    units = rights[0].shape[1]
    tile = math.gcd(width, 256)
    return pl.pallas_call(
        functools.partial(weight_grad_kernel, chunks),
        grid=(width // tile,),
        in_specs=[pl.BlockSpec((rows, tile), lambda step: (0, step))] * chunks
        + [pl.BlockSpec((rows, units), lambda step: (0, 0))] * chunks,
        out_specs=pl.BlockSpec((tile, units), lambda step: (step, 0)),
        out_shape=jax.ShapeDtypeStruct((width, units), BF),
        compiler_params=pltpu.CompilerParams(
            dimension_semantics=("arbitrary",), vmem_limit_bytes=48 * 1024 * 1024
        ),
        cost_estimate=pl.CostEstimate(
            flops=2 * chunks * rows * width * units,
            bytes_accessed=2 * (chunks * rows + units) * width,
            transcendentals=0,
        ),
        name=name,
    )(*lefts, *rights)


MESH = pl.DeviceIdType.MESH


def out_grad_kernel(tokens_ref, mixed_ref, out_ref):
    out_ref[...] = dot_trans_right(tokens_ref[...].T, mixed_ref[...]).astype(BF)


def out_weight_grad(tokens, mixed):
    rows, width = tokens.shape
    units = mixed.shape[0]
    tile = math.gcd(width, 256)
    return pl.pallas_call(
        out_grad_kernel,
        grid=(width // tile,),
        in_specs=[
            pl.BlockSpec((rows, tile), lambda step: (0, step)),
            pl.BlockSpec((units, rows), lambda step: (0, 0)),
        ],
        out_specs=pl.BlockSpec((tile, units), lambda step: (step, 0)),
        out_shape=jax.ShapeDtypeStruct((width, units), BF),
        cost_estimate=pl.CostEstimate(
            flops=2 * rows * width * units,
            bytes_accessed=2 * width * units,
            transcendentals=0,
        ),
        name="out_wg",
    )(tokens, mixed)


def flip(index, bit):
    return index + bit - 2 * bit * lax.rem(index // bit, 2)


def chip_bits(col_total):
    bits, bit = [], 2
    while bit < col_total:
        bits.append(bit)
        bit *= 2
    return bits


def turn_bit(bits, row, step, row_total):
    turn = lax.rem(step + (row * len(bits)) // row_total, len(bits))
    return sum(jnp.where(turn == at, bit, 0) for at, bit in enumerate(bits))


def greet(row_total, row_rank, col_rank, bits):
    barrier = pltpu.get_barrier_semaphore()
    for bit in [1] + bits:
        pl.semaphore_signal(
            barrier, inc=1, device_id=(row_rank, flip(col_rank, bit)), device_id_type=MESH
        )

    @pl.when(row_rank > 0)
    def _():
        pl.semaphore_signal(barrier, inc=1, device_id=(row_rank - 1, col_rank), device_id_type=MESH)

    @pl.when(row_rank < row_total - 1)
    def _():
        pl.semaphore_signal(barrier, inc=1, device_id=(row_rank + 1, col_rank), device_id_type=MESH)

    beside = lax.min(row_rank, 1) + lax.min(row_total - 1 - row_rank, 1)
    pl.semaphore_wait(barrier, 1 + len(bits) + beside)


def gather_kernel(
    row_total, col_total, arrays, *refs,
):
    own_refs, out_refs = refs[:arrays], refs[arrays : 2 * arrays]
    own_sem, line_send, line_recv, chip_send, chip_recv, core_send, core_recv = refs[2 * arrays :]
    row_rank, col_rank = lax.axis_index("row"), lax.axis_index("col")
    bits = chip_bits(col_total)
    masks = 2 ** len(bits)
    owns = [
        pltpu.make_async_copy(own_ref, out_ref.at[row_rank, col_rank], own_sem.at[at])
        for at, (own_ref, out_ref) in enumerate(zip(own_refs, out_refs))
    ]
    for own in owns:
        own.start()
    greet(row_total, row_rank, col_rank, bits)

    def block_col(row, mask):
        index = col_rank
        for step in range(len(bits)):
            if mask >> step & 1:
                index = flip(index, turn_bit(bits, row, step, row_total))
        return index

    def line_copy(at, way, row, own=False):
        ref = out_refs[at].at[row, col_rank]
        return pltpu.make_async_remote_copy(
            src_ref=own_refs[at] if own else ref, dst_ref=ref, send_sem=line_send.at[at, way, row],
            recv_sem=line_recv.at[at, row],
            device_id=(row_rank + 1 - 2 * way, col_rank), device_id_type=MESH,
        )

    def chip_copy(at, row, mask, step, own=False):
        ref = out_refs[at].at[row, block_col(row, mask)]
        to = mask + 2**step
        return pltpu.make_async_remote_copy(
            src_ref=own_refs[at] if own else ref, dst_ref=ref, send_sem=chip_send.at[at, row, to],
            recv_sem=chip_recv.at[at, row, to],
            device_id=(row_rank, flip(col_rank, turn_bit(bits, row, step, row_total))),
            device_id_type=MESH,
        )

    def core_copy(at, row, mask, own=False):
        ref = out_refs[at].at[row, block_col(row, mask)]
        return pltpu.make_async_remote_copy(
            src_ref=own_refs[at] if own else ref, dst_ref=ref, send_sem=core_send.at[at, row, mask],
            recv_sem=core_recv.at[at, row, mask], device_id=(row_rank, flip(col_rank, 1)),
            device_id_type=MESH,
        )

    def by_distance(act):
        for away in range(row_total):
            for side in (0,) if away == 0 else (-1, 1):
                row = row_rank + side * away

                @pl.when((row >= 0) & (row < row_total))
                def _():
                    act(row, away, side)

    def arrive(row, away, side):
        for at in range(arrays):
            if away > 0:
                line_copy(at, 0, row).wait_recv()
            if side <= 0:

                @pl.when(row_rank < row_total - 1)
                def _():
                    line_copy(at, 0, row, away == 0).start()

            if side >= 0:

                @pl.when(row_rank > 0)
                def _():
                    line_copy(at, 1, row, away == 0).start()

            for step in range(len(bits)):
                chip_copy(at, row, 0, step, away == 0).start()
            core_copy(at, row, 0, away == 0).start()

    by_distance(arrive)
    for mask in range(1, masks):
        top = mask.bit_length() - 1

        def forward(row, away, side):
            for at in range(arrays):
                chip_copy(at, row, mask - 2**top, top).wait_recv()
                for step in range(top + 1, len(bits)):
                    chip_copy(at, row, mask, step).start()
                core_copy(at, row, mask).start()

        by_distance(forward)
    for own in owns:
        own.wait()
    for at in range(arrays):
        for row in range(row_total):
            for mask in range(masks):
                core_copy(at, row, mask).wait()
                if mask > 0:
                    top = mask.bit_length() - 1
                    chip_copy(at, row, mask - 2**top, top).wait_send()

            @pl.when((row <= row_rank) & (row_rank < row_total - 1))
            def _():
                line_copy(at, 0, row).wait_send()

            @pl.when((row >= row_rank) & (row_rank > 0))
            def _():
                line_copy(at, 1, row).wait_send()


def gather_all(values, collective_id, name):
    row_total, col_total = lax.axis_size("row"), lax.axis_size("col")
    masks = 2 ** len(chip_bits(col_total))
    arrays = len(values)
    sem = pltpu.SemaphoreType.DMA
    anywhere = pl.BlockSpec(memory_space=pl.ANY)
    return pl.pallas_call(
        functools.partial(gather_kernel, row_total, col_total, arrays),
        in_specs=[anywhere] * arrays,
        out_specs=[anywhere] * arrays,
        out_shape=[
            jax.ShapeDtypeStruct((row_total, col_total) + array.shape, array.dtype)
            for array in values
        ],
        scratch_shapes=[
            sem((arrays,)),
            sem((arrays, 2, row_total)),
            sem((arrays, row_total)),
            sem((arrays, row_total, masks)),
            sem((arrays, row_total, masks)),
            sem((arrays, row_total, masks)),
            sem((arrays, row_total, masks)),
        ],
        compiler_params=pltpu.CompilerParams(
            collective_id=collective_id, has_side_effects=True
        ),
        name=name,
    )(*values)


def add_into(total_ref, other_ref):
    rows = total_ref.shape[0]
    tile = math.gcd(rows, 32)

    def one(step, carry):
        here = pl.ds(pl.multiple_of(step * tile, tile), tile)
        total = total_ref[here, :].astype(F32) + other_ref[here, :].astype(F32)
        total_ref[here, :] = total.astype(total_ref.dtype)
        return carry

    lax.fori_loop(0, rows // tile, one, 0)


class LineReduce:
    def __init__(self, row_total, row_rank, col_rank, block, landed, send, recv):
        self.row_total, self.row_rank, self.col_rank = row_total, row_rank, col_rank
        self.block, self.landed, self.send, self.recv = block, landed, send, recv

    def copy(self, way, row):
        return pltpu.make_async_remote_copy(
            src_ref=self.block(row), dst_ref=self.landed.at[way, row],
            send_sem=self.send.at[way, row], recv_sem=self.recv.at[way, row],
            device_id=(self.row_rank + 1 - 2 * way, self.col_rank), device_id_type=MESH,
        )

    def run(self):
        last = self.row_total - 1
        for step in range(last):
            for way, row in ((0, last - step), (1, step)):
                sends = self.row_rank < row if way == 0 else self.row_rank > row
                gets = self.row_rank > 0 if way == 0 else self.row_rank < last

                @pl.when(sends)
                def _():
                    @pl.when(gets)
                    def _():
                        self.copy(way, row).wait_recv()
                        add_into(self.block(row), self.landed.at[way, row])

                    self.copy(way, row).start()

        for way, gets in ((0, self.row_rank > 0), (1, self.row_rank < last)):

            @pl.when(gets)
            def _():
                self.copy(way, self.row_rank).wait_recv()
                add_into(self.block(self.row_rank), self.landed.at[way, self.row_rank])

    def load(self, from_ref, row):
        rows = from_ref.shape[1]
        tile = math.gcd(rows, 32)

        def one(step, carry):
            here = pl.ds(pl.multiple_of(step * tile, tile), tile)
            self.block(row)[here, :] = from_ref[row, here, :]
            return carry

        lax.fori_loop(0, rows // tile, one, 0)

    def finish(self, out_ref):
        rows = out_ref.shape[0]
        tile = math.gcd(rows, 32)
        own = self.block(self.row_rank)

        def one(step, carry):
            here = pl.ds(pl.multiple_of(step * tile, tile), tile)
            out_ref[here, :] = own[here, :].astype(out_ref.dtype)
            return carry

        lax.fori_loop(0, rows // tile, one, 0)
        for row in range(self.row_total):
            for way, sends in ((0, self.row_rank < row), (1, self.row_rank > row)):

                @pl.when(sends)
                def _():
                    self.copy(way, row).wait_send()


def reduce_kernel(row_total, col_total, part_ref, side_ref, out_ref, side_out_ref, *scratch):
    sums, chip_buf, line_buf, side_sums, side_buf = scratch[:5]
    core_send, core_recv, chip_send, chip_recv = scratch[5:9]
    line_send, line_recv, side_send, side_recv = scratch[9:]
    row_rank, col_rank = lax.axis_index("row"), lax.axis_index("col")
    bits = chip_bits(col_total)
    count = len(bits)
    masks = 2**count
    core = lax.rem(col_rank, 2)
    greet(row_total, row_rank, col_rank, bits)

    def order(row):
        turn = (row * count) // row_total
        return bits[turn:] + bits[:turn]

    def chip_at(row, mask):
        index = col_rank // 2
        for step, bit in enumerate(order(row)):
            if mask >> step & 1:
                index = flip(index, bit // 2)
        return index

    def core_copy(row, mask):
        return pltpu.make_async_remote_copy(
            src_ref=part_ref.at[row, chip_at(row, mask), 1 - core], dst_ref=sums.at[row, mask],
            send_sem=core_send.at[row, mask], recv_sem=core_recv.at[row, mask],
            device_id=(row_rank, flip(col_rank, 1)), device_id_type=MESH,
        )

    def chip_copy(row, mask, step):
        return pltpu.make_async_remote_copy(
            src_ref=sums.at[row, mask], dst_ref=chip_buf.at[row, mask],
            send_sem=chip_send.at[row, mask], recv_sem=chip_recv.at[row, mask],
            device_id=(row_rank, flip(col_rank, order(row)[step])), device_id_type=MESH,
        )

    for mask in range(masks - 1, -1, -1):
        for row in range(row_total):
            core_copy(row, mask).start()
    for mask in range(masks - 1, -1, -1):
        for row in range(row_total):
            core_copy(row, mask).wait_recv()
            add_into(sums.at[row, mask], part_ref.at[row, chip_at(row, mask), core])
            if mask >= masks // 2:
                chip_copy(row, mask, count - 1).start()
    side = LineReduce(
        row_total, row_rank, col_rank, lambda row: side_sums.at[row], side_buf, side_send, side_recv
    )
    for row in range(row_total):
        side.load(side_ref, row)
    side.run()
    for step in range(count - 1, -1, -1):
        half = 2**step
        for mask in range(half - 1, -1, -1):
            for row in range(row_total):
                chip_copy(row, mask + half, step).wait_recv()
                add_into(sums.at[row, mask], chip_buf.at[row, mask + half])
                if step > 0 and mask >= half // 2:
                    chip_copy(row, mask, step - 1).start()
    line = LineReduce(
        row_total, row_rank, col_rank, lambda row: sums.at[row, 0], line_buf, line_send, line_recv
    )
    line.run()
    line.finish(out_ref)
    side.finish(side_out_ref)
    for row in range(row_total):
        for mask in range(masks):
            core_copy(row, mask).wait_send()
            if mask > 0:
                chip_copy(row, mask, mask.bit_length() - 1).wait_send()


def whole_tiles(values):
    rows = values.shape[-2]
    more = -rows % 16
    return jnp.pad(values, ((0, 0),) * (values.ndim - 2) + ((0, more), (0, 0))) if more else values


def reduce_all(parts, side, collective_id, name):
    row_total, col_total, own_rows, lanes = parts.shape
    own_side = side.shape[1]
    parts, side = whole_tiles(parts), whole_tiles(side)
    rows = parts.shape[2]
    parts = parts.reshape(row_total, col_total // 2, 2, rows, lanes)
    masks = col_total // 2
    sem = pltpu.SemaphoreType.DMA
    vmem = pl.BlockSpec(memory_space=pltpu.VMEM)
    out, side_out = pl.pallas_call(
        functools.partial(reduce_kernel, row_total, col_total),
        in_specs=[vmem, vmem],
        out_specs=[vmem, vmem],
        out_shape=[
            jax.ShapeDtypeStruct((rows, lanes), F32),
            jax.ShapeDtypeStruct(side.shape[1:], F32),
        ],
        scratch_shapes=[
            pltpu.VMEM((row_total, masks, rows, lanes), BF),
            pltpu.VMEM((row_total, masks, rows, lanes), BF),
            pltpu.VMEM((2, row_total, rows, lanes), BF),
            pltpu.VMEM(side.shape, BF),
            pltpu.VMEM((2,) + side.shape, BF),
            sem((row_total, masks)),
            sem((row_total, masks)),
            sem((row_total, masks)),
            sem((row_total, masks)),
            sem((2, row_total)),
            sem((2, row_total)),
            sem((2, row_total)),
            sem((2, row_total)),
        ],
        compiler_params=pltpu.CompilerParams(
            collective_id=collective_id, has_side_effects=True, vmem_limit_bytes=48 * 1024 * 1024
        ),
        name=name,
    )(parts, side)
    return (out[:own_rows], side_out[:own_side])


together = lax.optimization_barrier


class Task:
    def __init__(self, steps):
        self.steps, self.state, self.value, self.over = steps, None, None, False

    def advance(self):
        if not self.over:
            try:
                return self.steps.send(self.state)
            except StopIteration as stop:
                self.value, self.over = stop.value, True
        return ()

    def advance_into(self):
        self.state = self.advance()
        return not self.over

    def result(self):
        self.advance()
        assert self.over
        return self.value


def slot(*tasks):
    states = together(tuple(task.advance() for task in tasks))
    for task, state in zip(tasks, states):
        task.state = state


def slots(count, *tasks):
    for _ in range(count):
        slot(*tasks)


def gather_steps(values):
    total = lax.axis_size("row")
    up, down = [None], [None]
    ways = (values, values)
    for step in range(1, total):
        ways = yield (
            lax.ppermute(ways[0], "row", [(i, i + 1) for i in range(step - 1, total - 1)]),
            lax.ppermute(ways[1], "row", [(i, i - 1) for i in range(1, total - step + 1)]),
        )
        up.append(ways[0])
        down.append(ways[1])
    return jnp.concatenate([values] + [up[step] + down[total - step] for step in range(1, total)])


def add_parts(left_op, right_op):
    return (left_op.astype(F32) + right_op.astype(F32)).astype(BF)


def reduce_steps(parts):
    total = lax.axis_size("row")
    ways = None
    for step in range(total - 1):
        sends = (parts[step + 1], parts[total - 1 - step])
        if step > 0:
            sends = (add_parts(sends[0], ways[0]), add_parts(sends[1], ways[1]))
        ways = yield (
            lax.ppermute(sends[0], "row", [(i, i + 1) for i in range(step + 1)]),
            lax.ppermute(sends[1], "row", [(i, i - 1) for i in range(total - 1 - step, total)]),
        )
    return parts[0].astype(F32) + ways[0].astype(F32) + ways[1].astype(F32)


def product_steps(product):
    total = lax.axis_size("row")
    rows = product.shape[0] // total
    parts = [product[at * rows : (at + 1) * rows] for at in range(total)]
    return (yield from reduce_steps(parts))


def pad_to(values, width):
    return jnp.pad(values, ((0, 0), (0, width - values.shape[1])))


def body(
    inputs,
    segments,
    valid_mask,
    teacher,
    cotangent,
    query_down,
    latent_down,
    query_up,
    latent_up,
    output_weight,
    gate_weight,
    up_weight,
    down_weight,
    attn_gain,
    query_gain,
    latent_gain,
    mlp_gain,
):
    both_axes = ("row", "col")
    row_total = lax.axis_size("row")
    col_total = lax.axis_size("col")
    devices = row_total * col_total
    row_rank = lax.axis_index("row")
    local_rows, width = inputs.shape
    length = segments.shape[0]
    q_rank = query_down.shape[1]
    kv_wide = latent_down.shape[1]
    lat_wide = q_rank + kv_wide
    down_rows = query_down.shape[0]
    q_part, kv_part = query_gain.shape[0], latent_gain.shape[0]
    heads_here = output_weight.shape[0] // VDIM
    query_rows = query_up.shape[0]
    offset = row_rank * local_rows

    count = jnp.sum(valid_mask)
    count_parts = jnp.stack([count // 256, count % 256]).astype(F32)
    misc = jnp.concatenate(
        [query_gain.astype(F32), latent_gain.astype(F32), count_parts]
    )
    misc = jnp.pad(misc, (0, down_rows - misc.shape[0])).astype(BF)
    down_pack = jnp.concatenate(
        [query_down, latent_down, attn_gain[:, None], mlp_gain[:, None], misc[:, None]], axis=1
    )
    pack_wide = -(-(lat_wide + 3) // 128) * 128
    down_pack = pad_to(down_pack, pack_wide)

    query_pack = jnp.pad(
        query_up.reshape(query_rows, heads_here, NOPE + ROPE),
        ((0, 0), (0, 0), (0, HEAD - NOPE - ROPE)),
    ).reshape(query_rows, heads_here * HEAD)
    up_pack = jnp.concatenate([query_pack, latent_up], axis=0)
    pack_rows = up_pack.shape[0]
    down_all, head_w = gather_all([down_pack, up_pack], 1, "gather_pack")
    down_all = down_all.reshape(devices * down_rows, pack_wide)
    attn_g = down_all[:, lat_wide].astype(F32)
    mlp_g = down_all[:, lat_wide + 1].astype(F32)
    misc_all = down_all[:, lat_wide + 2].astype(F32).reshape(devices, down_rows)
    query_g = misc_all[:, :q_part].reshape(-1)
    latent_g = misc_all[:, q_part : q_part + kv_part].reshape(-1)
    query_g, out_here = together((query_g, output_weight.T))
    out_all = lax.all_gather(out_here, both_axes, axis=0, tiled=True).reshape(
        row_total, width, heads_here * VDIM
    )
    counts = jnp.sum(misc_all[:, q_part + kv_part : q_part + kv_part + 2], axis=0)
    valid_total = counts[0] * 256.0 + counts[1]

    cosine, sine = rotary(segments)
    cos_here = lax.dynamic_slice_in_dim(cosine, offset, local_rows, 0)
    sin_here = lax.dynamic_slice_in_dim(sine, offset, local_rows, 0)
    tokens_f = inputs.astype(F32)
    normed, normed_unit = root_norm(tokens_f, attn_g)
    normed_b = normed.astype(BF)
    lat = dot_plain(normed_b, down_all)
    query_lat, kv_lat = lat[:, :q_rank], lat[:, q_rank:lat_wide]
    query_norm, query_unit = root_norm(query_lat, query_g)
    kv_norm, kv_unit = root_norm(kv_lat[:, :KV_RANK], latent_g)
    key_rope = rotate(kv_lat[:, KV_RANK:], cos_here, sin_here)
    query_nb = query_norm.astype(BF)
    latent_pack = jnp.concatenate(
        [
            kv_norm,
            jnp.zeros((local_rows, NOPE), F32),
            key_rope,
            jnp.zeros((local_rows, HEAD - NOPE - ROPE), F32),
        ],
        axis=1,
    ).astype(BF)
    latent_give = Task(gather_steps(latent_pack))
    while latent_give.advance_into():
        pass
    latent_blocks, gate_here, up_here, down_here = together(
        (latent_give.value, gate_weight, up_weight, down_weight.T)
    )
    gate_full, up_full, down_t = (
        lax.all_gather(gate_here, "col", axis=0, tiled=True),
        lax.all_gather(up_here, "col", axis=0, tiled=True),
        lax.all_gather(down_here, "col", axis=0, tiled=True),
    )
    froms = [lax.rem(row_rank + row_total - step, row_total) for step in range(row_total)]

    kept = 0
    for block in range(row_total):
        begin = block * local_rows
        ahead = [CONTS - at for at in range(1, CONTS + 1) if begin < length - (CONTS - at) * CONT_LEN]
        passed = CONTS - 1 - max(ahead)
        kept = max(kept, begin + local_rows - passed * CONT_LEN)
    kept = min(length, -(-kept // 256) * 256)
    query_at = offset + jnp.arange(local_rows, dtype=jnp.int32)
    query_seg = lax.dynamic_slice_in_dim(segments, offset, local_rows, 0)
    prompt = jnp.sum((segments == 0).astype(jnp.int32))
    shift = jnp.maximum(jnp.sum((segments < query_seg[0]).astype(jnp.int32)) - prompt, 0)

    def keep(values):
        far = lax.dynamic_slice_in_dim(values, shift, kept, 0)
        near = jnp.arange(kept, dtype=jnp.int32) < prompt
        return jnp.where(near.reshape((kept,) + (1,) * (values.ndim - 1)), values[:kept], far)

    def spread(values):
        places = jnp.arange(length, dtype=jnp.int32)[:, None]
        near = jnp.pad(values, ((0, length - kept), (0, 0)))
        far = jnp.pad(values, ((length, length - kept), (0, 0)))
        far = lax.dynamic_slice_in_dim(far, length - shift, length, 0)
        return jnp.where(places < prompt, near, jnp.where(places < prompt + shift, 0.0, far))

    latent_all = jnp.zeros((length + kept, latent_pack.shape[1]), BF)
    for step, at in enumerate(froms):
        latent_all = lax.dynamic_update_slice_in_dim(
            latent_all, latent_blocks[step * local_rows : (step + 1) * local_rows],
            at * local_rows, 0,
        )
    kept_all = keep(latent_all)
    kv_all = kept_all[:, :KV_RANK]
    rope_all = kept_all[:, KV_RANK:]
    key_at = jnp.arange(kept, dtype=jnp.int32)
    key_at = jnp.where(key_at < prompt, key_at, key_at + shift)
    key_seg = keep(jnp.pad(segments, (0, kept)))
    allowed_t = (key_at[:, None] <= query_at[None, :]) & (
        (key_seg[:, None] == 0) | (key_seg[:, None] == query_seg[None, :])
    )
    bias_t = jnp.where(allowed_t, 0.0, HIDE).astype(F32)
    query_t = query_nb.T
    cos_t, sin_t = cos_here.T, sin_here.T
    cut = row_total // 2
    mixed = [
        attend(head_w, query_t, kv_all, rope_all, cos_t, sin_t, bias_t, query_rows, block)
        for block in range(cut)
    ]
    mixed, out_all, query_t = together((mixed, out_all, query_t))
    mixed += [
        attend(head_w, query_t, kv_all, rope_all, cos_t, sin_t, bias_t, query_rows, block)
        for block in range(cut, row_total)
    ]
    attn_sum = None
    for block in range(row_total):
        term = dot_dims(mixed[block][0], out_all[block], (0,), (1,))
        attn_sum = term if attn_sum is None else attn_sum + term

    residual = tokens_f + RES * attn_sum
    mlp_in, mlp_unit = root_norm(residual, mlp_g)
    mlp_b = mlp_in.astype(BF)
    weight_v = valid_mask.astype(F32)[:, None]
    out_scale = local_rows * devices / valid_total
    rows = local_rows // 2
    parts = [slice(0, rows), slice(rows, 2 * rows)]

    def forward_steps(tokens):
        gate_act = yield dot_plain(tokens, gate_full).astype(BF)
        gate_f = gate_act.astype(F32)
        up_act = dot_plain(tokens, up_full)
        hidden = yield (gate_f * jax.nn.sigmoid(gate_f) * up_act).astype(BF)
        up_act = up_act.astype(BF)
        product = yield dot_trans_right(hidden, down_t).astype(BF)
        return (gate_act, up_act, hidden, product)

    def judge(part, down_sum):
        out_rows = residual[part] + RES * down_sum
        error_val = out_rows - teacher[part].astype(F32)
        squared = 0.5 * jnp.sum(weight_v[part] * error_val * error_val)
        grad_rows = cotangent[part].astype(F32) + out_scale * weight_v[part] * error_val
        return (out_rows.astype(BF), squared, grad_rows, (RES * grad_rows).astype(BF))

    def backward_steps(branch, gate_act, up_act):
        gate_act, up_act = gate_act.astype(F32), up_act.astype(F32)
        gate_sig = jax.nn.sigmoid(gate_act)
        hidden_grad = dot_plain(branch, down_t)
        gate_grad, up_grad = yield (
            (hidden_grad * up_act * gate_sig * (1.0 + gate_act * (1.0 - gate_sig))).astype(BF),
            (hidden_grad * gate_act * gate_sig).astype(BF),
        )
        product = yield dot_trans_right(gate_grad, gate_full)
        product = yield (product + dot_trans_right(up_grad, up_full)).astype(BF)
        return (gate_grad, up_grad, product)

    def weight_steps(work):
        got = []
        for lefts, rights, name in work:
            got.append((yield weight_grad(lefts, rights, name)))
        return got

    hops = row_total - 1
    mlp_b = mlp_in.astype(BF)
    give_0, give_1 = [Task(gather_steps(mlp_b[part])) for part in parts]
    slots(hops, give_0)
    tokens_0, gate_full, up_full = together((give_0.result(), gate_full, up_full))
    fore_0 = Task(forward_steps(tokens_0))
    slots(hops, give_1, fore_0)
    tokens_1 = give_1.result()
    fore_0 = fore_0.result()
    take_0 = Task(product_steps(fore_0[3]))
    fore_1 = Task(forward_steps(tokens_1))
    slots(hops, take_0, fore_1)
    judged_0 = judge(parts[0], take_0.result())
    fore_1 = fore_1.result()
    take_1 = Task(product_steps(fore_1[3]))
    give_0 = Task(gather_steps(judged_0[3]))
    slot(give_0)
    slots(hops - 1, give_0, take_1)
    branch_0 = give_0.result()
    back_0 = Task(backward_steps(branch_0, fore_0[0], fore_0[1]))
    slot(take_1, back_0)
    judged_1 = judge(parts[1], take_1.result())
    give_1 = Task(gather_steps(judged_1[3]))
    slots(hops - 1, give_1, back_0)
    back_0 = back_0.result()
    take_0 = Task(product_steps(back_0[2]))
    slot(give_1, take_0)
    branch_1 = give_1.result()
    back_1 = Task(backward_steps(branch_1, fore_1[0], fore_1[1]))
    down_work = Task(weight_steps([([branch_0, branch_1], [fore_0[2], fore_1[2]], "down_wg")]))
    slot(take_0, down_work)
    slots(hops - 2, take_0, back_1)
    grad_0 = take_0.result()
    (down_wg,) = down_work.result()
    while back_1.advance_into():
        pass
    back_1 = back_1.value
    take_1 = Task(product_steps(back_1[2]))
    work = Task(
        weight_steps(
            [
                ([tokens_0, tokens_1], [back_0[0], back_1[0]], "gate_wg"),
                ([tokens_0, tokens_1], [back_0[1], back_1[1]], "up_wg"),
            ]
        )
    )
    slots(max(hops, 2), take_1, work)
    grad_1 = take_1.result()
    gate_wg, up_wg = work.result()
    outputs = jnp.concatenate([judged_0[0], judged_1[0]])
    squared = judged_0[1] + judged_1[1]
    out_grad = jnp.concatenate([judged_0[2], judged_1[2]])
    mlp_in_grad = jnp.concatenate([grad_0, grad_1])
    gate_wg, up_wg, down_wg = (
        lax.psum_scatter(gate_wg, "col", scatter_dimension=0, tiled=True),
        lax.psum_scatter(up_wg, "col", scatter_dimension=0, tiled=True),
        lax.psum_scatter(down_wg, "col", scatter_dimension=0, tiled=True),
    )
    residual_part, mlp_gain_grad = norm_back(mlp_in_grad, mlp_unit, residual, mlp_g)
    residual_grad = out_grad + residual_part

    attn_grad_in = (RES * residual_grad).astype(BF)
    grad_t = dot_dims(out_all, attn_grad_in, (1,), (1,)).astype(BF)
    latent_t = kv_all.T
    out_wg = out_weight_grad(attn_grad_in, jnp.concatenate([mixed_t for mixed_t, _ in mixed]))
    grad_t, out_wg = together((grad_t.reshape(-1, local_rows), out_wg))
    out_wg = lax.psum_scatter(out_wg, "col", scatter_dimension=0, tiled=True)
    query_back_t = jnp.zeros(query_t.shape, F32)
    latent_back = jnp.zeros(kept_all.shape, F32)
    head_wg = None
    for block, (mixed_t, lse) in enumerate(mixed):
        if block == cut:
            query_back_t, gate_wg, up_wg, down_wg = together((query_back_t, gate_wg, up_wg, down_wg))
        head_wg, query_back_t, latent_back = attend_back(
            head_w, query_t, kv_all, latent_t, rope_all, cos_t, sin_t, bias_t, mixed_t,
            grad_t, lse, query_back_t, latent_back, head_wg, query_rows, block,
        )
    head_wg = lax.psum_scatter(
        head_wg.reshape(devices * pack_rows, heads_here * HEAD), "col",
        scatter_dimension=0, tiled=True,
    ).reshape(row_total, pack_rows, heads_here * HEAD)
    latent_rows = spread(latent_back).astype(BF).reshape(row_total, local_rows, -1)
    latent_reduce = Task(
        reduce_steps(
            [lax.dynamic_index_in_dim(latent_rows, at, 0, keepdims=False) for at in froms]
        )
    )
    while latent_reduce.advance_into():
        pass
    latent_back = latent_reduce.value
    kv_norm_grad = latent_back[:, :KV_RANK]
    rope_grad = latent_back[:, KV_RANK + NOPE : KV_RANK + NOPE + ROPE]
    query_norm_grad = query_back_t.T
    query_lat_grad, query_gain_grad = norm_back(query_norm_grad, query_unit, query_lat, query_g)
    kv_lat_part, latent_gain_grad = norm_back(kv_norm_grad, kv_unit, kv_lat[:, :KV_RANK], latent_g)
    lat_grad = jnp.concatenate(
        [
            query_lat_grad,
            kv_lat_part,
            rotate(rope_grad, cos_here, -sin_here),
            jnp.zeros((local_rows, pack_wide - lat_wide), F32),
        ],
        axis=-1,
    ).astype(BF)
    lat_wg = dot_trans_left(normed_b, lat_grad)
    normed_grad = dot_trans_right(lat_grad, down_all)
    input_part, attention_gain_gradient = norm_back(normed_grad, normed_unit, tokens_f, attn_g)
    input_grad = residual_grad + input_part

    loss_high = squared.astype(BF).astype(F32)
    loss_low = squared - loss_high
    misc_grad = jnp.concatenate(
        [
            query_gain_grad.reshape(devices, q_part),
            latent_gain_grad.reshape(devices, kv_part),
            jnp.broadcast_to(loss_high, (devices, 1)),
            jnp.broadcast_to(loss_low, (devices, 1)),
        ],
        axis=1,
    )
    misc_grad = pad_to(misc_grad, down_rows).reshape(devices * down_rows, 1)
    lane = lax.broadcasted_iota(jnp.int32, lat_wg.shape, 1)
    small = jnp.where(lane == lat_wide, attention_gain_gradient[:, None], lat_wg)
    small = jnp.where(lane == lat_wide + 1, mlp_gain_grad[:, None], small)
    small = jnp.where(lane == lat_wide + 2, misc_grad, small).astype(BF)
    small = small.reshape(row_total, col_total, down_rows, pack_wide)
    units = heads_here * VDIM
    out_wg = jnp.stack(
        [out_wg[:, at * units : (at + 1) * units] for at in range(row_total)]
    )
    small, out_wg = reduce_all(small, out_wg, 3, "reduce_down")
    out_wg = out_wg.T
    small, head_wg = together((small, head_wg))
    head_reduce = Task(
        reduce_steps([lax.dynamic_index_in_dim(head_wg, at, 0, keepdims=False) for at in froms])
    )
    slots(hops, head_reduce)
    head_wg = head_reduce.result()
    qu_wg = head_wg[:query_rows].reshape(query_rows, heads_here, HEAD)[:, :, : NOPE + ROPE]
    qu_wg = qu_wg.reshape(query_rows, heads_here * (NOPE + ROPE))
    kvu_wg = head_wg[query_rows:]
    misc_sum = small[:, lat_wide + 2]
    at = q_part + kv_part
    loss = (misc_sum[at] + misc_sum[at + 1]) / valid_total
    return (
        outputs,
        loss,
        input_grad,
        small[:, :q_rank],
        small[:, q_rank:lat_wide],
        qu_wg,
        kvu_wg,
        out_wg,
        gate_wg.astype(F32),
        up_wg.astype(F32),
        down_wg.astype(F32).T,
        small[:, lat_wide],
        misc_sum[:q_part],
        misc_sum[q_part : q_part + kv_part],
        small[:, lat_wide + 1],
    )


def solution(mesh):
    in_specs = (
        P(("col", "row"), None),
        P("col"),
        P(("col", "row")),
        P(("col", "row"), None),
        P(("col", "row"), None),
        P(("row", "col"), None),
        P(("row", "col"), None),
        P("col", "row"),
        P("col", "row"),
        P("row", "col"),
        P("col", "row"),
        P("col", "row"),
        P("row", "col"),
        P(("row", "col")),
        P(("row", "col")),
        P(("row", "col")),
        P(("row", "col")),
    )
    out_specs = (
        P(("col", "row"), None),
        P(),
        P(("col", "row"), None),
        P(("row", "col"), None),
        P(("row", "col"), None),
        P("col", "row"),
        P("col", "row"),
        P("row", "col"),
        P("col", "row"),
        P("col", "row"),
        P("row", "col"),
        P(("row", "col")),
        P(("row", "col")),
        P(("row", "col")),
        P(("row", "col")),
    )
    return jax.shard_map(body, mesh=mesh, in_specs=in_specs, out_specs=out_specs, check_vma=False)
```
